128 devices in a mesh: lat: 16 (over y, x_lo, core), ens: 8 (over z, x_hi).
Axes of the slice: x: 4 (x_hi: 2, x_lo: 2; x = x_hi * 2 + x_lo), y: 4, z: 4, core: 2. Of those that a mesh axis runs over, the one named last changes fastest.
Arguments:
- passed_on: float32 [8, 192, 16, 384], P('ens', None, None, 'lat'), may hold values from -6 to 6
- passed_grad: float32 [8, 192, 16, 384], P('ens', None, None, 'lat'), may hold values from -6 to 6
- latent: float32 [8, 192, 16, 384], P('ens', None, 'lat'), may hold values from -6 to 6
- mix_factors: float32 [2, 96, 96], replicated, may hold values from -0.25 to 0.25
- in_kernel: bfloat16 [2, 9, 48, 512], replicated, may hold values from -0.3125 to 0.3125
- in_bias: float32 [2, 512], replicated, may hold values from -3 to 3
- out_kernel: bfloat16 [2, 9, 96, 512], replicated, may hold values from -0.09375 to 0.09375
- out_bias: float32 [2, 96], replicated, may hold values from -3 to 3
Outputs:
- rebuilt: float32 [8, 96, 32, 768], P('ens', None, 'lat')
- input_grad: float32 [8, 96, 32, 768], P('ens', None, 'lat')
- mix_grad: float32 [2, 96, 96], replicated
- in_kernel_grad: float32 [2, 9, 48, 512], replicated
- in_bias_grad: float32 [2, 512], replicated
- out_kernel_grad: float32 [2, 9, 96, 512], replicated
- out_bias_grad: float32 [2, 96], replicated
The draws below stay inside these ranges and needn't reach their ends.
All inputs are finite; a program needn't handle non-finite values.
Results may differ from the reference program's by a relative error of at most 0.0028.
Values may be sent and summed in bfloat16 or wider, within the bound.
No kernel may reach another device: no remote copies, remote signals or barrier semaphores. Data moves between devices by JAX's collectives and lax.ppermute only.
A program may use at most 192 MiB of HBM per device.

```python
import jax
import jax.numpy as jnp
from jax import lax

C = 96
HID = 512
LON = 768
FLOWS = 2
NLAT = 32
ENSEMBLE = 8


def level_of(rng, shape, shards, least, high):
    loudness, own = 1.0, jax.random.fold_in(rng, 6)
    for position, parts in shards:
        steps = jnp.exp(jax.random.uniform(jax.random.fold_in(own, position), (parts,), jnp.float32, least / len(shards), high / len(shards)))
        loudness = loudness * jnp.repeat(steps, shape[position] // parts).reshape([-1 if axis == position else 1 for axis in range(len(shape))])
    return loudness


def centred(own_key, extent, deviation, reach, split=(), kind=jnp.bfloat16):
    loudness = level_of(own_key, extent, split, -0.22, 0.18) if split else 1.0
    result = jax.random.normal(own_key, extent, jnp.float32) * deviation * loudness
    return jnp.minimum(jnp.maximum(result, -reach), reach).astype(kind)


def setup_inputs(seed: int = 0) -> dict:
    key_of = jax.random.split(jax.random.key(seed), 9)
    passed_on = centred(key_of[0], (ENSEMBLE, 2 * C, NLAT // 2, LON // 2), 1.0, 6.0, ((0, 8), (3, 16)), jnp.float32)
    passed_grad = centred(key_of[1], (ENSEMBLE, 2 * C, NLAT // 2, LON // 2), 1.0, 6.0, ((0, 8), (3, 16)), jnp.float32)
    latent = centred(key_of[2], (ENSEMBLE, 2 * C, NLAT // 2, LON // 2), 1.0, 6.0, ((0, 8), (2, 16)), jnp.float32)
    mix_factors = centred(key_of[3], (FLOWS, C, C), (6 * C) ** -0.5, 0.25, (), jnp.float32)
    in_kernel = centred(key_of[4], (FLOWS, 9, C // 2, HID), (9 * C // 2) ** -0.5, 0.3125)
    in_bias = centred(key_of[5], (FLOWS, HID), 0.5, 3.0, (), jnp.float32)
    out_kernel = centred(key_of[6], (FLOWS, 9, C, HID), (9 * HID) ** -0.5, 0.09375)
    out_bias = centred(key_of[7], (FLOWS, C), 0.5, 3.0, (), jnp.float32)
    return {"passed_on": passed_on, "passed_grad": passed_grad, "latent": latent, "mix_factors": mix_factors, "in_kernel": in_kernel, "in_bias": in_bias, "out_kernel": out_kernel, "out_bias": out_bias}


def unsqueeze(packed):
    channels, half_rows, half_cols = packed.shape
    base_count = channels // 4
    split_view = packed.reshape(base_count, 2, 2, half_rows, half_cols)
    return jnp.transpose(split_view, (0, 3, 1, 4, 2)).reshape(base_count, 2 * half_rows, 2 * half_cols)

def pad_grid(values):
    return jnp.pad(values, ((0, 0), (1, 1), (1, 1)))

def correlate(padded, kernel, row_count, col_count, pattern, flipped):
    summed = None
    for row_tap in range(3):
        for col_tap in range(3):
            row_start = 2 - row_tap if flipped else row_tap
            col_start = 2 - col_tap if flipped else col_tap
            window = padded[:, row_start:row_start + row_count, col_start:col_start + col_count]
            contrib = jnp.einsum(pattern, window.astype(jnp.float32), kernel[3 * row_tap + col_tap].astype(jnp.float32))
            summed = contrib if summed is None else summed + contrib
    return summed

def tap_grads(padded, cotangent, row_count, col_count, pattern):
    stacked = []
    for row_tap in range(3):
        for col_tap in range(3):
            window = padded[:, row_tap:row_tap + row_count, col_tap:col_tap + col_count]
            stacked.append(jnp.einsum(pattern, window.astype(jnp.float32), cotangent.astype(jnp.float32)))
    return jnp.stack(stacked)

def silu_slope(preact):
    gate_value = jax.nn.sigmoid(preact)
    return gate_value * (1.0 + preact * (1.0 - gate_value))

def triangles(factors):
    identity = jnp.eye(factors.shape[0], dtype=factors.dtype)
    return (identity + jnp.tril(factors, -1), identity + jnp.triu(factors, 1))

def factor_grad(outer_sum, lower_unit, upper_unit):
    high = lax.Precision.HIGHEST
    lower_part = jnp.tril(jnp.dot(outer_sum, upper_unit.T, precision=high), -1)
    upper_part = jnp.triu(jnp.dot(lower_unit.T, outer_sum, precision=high), 1)
    return lower_part + upper_part

def flow_member(current, cotangent, factors, in_taps, in_shift, out_taps, out_shift):
    high = lax.Precision.HIGHEST
    channels, row_count, col_count = current.shape
    half_width = channels // 2
    kept_part = current[:half_width]
    moved_part = current[half_width:]
    inputs_bf = kept_part.astype(jnp.bfloat16)
    input_rim = pad_grid(inputs_bf)
    preact = correlate(input_rim, in_taps, row_count, col_count, 'chw,co->ohw', False) + in_shift[:, None, None]
    hidden = jax.nn.silu(preact).astype(jnp.bfloat16)
    hidden_rim = pad_grid(hidden)
    output = correlate(hidden_rim, out_taps, row_count, col_count, 'chw,oc->ohw', False) + out_shift[:, None, None]
    raw_scale = output[:half_width]
    shifts = output[half_width:]
    scales = jax.nn.sigmoid(raw_scale + 2.0)
    moved_in = moved_part / scales - shifts
    mixed_field = jnp.concatenate([kept_part, moved_in], axis=0)
    lower_unit, upper_unit = triangles(factors)
    flat_field = mixed_field.reshape(channels, -1)
    solved = jax.scipy.linalg.solve_triangular(lower_unit, flat_field, lower=True)
    flat_input = jax.scipy.linalg.solve_triangular(upper_unit, solved, lower=False)
    inputs_field = flat_input.reshape(channels, row_count, col_count)
    kept_grad = cotangent[:half_width]
    moved_grad = cotangent[half_width:]
    moved_back = moved_grad * scales
    raw_grad = (moved_grad * (moved_in + shifts) * scales - 1.0) * (1.0 - scales)
    out_grad = jnp.concatenate([raw_grad, moved_back], axis=0).astype(jnp.bfloat16)
    hidden_grad = correlate(pad_grid(out_grad), out_taps, row_count, col_count, 'ohw,oc->chw', True)
    pre_grad = (hidden_grad * silu_slope(preact)).astype(jnp.bfloat16)
    keep_back = correlate(pad_grid(pre_grad), in_taps, row_count, col_count, 'ohw,co->chw', True)
    mixed_grad = jnp.concatenate([kept_grad + keep_back, moved_back], axis=0)
    flat_grad = mixed_grad.reshape(channels, -1)
    back_flat = jnp.dot(upper_unit.T, jnp.dot(lower_unit.T, flat_grad, precision=high), precision=high)
    input_back = back_flat.reshape(channels, row_count, col_count)
    outer_sum = jnp.dot(flat_grad, flat_input.T, precision=high)
    in_taps_grad = tap_grads(input_rim, pre_grad, row_count, col_count, 'chw,ohw->co')
    in_shift_grad = lax.optimization_barrier(jnp.sum(pre_grad.astype(jnp.float32), axis=(1, 2)))
    out_taps_grad = tap_grads(hidden_rim, out_grad, row_count, col_count, 'chw,ohw->oc')
    out_shift_grad = lax.optimization_barrier(jnp.sum(out_grad.astype(jnp.float32), axis=(1, 2)))
    return (inputs_field, input_back, (outer_sum, in_taps_grad, in_shift_grad, out_taps_grad, out_shift_grad))

def reference(passed_on, passed_grad, latent, mix_factors, in_kernel, in_bias, out_kernel, out_bias):
    flow_count = mix_factors.shape[0]

    def member(running, member_items):
        coarse, coarse_grad, latent_part = member_items
        current = unsqueeze(jnp.concatenate([coarse, latent_part], axis=0))
        cotangent = unsqueeze(jnp.concatenate([coarse_grad, latent_part], axis=0))
        collected = [None] * flow_count
        for flow_index in range(flow_count - 1, -1, -1):
            current, cotangent, collected[flow_index] = flow_member(current, cotangent, mix_factors[flow_index], in_kernel[flow_index], in_bias[flow_index], out_kernel[flow_index], out_bias[flow_index])
        updated = tuple((running[slot] + jnp.stack([collected[flow_index][slot] for flow_index in range(flow_count)]) for slot in range(5)))
        return (updated, (current, cotangent))
    start = (jnp.zeros(mix_factors.shape, jnp.float32), jnp.zeros(in_kernel.shape, jnp.float32), jnp.zeros(in_bias.shape, jnp.float32), jnp.zeros(out_kernel.shape, jnp.float32), jnp.zeros(out_bias.shape, jnp.float32))
    running, (rebuilt, input_grad) = lax.scan(member, start, (passed_on, passed_grad, latent))
    scale_factor = 1.0 / (ENSEMBLE * NLAT * LON)
    mix_grad = jnp.stack([factor_grad(running[0][flow_index], *triangles(mix_factors[flow_index])) for flow_index in range(flow_count)]) * scale_factor
    return (rebuilt, input_grad, mix_grad, running[1] * scale_factor, running[2] * scale_factor, running[3] * scale_factor, running[4] * scale_factor)
```

```python
import functools

import jax
import jax.numpy as jnp
from jax import lax
from jax.experimental import pallas as pl
from jax.experimental.pallas import tpu as pltpu
from jax.sharding import Mesh, PartitionSpec as P

BF = jnp.bfloat16
F32 = jnp.float32
HIGH = lax.Precision.HIGHEST
LAT = ("y", "xl", "c")
ENS = ("z", "xh")
CHIPS = ("y", "xl", "z", "xh")
HALF = 48
CH = 96
HID = 512
COLS = 384
ROW = 768
CELLS = 1536
PACK = 1536
VMEM_LIMIT = 56 * 1024 * 1024


def mm(a, b):
    return lax.dot_general(a, b, (((1,), (0,)), ((), ())), preferred_element_type=F32)


def mm_nt(a, b):
    return lax.dot_general(a, b, (((1,), (1,)), ((), ())), preferred_element_type=F32)


def mm_high(a, b):
    return lax.dot_general(
        a, b, (((1,), (0,)), ((), ())), preferred_element_type=F32, precision=HIGH
    )


def split3(x):
    hi = x.astype(BF)
    rest = x - hi.astype(F32)
    mid = rest.astype(BF)
    low = (rest - mid.astype(F32)).astype(BF)
    return hi, mid, low


def from_left(x):
    lane = lax.broadcasted_iota(jnp.int32, x.shape, 1)
    return jnp.where(lane == 0, 0.0, pltpu.roll(x, 1, 1))


def from_right(x):
    width = x.shape[1]
    lane = lax.broadcasted_iota(jnp.int32, x.shape, 1)
    return jnp.where(lane == width - 1, 0.0, pltpu.roll(x, width - 1, 1))


def call(body, outs, ins, scratch=(), smem=(), flops=0, name=None):
    in_specs = [
        pl.BlockSpec(memory_space=pltpu.SMEM if i in smem else pltpu.VMEM) for i in range(len(ins))
    ]
    moved = sum(x.size * x.dtype.itemsize for x in ins) + sum(
        x.size * x.dtype.itemsize for x in outs
    )
    return pl.pallas_call(
        body,
        out_shape=outs,
        in_specs=in_specs,
        out_specs=[pl.BlockSpec(memory_space=pltpu.VMEM) for _ in outs],
        scratch_shapes=list(scratch),
        compiler_params=pltpu.CompilerParams(vmem_limit_bytes=VMEM_LIMIT),
        cost_estimate=pl.CostEstimate(flops=flops, bytes_accessed=moved, transcendentals=0),
        name=name,
    )(*ins)


def sds(shape, dtype):
    return jax.ShapeDtypeStruct(shape, dtype)


def prep_kernel(mix_ref, w1_ref, w2_ref, inv_ref, lut_ref, w1t_ref, w2t_ref, w2k_ref):
    flows = mix_ref.shape[0]
    row = lax.broadcasted_iota(jnp.int32, (CH, CH), 0)
    col = lax.broadcasted_iota(jnp.int32, (CH, CH), 1)
    eye = (row == col).astype(F32)
    near = (row // 16) == (col // 16)
    units = []
    for k in range(flows):
        mix = mix_ref[k]
        units.append(jnp.where(row > col, mix, 0.0))
        units.append(jnp.where(row < col, mix, 0.0))
    inner = [jnp.where(near, u, 0.0) for u in units]
    outer = [u - i for u, i in zip(units, inner)]
    power = inner
    blocks = [eye - n for n in inner]
    for _ in range(3):
        power = [mm_high(p, p) for p in power]
        blocks = [mm_high(b, eye + p) for b, p in zip(blocks, power)]
    power = [mm_high(b, o) for b, o in zip(blocks, outer)]
    whole = [eye - p for p in power]
    for _ in range(2):
        power = [mm_high(p, p) for p in power]
        whole = [mm_high(w, eye + p) for w, p in zip(whole, power)]
    inverses = [mm_high(w, b) for w, b in zip(whole, blocks)]
    for k in range(flows):
        inv_ref[k] = mm_high(inverses[2 * k + 1], inverses[2 * k])
        lut_ref[k] = mm_high(units[2 * k] + eye, units[2 * k + 1] + eye).T
        for tap in range(9):
            w1t_ref[k, :, tap * HALF : (tap + 1) * HALF] = (
                w1_ref[k, tap].astype(F32).T.astype(BF)
            )
            w2t_ref[k, :, tap * CH : (tap + 1) * CH] = (
                w2_ref[k, 8 - tap].astype(F32).T.astype(BF)
            )
        for a in range(3):
            for b in range(3):
                w2k_ref[k, b * CH : (b + 1) * CH, a * HID : (a + 1) * HID] = w2_ref[k, 3 * a + b]


def prep(mix_factors, in_kernel, out_kernel):
    flows = mix_factors.shape[0]
    return call(
        prep_kernel,
        [
            sds((flows, CH, CH), F32),
            sds((flows, CH, CH), F32),
            sds((flows, HID, 9 * HALF), BF),
            sds((flows, HID, 9 * CH), BF),
            sds((flows, 3 * CH, 3 * HID), BF),
        ],
        [mix_factors, in_kernel, out_kernel],
        name="prep",
    )


def turn_kernel(recv_ref, above_ref, mid_ref, below_ref, ya_ref, ga_ref, stage):
    row = lax.broadcasted_iota(jnp.int32, (2 * CH, 2 * CH), 0)
    col = lax.broadcasted_iota(jnp.int32, (2 * CH, 2 * CH), 1)
    pick = (col == 4 * (row % HALF) + row // HALF).astype(BF)
    sources, kinds, width = recv_ref.shape[0], 6, recv_ref.shape[2]
    turned = []
    for kind in range(kinds):
        for s in range(sources):
            stage[s * width : (s + 1) * width, :] = recv_ref[s, kind].astype(F32)
        turned.append(mm_nt(pick, stage[...].astype(BF)))
    above_ref[...] = turned[0].astype(BF)
    mid_ref[...] = turned[1].astype(BF)
    below_ref[...] = turned[2].astype(BF)
    kept = turned[1] + turned[3]
    grad = turned[4] + turned[5]
    for k in range(4):
        ya_ref[:, k * COLS : (k + 1) * COLS] = kept[k * HALF : (k + 1) * HALF]
        ga_ref[:, k * COLS : (k + 1) * COLS] = grad[k * HALF : (k + 1) * HALF]


def turn(recv):
    return call(
        turn_kernel,
        [sds((2 * CH, COLS), BF)] * 3 + [sds((HALF, CELLS), F32)] * 2,
        [recv],
        scratch=[pltpu.VMEM((COLS, 2 * CH), F32)],
        name="turn",
    )


def stack_planes(even, odd):
    left = from_left(odd.astype(F32)).astype(BF)
    right = from_right(even.astype(F32)).astype(BF)
    return jnp.concatenate([left, even, odd, right], axis=0)


def fill_input_columns(above_ref, mid_ref, below_ref, columns, first, count):
    refs = {-2: (above_ref, 0), -1: (above_ref, CH), 0: (mid_ref, 0)}
    refs.update({1: (mid_ref, CH), 2: (below_ref, 0), 3: (below_ref, CH)})
    for source in range(first - 1, first + count + 1):
        ref, at = refs[source]
        stacked = stack_planes(ref[at : at + HALF], ref[at + HALF : at + CH])
        for a in range(3):
            target = source - a + 1 - first
            if 0 <= target < count:
                for p in range(2):
                    lane = (2 * target + p) * COLS
                    columns[a * 144 : (a + 1) * 144, lane : lane + COLS] = stacked[
                        p * HALF : p * HALF + 144
                    ]


def fill_grad_columns(top_ref, mid_ref, bottom_ref, columns):
    refs = [(top_ref, 0), (mid_ref, 0), (mid_ref, 2 * CH), (bottom_ref, 0)]
    for source in range(4):
        ref, at = refs[source]
        stacked = stack_planes(ref[at : at + CH], ref[at + CH : at + 2 * CH])
        for a in range(3):
            target = source - a
            if 0 <= target < 2:
                for p in range(2):
                    lane = (2 * target + p) * COLS
                    columns[a * 288 : (a + 1) * 288, lane : lane + COLS] = stacked[
                        p * CH : p * CH + 288
                    ]


def put_out_grad(raw, moved, out_ref):
    for r in range(2):
        for p in range(2):
            lane = (2 * r + p) * COLS
            at = (2 * r + p) * CH
            out_ref[at : at + HALF] = raw[:, lane : lane + COLS].astype(BF)
            out_ref[at + HALF : at + CH] = moved[:, lane : lane + COLS].astype(BF)


def forward_kernel(
    with_grad,
    flags_ref,
    above_ref,
    mid_ref,
    below_ref,
    w1t_ref,
    b1_ref,
    w2k_ref,
    b2_ref,
    inv_ref,
    ya_ref,
    yb_ref,
    x_ref,
    next_ref,
    scale_ref,
    hid_ref,
    slope_ref,
    *rest,
):
    if with_grad:
        grad_ref, moved_ref = rest[0], rest[1]
    columns, pre, rows, outs = rest[-4:]
    fill_input_columns(above_ref, mid_ref, below_ref, columns, -1, 4)
    bias = b1_ref[...]
    for h in range(4):
        pre[...] = mm(w1t_ref[...], columns[:, h * ROW : (h + 1) * ROW])
        inside = flags_ref[0] if h == 0 else flags_ref[1] if h == 3 else None

        def activate(step, carry):
            at = pl.multiple_of(step * 16, 16)
            value = pre[pl.ds(at, 16), :] + b1_ref[pl.ds(at, 16), :]
            gate = 0.5 + 0.5 * jnp.tanh(0.5 * value)
            hidden = value * gate
            if inside is not None:
                rows[pl.ds(h * HID + at, 16), :] = (hidden * inside).astype(BF)
            else:
                rows[pl.ds(h * HID + at, 16), :] = hidden.astype(BF)
                hid_ref[pl.ds((h - 1) * HID + at, 16), :] = hidden.astype(BF)
                slope_ref[pl.ds((h - 1) * HID + at, 16), :] = gate + hidden * (1.0 - gate)
            return carry

        lax.fori_loop(0, HID // 16, activate, 0)
    for r in range(2):
        taps = mm(w2k_ref[...], rows[r * HID : (r + 3) * HID, :])
        even, odd = taps[:, :COLS], taps[:, COLS:]
        lane = 2 * r * COLS
        outs[:, lane : lane + COLS] = from_left(odd[:CH]) + even[CH : 2 * CH] + odd[2 * CH :]
        outs[:, lane + COLS : lane + ROW] = even[:CH] + odd[CH : 2 * CH] + from_right(even[2 * CH :])
    raw = outs[:HALF] + b2_ref[:HALF]
    shift = outs[HALF:] + b2_ref[HALF:]
    inverse = 1.0 + jnp.exp(-(raw + 2.0))
    scale = 1.0 / inverse
    moved_in = yb_ref[...] * inverse - shift
    scale_ref[...] = scale
    x = mm_high(inv_ref[...], jnp.concatenate([ya_ref[...], moved_in], axis=0))
    x_ref[...] = x
    for k in range(4):
        next_ref[k * HALF : (k + 1) * HALF] = x[:HALF, k * COLS : (k + 1) * COLS].astype(BF)
    if with_grad:
        moved_grad = yb_ref[...]
        moved = moved_grad * scale
        moved_ref[...] = moved
        put_out_grad((moved_grad * yb_ref[...] - 1.0) * (1.0 - scale), moved, grad_ref)


def forward(flags, above, mid, below, w1t, b1, w2k, b2, inv, ya, yb, with_grad):
    outs = [
        sds((CH, CELLS), F32),
        sds((2 * CH, COLS), BF),
        sds((HALF, CELLS), F32),
        sds((2 * HID, ROW), BF),
        sds((2 * HID, ROW), F32),
    ]
    if with_grad:
        outs += [sds((4 * CH, COLS), BF), sds((HALF, CELLS), F32)]
    return call(
        functools.partial(forward_kernel, with_grad),
        outs,
        [flags, above, mid, below, w1t, b1, w2k, b2, inv, ya, yb],
        scratch=[
            pltpu.VMEM((9 * HALF, 4 * ROW), BF),
            pltpu.VMEM((HID, ROW), F32),
            pltpu.VMEM((4 * HID, ROW), BF),
            pltpu.VMEM((CH, CELLS), F32),
        ],
        smem=(0,),
        flops=4 * 10**9,
        name="forward",
    )


def backward_kernel(
    top_ref, mid_ref, bottom_ref, w2t_ref, slope_ref, w1_ref, gpre_ref, up_ref, in_ref, down_ref,
    columns, hid_grad, sums,
):
    fill_grad_columns(top_ref, mid_ref, bottom_ref, columns)
    sums[...] = jnp.zeros_like(sums)
    for r in range(2):
        hid_grad[...] = mm(w2t_ref[...], columns[:, r * ROW : (r + 1) * ROW])

        def slope(step, carry):
            at = pl.multiple_of(step * 16, 16)
            gpre_ref[pl.ds(r * HID + at, 16), :] = (
                hid_grad[pl.ds(at, 16), :] * slope_ref[pl.ds(r * HID + at, 16), :]
            ).astype(BF)
            return carry

        lax.fori_loop(0, HID // 16, slope, 0)
        taps = mm(w1_ref[...], gpre_ref[r * HID : (r + 1) * HID, :])
        for a in range(3):
            sums[r + a] += taps[a * 144 : (a + 1) * 144]
    for row, (ref, at) in enumerate(((up_ref, 0), (in_ref, 0), (in_ref, CH), (down_ref, 0))):
        total = sums[row]
        even, odd = total[:, :COLS], total[:, COLS:]
        b0, b1, b2 = slice(0, HALF), slice(HALF, CH), slice(CH, 3 * HALF)
        new_even = odd[b0] + even[b1] + from_left(odd[b2])
        new_odd = from_right(even[b0]) + odd[b1] + even[b2]
        ref[at : at + HALF] = new_even.astype(ref.dtype)
        ref[at + HALF : at + CH] = new_odd.astype(ref.dtype)


def backward(top, mid, bottom, w2t, slope, w1):
    return call(
        backward_kernel,
        [
            sds((2 * HID, ROW), BF),
            sds((CH, COLS), BF),
            sds((2 * CH, COLS), F32),
            sds((CH, COLS), BF),
        ],
        [top, mid, bottom, w2t, slope, w1],
        scratch=[
            pltpu.VMEM((9 * CH, CELLS), BF),
            pltpu.VMEM((HID, ROW), F32),
            pltpu.VMEM((4, 144, ROW), F32),
        ],
        flops=4 * 10**9,
        name="backward",
    )


def weight_kernel(
    above_ref, mid_ref, below_ref, top_ref, gmid_ref, bottom_ref, hid_ref, gpre_ref, out_ref,
    in_columns, grad_columns,
):
    fill_input_columns(above_ref, mid_ref, below_ref, in_columns, 0, 2)
    fill_grad_columns(top_ref, gmid_ref, bottom_ref, grad_columns)
    out_ref[:432] = mm_nt(in_columns[:, :ROW], gpre_ref[:HID]) + mm_nt(
        in_columns[:, ROW:], gpre_ref[HID:]
    )
    out_ref[432:1296] = mm_nt(grad_columns[:, :ROW], hid_ref[:HID]) + mm_nt(
        grad_columns[:, ROW:], hid_ref[HID:]
    )
    out_ref[1296:] = jnp.zeros((PACK - 1296, HID), F32)
    ones = jnp.ones((8, ROW), BF)
    out_ref[1392:1400] = mm_nt(ones, gpre_ref[:HID]) + mm_nt(ones, gpre_ref[HID:])
    own = slice(4 * CH, 5 * CH)
    out_ref[1400:1408, :CH] = mm_nt(ones, grad_columns[own, :ROW]) + mm_nt(
        ones, grad_columns[own, ROW:]
    )


def weight(above, mid, below, top, gmid, bottom, hid, gpre):
    return call(
        weight_kernel,
        [sds((PACK, HID), F32)],
        [above, mid, below, top, gmid, bottom, hid, gpre],
        scratch=[pltpu.VMEM((9 * HALF, CELLS), BF), pltpu.VMEM((9 * CH, CELLS), BF)],
        flops=4 * 10**9,
        name="weights",
    )[0]


def close_kernel(
    next_step, in_ref, low_ref, high_ref, ga_ref, moved_ref, lut_ref, x_ref, *rest
):
    if next_step:
        scale_ref, dmix_ref, gx_ref, grad_ref, nmoved_ref, whole = rest
    else:
        dmix_ref, gx_ref, whole = rest
    for k in range(4):
        part = in_ref[k * HALF : (k + 1) * HALF]
        if k < 2:
            part = part + low_ref[k * HALF : (k + 1) * HALF].astype(F32)
        else:
            part = part + high_ref[(k - 2) * HALF : (k - 1) * HALF].astype(F32)
        lane = k * COLS
        whole[:HALF, lane : lane + COLS] = ga_ref[:, lane : lane + COLS] + part
    whole[HALF:] = moved_ref[...]
    gx = mm_high(lut_ref[...], whole[...])
    gx_ref[...] = gx
    if next_step:
        scale = scale_ref[...]
        moved_grad = gx[HALF:]
        moved = moved_grad * scale
        nmoved_ref[...] = moved
        put_out_grad((moved_grad * x_ref[HALF:] - 1.0) * (1.0 - scale), moved, grad_ref)
    ghi, gmid, _ = split3(whole[...])
    xhi, xmid, _ = split3(x_ref[...])
    dmix_ref[...] = mm_nt(ghi, xhi) + (mm_nt(ghi, xmid) + mm_nt(gmid, xhi))


def close(gin, low, high, ga, moved, lut, x, scale=None):
    outs = [sds((CH, CH), F32), sds((CH, CELLS), F32)]
    ins = [gin, low, high, ga, moved, lut, x]
    if scale is not None:
        outs += [sds((4 * CH, COLS), BF), sds((HALF, CELLS), F32)]
        ins += [scale]
    return call(
        functools.partial(close_kernel, scale is not None),
        outs,
        ins,
        scratch=[pltpu.VMEM((CH, CELLS), F32)],
        flops=10**9,
        name="close",
    )


def weave_kernel(x_ref, out_ref):
    size = 256
    row = lax.broadcasted_iota(jnp.int32, (size, size), 0)
    col = lax.broadcasted_iota(jnp.int32, (size, size), 1)
    place = (col == 2 * (row % 128) + row // 128).astype(BF)
    for r in range(2):
        for t in range(3):
            lane = r * ROW + t * 128
            pair = jnp.concatenate(
                [x_ref[:, lane : lane + 128], x_ref[:, lane + COLS : lane + COLS + 128]], axis=1
            )
            hi, mid, low = split3(pair)
            woven = mm(hi, place) + (mm(mid, place) + mm(low, place))
            out_ref[0, :, r, t * size : (t + 1) * size] = woven


def weave(x):
    return call(weave_kernel, [sds((1, CH, 2, ROW), F32)], [x], name="weave")[0]


def triangle_grad(outer_sum, mix):
    eye = jnp.eye(CH, dtype=F32)
    lower = eye + jnp.tril(mix, -1)
    upper = eye + jnp.triu(mix, 1)
    low = jnp.tril(jnp.dot(outer_sum, upper.T, precision=HIGH), -1)
    high = jnp.triu(jnp.dot(lower.T, outer_sum, precision=HIGH), 1)
    return low + high


def local(passed_on, passed_grad, latent, mix_factors, in_kernel, in_bias, out_kernel, out_bias):
    lat_index = lax.axis_index(LAT)
    lat_count = lax.axis_size(LAT)
    forth = [(i, i + 1) for i in range(lat_count - 1)]
    back = [(i + 1, i) for i in range(lat_count - 1)]
    flags = jnp.stack([lat_index > 0, lat_index < lat_count - 1]).astype(F32)

    on = jnp.transpose(passed_on[0], (1, 2, 0))
    grad = jnp.transpose(passed_grad[0], (1, 2, 0))
    on_hi = on.astype(BF)
    on_lo = (on - on_hi.astype(F32)).astype(BF)
    grad_hi = grad.astype(BF)
    grad_lo = (grad - grad_hi.astype(F32)).astype(BF)
    blank = jnp.zeros_like(on_hi[:1])
    payload = jnp.stack(
        [
            jnp.concatenate([blank, on_hi[:-1]]),
            on_hi,
            jnp.concatenate([on_hi[1:], blank]),
            on_lo,
            grad_hi,
            grad_lo,
        ],
        axis=1,
    )
    recv = lax.all_to_all(payload, LAT, 0, 0, tiled=True)
    inv, lut, w1t, w2t, w2k = prep(mix_factors, in_kernel, out_kernel)
    w1 = in_kernel.reshape(2, 9 * HALF, HID)
    yb = latent.reshape(HALF, 4, COLS).reshape(HALF, CELLS)
    b1 = in_bias[:, :, None]
    b2 = out_bias[:, :, None]

    above, mid, below, ya, ga = turn(recv)
    x1, next_mid, _, hid1, slope1, grad1, moved1 = forward(
        flags, above, mid, below, w1t[1], b1[1], w2k[1], b2[1], inv[1], ya, yb, True
    )
    gtop = lax.ppermute(grad1[2 * CH :], LAT, forth)
    gbottom = lax.ppermute(grad1[: 2 * CH], LAT, back)
    above0 = lax.ppermute(next_mid, LAT, forth)
    below0 = lax.ppermute(next_mid, LAT, back)
    gpre1, up1, in1, down1 = backward(gtop, grad1, gbottom, w2t[1], slope1, w1[1])
    low1 = lax.ppermute(down1, LAT, forth)
    high1 = lax.ppermute(up1, LAT, back)
    x0, _, scale0, hid0, slope0 = forward(
        flags, above0, next_mid, below0, w1t[0], b1[0], w2k[0], b2[0], inv[0],
        x1[:HALF], x1[HALF:], False,
    )
    dmix1, gx1, grad0, moved0 = close(in1, low1, high1, ga, moved1, lut[1], x1, scale0)
    gtop0 = lax.ppermute(grad0[2 * CH :], LAT, forth)
    gbottom0 = lax.ppermute(grad0[: 2 * CH], LAT, back)
    pack1 = weight(above, mid, below, gtop, grad1, gbottom, hid1, gpre1)
    rebuilt = weave(x0)
    gpre0, up0, in0, down0 = backward(gtop0, grad0, gbottom0, w2t[0], slope0, w1[0])
    low0 = lax.ppermute(down0, LAT, forth)
    high0 = lax.ppermute(up0, LAT, back)
    pack0 = weight(above0, next_mid, below0, gtop0, grad0, gbottom0, hid0, gpre0)
    dmix0, gx0 = close(in0, low0, high0, gx1[:HALF], moved0, lut[0], x0)
    input_grad = weave(gx0)

    def place(pack, dmix):
        return lax.dynamic_update_slice(pack, dmix, (1296, 0))

    pack0 = place(pack0, dmix0)
    pack1 = place(pack1, dmix1)
    is_one = lax.axis_index("c") == 1
    keep = jnp.where(is_one, pack1, pack0)
    give = jnp.where(is_one, pack0, pack1)
    swap = [(0, 1), (1, 0)]
    got = lax.ppermute(give, "c", swap)
    chips = lax.axis_size(CHIPS)
    total = (keep + got).astype(BF).reshape(chips, PACK // chips, HID)
    shares = lax.all_to_all(total, CHIPS, 0, 0, tiled=True)
    cells = float(CELLS * lat_count * lax.axis_size(ENS))
    share = (jnp.sum(shares.astype(F32), axis=0, keepdims=True) / cells).astype(BF)
    spread = jnp.broadcast_to(share, (chips, PACK // chips, HID))
    mine = lax.all_to_all(spread, CHIPS, 0, 0, tiled=True).reshape(PACK, HID)
    other = lax.ppermute(mine, "c", swap)
    sums = jnp.stack([jnp.where(is_one, other, mine), jnp.where(is_one, mine, other)]).astype(F32)
    mix_grad = jnp.stack(
        [triangle_grad(sums[k, 1296:1392, :CH], mix_factors[k]) for k in range(2)]
    )
    return (
        rebuilt,
        input_grad,
        mix_grad,
        sums[:, :432].reshape(2, 9, HALF, HID),
        sums[:, 1392],
        sums[:, 432:1296].reshape(2, 9, CH, HID)[:, ::-1],
        sums[:, 1400, :CH],
    )


def solution(mesh):
    split = Mesh(mesh.devices.reshape(4, 2, 2, 4, 2), ("y", "xl", "c", "z", "xh"))
    return jax.shard_map(
        local,
        mesh=split,
        in_specs=(
            P(ENS, None, None, LAT),
            P(ENS, None, None, LAT),
            P(ENS, None, LAT, None),
            P(),
            P(),
            P(),
            P(),
            P(),
        ),
        out_specs=(P(ENS, None, LAT, None), P(ENS, None, LAT, None), P(), P(), P(), P(), P()),
        check_vma=False,
    )
```

```python
import functools

import jax
import jax.numpy as jnp
from jax import lax
from jax.experimental import pallas as pl
from jax.experimental.pallas import tpu as pltpu
from jax.sharding import Mesh, PartitionSpec as P

BF = jnp.bfloat16
F32 = jnp.float32
HIGH = lax.Precision.HIGHEST
LAT = ("y", "xl", "c")
ENS = ("z", "xh")
CHIPS = ("y", "xl", "z", "xh")
HALF = 48
CH = 96
HID = 512
COLS = 384
ROW = 768
CELLS = 1536
IN_ROWS = 448
IN_HALF = 224
TAP_HALF = 144
VMEM_LIMIT = 56 * 1024 * 1024


def mm(a, b):
    return lax.dot_general(a, b, (((1,), (0,)), ((), ())), preferred_element_type=F32)


def mm_nt(a, b):
    return lax.dot_general(a, b, (((1,), (1,)), ((), ())), preferred_element_type=F32)


def mm_high(a, b):
    return lax.dot_general(
        a, b, (((1,), (0,)), ((), ())), preferred_element_type=F32, precision=HIGH
    )


def split3(x):
    hi = x.astype(BF)
    rest = x - hi.astype(F32)
    mid = rest.astype(BF)
    low = (rest - mid.astype(F32)).astype(BF)
    return hi, mid, low


def from_left(x):
    lane = lax.broadcasted_iota(jnp.int32, x.shape, 1)
    return jnp.where(lane == 0, 0.0, pltpu.roll(x, 1, 1))


def from_right(x):
    width = x.shape[1]
    lane = lax.broadcasted_iota(jnp.int32, x.shape, 1)
    return jnp.where(lane == width - 1, 0.0, pltpu.roll(x, width - 1, 1))


def sds(shape, dtype):
    return jax.ShapeDtypeStruct(shape, dtype)


def call(body, outs, ins, scratch=(), smem=(), flops=0, name=None):
    moved = sum(x.size * x.dtype.itemsize for x in list(ins) + list(outs))
    return pl.pallas_call(
        body,
        out_shape=outs,
        in_specs=[
            pl.BlockSpec(memory_space=pltpu.SMEM if i in smem else pltpu.VMEM)
            for i in range(len(ins))
        ],
        out_specs=[pl.BlockSpec(memory_space=pltpu.VMEM) for _ in outs],
        scratch_shapes=list(scratch),
        compiler_params=pltpu.CompilerParams(vmem_limit_bytes=VMEM_LIMIT),
        cost_estimate=pl.CostEstimate(flops=flops, bytes_accessed=moved, transcendentals=0),
        name=name,
    )(*ins)


def payload_kernel(on_ref, grad_ref, out_ref):
    bands, width = on_ref.shape[2], 2 * CH
    blank = jnp.zeros(on_ref.shape[1:], BF)
    for s in range(on_ref.shape[0]):
        on = on_ref[s]
        hi = on.astype(BF)
        grad = grad_ref[s]
        ghi = grad.astype(BF)
        out_ref[s, :, :width] = hi
        out_ref[s, :, width : 2 * width] = (on - hi.astype(F32)).astype(BF)
        if s + 1 < on_ref.shape[0]:
            out_ref[s + 1, :, 2 * width : 3 * width] = hi
        if s > 0:
            out_ref[s - 1, :, 3 * width : 4 * width] = hi
        out_ref[s, :, 4 * width : 5 * width] = ghi
        out_ref[s, :, 5 * width : 6 * width] = (grad - ghi.astype(F32)).astype(BF)
    out_ref[0, :, 2 * width : 3 * width] = blank
    out_ref[on_ref.shape[0] - 1, :, 3 * width : 4 * width] = blank


def payload(on, grad):
    bands, width, channels = on.shape
    return call(
        payload_kernel, [sds((bands, width, 6 * channels), BF)], [on, grad], name="payload"
    )[0]


def prep_kernel(
    mix_ref, w1_ref, w2_ref, b1_ref, b2_ref, *refs
):
    stage1, stage2 = refs[-2:]
    flows = mix_ref.shape[0]
    row = lax.broadcasted_iota(jnp.int32, (CH, CH), 0)
    col = lax.broadcasted_iota(jnp.int32, (CH, CH), 1)
    eye = (row == col).astype(F32)
    near = (row // 16) == (col // 16)
    units = []
    for k in range(flows):
        mix = mix_ref[k]
        units.append(jnp.where(row > col, mix, 0.0))
        units.append(jnp.where(row < col, mix, 0.0))
    inner = [jnp.where(near, u, 0.0) for u in units]
    outer = [u - i for u, i in zip(units, inner)]
    power = inner
    blocks = [eye - n for n in inner]
    for _ in range(3):
        power = [mm_high(p, p) for p in power]
        blocks = [mm_high(b, eye + p) for b, p in zip(blocks, power)]
    power = [mm_high(b, o) for b, o in zip(blocks, outer)]
    whole = [eye - p for p in power]
    for _ in range(2):
        power = [mm_high(p, p) for p in power]
        whole = [mm_high(w, eye + p) for w, p in zip(whole, power)]
    inverses = [mm_high(w, b) for w, b in zip(whole, blocks)]
    for k in range(flows):
        inv_ref, lut_ref, w1t_ref, w2t_ref, w2k_ref, b2c_ref = refs[6 * k : 6 * k + 6]
        inv_ref[...] = mm_high(inverses[2 * k + 1], inverses[2 * k])
        lut_ref[...] = mm_high(units[2 * k] + eye, units[2 * k + 1] + eye).T
        for tap in range(9):
            stage1[tap * HALF : (tap + 1) * HALF, :] = 0.5 * w1_ref[k, tap].astype(F32)
            stage2[tap * CH : (tap + 1) * CH, :] = 0.5 * w2_ref[k, 8 - tap].astype(F32)
        hi, mid, low = split3(0.5 * b1_ref[k : k + 1, :])
        stage1[9 * HALF :, :] = jnp.zeros((IN_ROWS - 9 * HALF, HID), F32)
        for i, part in enumerate((hi, mid, low)):
            stage1[9 * HALF + i : 9 * HALF + i + 1, :] = part.astype(F32)
        w1t_ref[...] = stage1[...].T.astype(BF)
        w2t_ref[...] = stage2[...].T.astype(BF)
        for a in range(3):
            for b in range(3):
                w2k_ref[b * CH : (b + 1) * CH, a * HID : (a + 1) * HID] = w2_ref[k, 3 * a + b]
        b2c_ref[...] = jnp.broadcast_to(b2_ref[k : k + 1, :], (8, CH)).T


def prep(mix_factors, in_kernel, out_kernel, in_bias, out_bias):
    flows = mix_factors.shape[0]
    outs = call(
        prep_kernel,
        [
            sds((CH, CH), F32),
            sds((CH, CH), F32),
            sds((HID, IN_ROWS), BF),
            sds((HID, 9 * CH), BF),
            sds((3 * CH, 3 * HID), BF),
            sds((CH, 8), F32),
        ]
        * flows,
        [mix_factors, in_kernel, out_kernel, in_bias, out_bias],
        scratch=[pltpu.VMEM((IN_ROWS, HID), F32), pltpu.VMEM((9 * CH, HID), F32)],
        name="prep",
    )
    return [outs[i::6] for i in range(6)]


def turn_kernel(recv_ref, above_ref, mid_ref, below_ref, ya_ref, ga_ref, stage):
    width = 2 * CH
    row = lax.broadcasted_iota(jnp.int32, (width, width), 0)
    col = lax.broadcasted_iota(jnp.int32, (width, width), 1)
    pick = (col == 4 * (row % HALF) + row // HALF).astype(BF)
    none = jnp.zeros((width, width), BF)
    first = jnp.concatenate([pick, none], axis=1)
    second = jnp.concatenate([none, pick], axis=1)
    both = jnp.concatenate([pick, pick], axis=1)
    sources, count = recv_ref.shape[0], recv_ref.shape[1]
    for s in range(sources):
        stage[s * count : (s + 1) * count, :] = recv_ref[s].astype(F32)
    pair = stage[:, : 2 * width].astype(BF)
    kept = mm_nt(both, pair)
    mid_ref[...] = mm_nt(first, pair).astype(BF)
    pair = stage[:, 2 * width : 4 * width].astype(BF)
    above_ref[...] = mm_nt(first, pair).astype(BF)
    below_ref[...] = mm_nt(second, pair).astype(BF)
    grad = mm_nt(both, stage[:, 4 * width :].astype(BF))
    for k in range(4):
        ya_ref[:, k * COLS : (k + 1) * COLS] = kept[k * HALF : (k + 1) * HALF]
        ga_ref[:, k * COLS : (k + 1) * COLS] = grad[k * HALF : (k + 1) * HALF]


def turn(recv):
    return call(
        turn_kernel,
        [sds((2 * CH, COLS), BF)] * 3 + [sds((HALF, CELLS), F32)] * 2,
        [recv],
        scratch=[pltpu.VMEM((COLS, recv.shape[2]), F32)],
        name="turn",
    )


def stack_planes(even, odd, factor=None):
    if factor is not None:
        even = (even.astype(F32) * factor).astype(BF)
        odd = (odd.astype(F32) * factor).astype(BF)
    left = from_left(odd.astype(F32)).astype(BF)
    right = from_right(even.astype(F32)).astype(BF)
    return jnp.concatenate([left, even, odd, right], axis=0)


def fill_input_columns(flags_ref, above_ref, mid_ref, below_ref, columns, first, count):
    refs = {-2: (above_ref, 0), -1: (above_ref, CH), 0: (mid_ref, 0)}
    refs.update({1: (mid_ref, CH), 2: (below_ref, 0), 3: (below_ref, CH)})
    for source in range(first - 1, first + count + 1):
        ref, at = refs[source]
        factor = flags_ref[0] if source < 0 else flags_ref[1] if source > 1 else None
        stacked = stack_planes(ref[at : at + HALF], ref[at + HALF : at + CH], factor)
        for a in range(3):
            target = source - a + 1 - first
            if 0 <= target < count:
                for p in range(2):
                    lane = (2 * target + p) * COLS
                    columns[a * 144 : (a + 1) * 144, lane : lane + COLS] = stacked[
                        p * HALF : p * HALF + 144
                    ]
    extra = IN_ROWS - 9 * HALF
    row = lax.broadcasted_iota(jnp.int32, (extra, count * ROW), 0)
    columns[9 * HALF :, :] = jnp.where(row < 3, 1.0, 0.0).astype(BF)


def fill_grad_columns(flags_ref, top_ref, mid_ref, bottom_ref, columns):
    refs = [(top_ref, 0), (mid_ref, 0), (mid_ref, 2 * CH), (bottom_ref, 0)]
    for source in range(4):
        ref, at = refs[source]
        factor = flags_ref[0] if source == 0 else flags_ref[1] if source == 3 else None
        stacked = stack_planes(ref[at : at + CH], ref[at + CH : at + 2 * CH], factor)
        for a in range(3):
            target = source - a
            if 0 <= target < 2:
                for p in range(2):
                    lane = (2 * target + p) * COLS
                    columns[a * 288 : (a + 1) * 288, lane : lane + COLS] = stacked[
                        p * CH : p * CH + 288
                    ]


def put_out_grad(raw, moved, out_ref):
    for r in range(2):
        for p in range(2):
            lane = (2 * r + p) * COLS
            at = (2 * r + p) * CH
            out_ref[at : at + HALF] = raw[:, lane : lane + COLS].astype(BF)
            out_ref[at + HALF : at + CH] = moved[:, lane : lane + COLS].astype(BF)


def forward_kernel(with_grad, flags_ref, *refs):
    above_ref, mid_ref, below_ref, w1t_ref, w2k_ref, b2_ref, inv_ref, ya_ref, yb_ref = refs[:9]
    columns, pre, outs = refs[-3:]
    if with_grad:
        x_ref, rows, slope_ref, next_ref, grad_ref, moved_ref, up_ref, down_ref = refs[9:-3]
    else:
        x_ref, rows, slope_ref, scale_ref = refs[9:-3]
    fill_input_columns(flags_ref, above_ref, mid_ref, below_ref, columns, -1, 4)
    for h in range(4):
        pre[h % 2] = mm(w1t_ref[...], columns[:, h * ROW : (h + 1) * ROW])
        inside = flags_ref[0] if h == 0 else flags_ref[1] if h == 3 else None

        def activate(step, carry):
            at = pl.multiple_of(step * 16, 16)
            half = pre[h % 2, pl.ds(at, 16), :]
            bent = jnp.tanh(half)
            more = 1.0 + bent
            hidden = half * more
            if inside is not None:
                rows[pl.ds(h * HID + at, 16), :] = (hidden * inside).astype(BF)
            else:
                rows[pl.ds(h * HID + at, 16), :] = hidden.astype(BF)
                slope_ref[pl.ds((h - 1) * HID + at, 16), :] = more * (1.0 + half * (1.0 - bent))
            return carry

        lax.fori_loop(0, HID // 16, activate, 0, unroll=UNROLL)
    for r in range(2):
        taps = mm(w2k_ref[...], rows[r * HID : (r + 3) * HID, :])
        even, odd = taps[:, :COLS], taps[:, COLS:]
        lane = 2 * r * COLS
        outs[:, lane : lane + COLS] = from_left(odd[:CH]) + even[CH : 2 * CH] + odd[2 * CH :]
        outs[:, lane + COLS : lane + ROW] = even[:CH] + odd[CH : 2 * CH] + from_right(even[2 * CH :])
    raw = outs[:HALF] + b2_ref[:HALF, :1]
    shift = outs[HALF:] + b2_ref[HALF:, :1]
    inverse = 1.0 + jnp.exp(-(raw + 2.0))
    scale = 1.0 / inverse
    moved_in = yb_ref[...] * inverse - shift
    x = mm_high(inv_ref[...], jnp.concatenate([ya_ref[...], moved_in], axis=0))
    x_ref[...] = x
    if with_grad:
        moved_grad = yb_ref[...]
        moved = moved_grad * scale
        moved_ref[...] = moved
        put_out_grad((moved_grad * yb_ref[...] - 1.0) * (1.0 - scale), moved, grad_ref)
        for k in range(4):
            next_ref[k * HALF : (k + 1) * HALF] = x[:HALF, k * COLS : (k + 1) * COLS].astype(BF)
        up_ref[: 2 * CH] = grad_ref[: 2 * CH]
        down_ref[: 2 * CH] = grad_ref[2 * CH :]
        up_ref[2 * CH :] = next_ref[...]
        down_ref[2 * CH :] = next_ref[...]
    else:
        scale_ref[...] = scale


UNROLL = 4


def forward(flags, above, mid, below, w1t, w2k, b2c, inv, ya, yb, with_grad):
    outs = [sds((CH, CELLS), F32), sds((4 * HID, ROW), BF), sds((2 * HID, ROW), F32)]
    if with_grad:
        outs += [
            sds((2 * CH, COLS), BF),
            sds((4 * CH, COLS), BF),
            sds((HALF, CELLS), F32),
            sds((4 * CH, COLS), BF),
            sds((4 * CH, COLS), BF),
        ]
    else:
        outs += [sds((HALF, CELLS), F32)]
    return call(
        functools.partial(forward_kernel, with_grad),
        outs,
        [flags, above, mid, below, w1t, w2k, b2c, inv, ya, yb],
        scratch=[
            pltpu.VMEM((IN_ROWS, 4 * ROW), BF),
            pltpu.VMEM((2, HID, ROW), F32),
            pltpu.VMEM((CH, CELLS), F32),
        ],
        smem=(0,),
        flops=4 * 10**9,
        name="forward",
    )


def backward_kernel(
    flow, flags_ref, top_ref, mid_ref, bottom_ref, w2t_ref, slope_ref, w1_ref, gpre_ref, up_ref, in_ref,
    down_ref, columns, hid_grad, sums,
):
    fill_grad_columns(flags_ref, top_ref, mid_ref, bottom_ref, columns)
    sums[0] = jnp.zeros_like(sums[0])
    for r in range(2):
        hid_grad[r] = mm(w2t_ref[...], columns[:, r * ROW : (r + 1) * ROW])

        def slope(step, carry):
            at = pl.multiple_of(step * 16, 16)
            gpre_ref[pl.ds(r * HID + at, 16), :] = (
                hid_grad[r, pl.ds(at, 16), :] * slope_ref[pl.ds(r * HID + at, 16), :]
            ).astype(BF)
            return carry

        lax.fori_loop(0, HID // 16, slope, 0, unroll=UNROLL)
        taps = mm(w1_ref[flow], gpre_ref[r * HID : (r + 1) * HID, :])
        for a in range(3):
            part = taps[a * 144 : (a + 1) * 144]
            if r == 0 or a == 2:
                sums[r + a] = part
            else:
                sums[r + a] += part
    for row, (ref, at) in enumerate(((up_ref, 0), (in_ref, 0), (in_ref, CH), (down_ref, 0))):
        total = sums[row]
        even, odd = total[:, :COLS], total[:, COLS:]
        b0, b1, b2 = slice(0, HALF), slice(HALF, CH), slice(CH, 3 * HALF)
        new_even = odd[b0] + even[b1] + from_left(odd[b2])
        new_odd = from_right(even[b0]) + odd[b1] + even[b2]
        ref[at : at + HALF] = new_even.astype(ref.dtype)
        ref[at + HALF : at + CH] = new_odd.astype(ref.dtype)


def backward(flags, top, mid, bottom, w2t, slope, w1, flow):
    return call(
        functools.partial(backward_kernel, flow),
        [
            sds((2 * HID, ROW), BF),
            sds((CH, COLS), BF),
            sds((2 * CH, COLS), F32),
            sds((CH, COLS), BF),
        ],
        [flags, top, mid, bottom, w2t, slope, w1],
        scratch=[
            pltpu.VMEM((9 * CH, CELLS), BF),
            pltpu.VMEM((2, HID, ROW), F32),
            pltpu.VMEM((4, 144, ROW), F32),
        ],
        smem=(0,),
        flops=4 * 10**9,
        name="backward",
    )


def out_weight_kernel(core_ref, grad_ref, rows_ref, keep_ref, give_ref, bias_ref, left, right):
    for r in range(2):
        at = 2 * r * CH
        stacked = stack_planes(grad_ref[at : at + CH], grad_ref[at + CH : at + 2 * CH])
        left[r] = stacked[: 3 * CH]
        right[r] = stacked[CH:]
    for ref, core in ((keep_ref, core_ref[0]), (give_ref, 1 - core_ref[0])):
        at = pl.multiple_of(core * TAP_HALF, 16)
        part = [
            jnp.concatenate(
                [left[r, pl.ds(at, TAP_HALF), :], right[r, pl.ds(at, TAP_HALF), :]], axis=1
            )
            for r in range(2)
        ]
        for a in range(3):
            ref[a] = mm_nt(part[0], rows_ref[a * HID : (a + 1) * HID]) + mm_nt(
                part[1], rows_ref[(a + 1) * HID : (a + 2) * HID]
            )
    ones = jnp.ones((8, COLS), BF)
    total = mm_nt(ones, grad_ref[:CH]) + mm_nt(ones, grad_ref[CH : 2 * CH])
    bias_ref[...] = total + (
        mm_nt(ones, grad_ref[2 * CH : 3 * CH]) + mm_nt(ones, grad_ref[3 * CH :])
    )


def out_weight(core, grad, rows):
    return call(
        out_weight_kernel,
        [sds((3, TAP_HALF, HID), F32), sds((3, TAP_HALF, HID), F32), sds((8, CH), F32)],
        [core, grad, rows],
        scratch=[pltpu.VMEM((2, 3 * CH, COLS), BF), pltpu.VMEM((2, 3 * CH, COLS), BF)],
        smem=(0,),
        flops=2 * 10**9,
        name="out_weight",
    )


def in_weight_kernel(
    core_ref, flags_ref, above_ref, mid_ref, below_ref, gpre_ref, keep_ref, give_ref, columns
):
    fill_input_columns(flags_ref, above_ref, mid_ref, below_ref, columns, 0, 2)
    for ref, core in ((keep_ref, core_ref[0]), (give_ref, 1 - core_ref[0])):
        at = pl.multiple_of(core * IN_HALF, 16)
        part = columns[pl.ds(at, IN_HALF), :]
        ref[...] = mm_nt(part[:, :ROW], gpre_ref[:HID]) + mm_nt(part[:, ROW:], gpre_ref[HID:])


def in_weight(core, flags, above, mid, below, gpre):
    return call(
        in_weight_kernel,
        [sds((IN_HALF, HID), F32), sds((IN_HALF, HID), F32)],
        [core, flags, above, mid, below, gpre],
        scratch=[pltpu.VMEM((IN_ROWS, CELLS), BF)],
        smem=(0, 1),
        flops=10**9,
        name="in_weight",
    )


def close_kernel(next_step, flow, core_ref, flags_ref, *refs):
    in_ref, low_ref, high_ref, ga_ref, moved_ref, lut_ref, x_ref, mix_ref, bias_ref = refs[:9]
    whole, small = refs[-2:]
    if next_step:
        scale_ref, gx_ref, keep_ref, give_ref, grad_ref, nmoved_ref = refs[9:-2]
    else:
        gx_ref, keep_ref, give_ref = refs[9:-2]
    for k in range(4):
        part = in_ref[k * HALF : (k + 1) * HALF]
        if k < 2:
            part = part + flags_ref[0] * low_ref[k * HALF : (k + 1) * HALF].astype(F32)
        else:
            part = part + flags_ref[1] * high_ref[(k - 2) * HALF : (k - 1) * HALF].astype(F32)
        lane = k * COLS
        whole[:HALF, lane : lane + COLS] = ga_ref[:HALF, lane : lane + COLS] + part
    whole[HALF:] = moved_ref[...]
    gx = mm_high(lut_ref[...], whole[...])
    gx_ref[...] = gx
    if next_step:
        scale = scale_ref[...]
        moved_grad = gx[HALF:]
        moved = moved_grad * scale
        nmoved_ref[...] = moved
        put_out_grad((moved_grad * x_ref[HALF:] - 1.0) * (1.0 - scale), moved, grad_ref)
    ghi, gmid, _ = split3(whole[...])
    xhi, xmid, _ = split3(x_ref[...])
    outer = mm_nt(ghi, xhi) + (mm_nt(ghi, xmid) + mm_nt(gmid, xhi))
    row = lax.broadcasted_iota(jnp.int32, (CH, CH), 0)
    col = lax.broadcasted_iota(jnp.int32, (CH, CH), 1)
    eye = (row == col).astype(F32)
    mix = mix_ref[flow]
    lower = jnp.where(row > col, mix, 0.0) + eye
    upper = jnp.where(row < col, mix, 0.0) + eye
    by_upper = mm_high(outer, upper.T)
    by_lower = mm_high(lower.T, outer)
    small[:, :CH] = jnp.where(row > col, by_upper, jnp.where(row < col, by_lower, 0.0))
    small[:, CH:] = jnp.zeros((CH, 2 * 128 - CH), F32)
    small[:8, 128 : 128 + CH] = bias_ref[...]
    for ref, core in ((keep_ref, core_ref[0]), (give_ref, 1 - core_ref[0])):
        ref[...] = small[pl.ds(pl.multiple_of(core * HALF, 8), HALF), :]


def close(core, flags, gin, low, high, ga, moved, lut, x, mix, flow, bias, scale=None):
    outs = [sds((CH, CELLS), F32), sds((HALF, 256), F32), sds((HALF, 256), F32)]
    ins = [core, flags, gin, low, high, ga, moved, lut, x, mix, bias]
    if scale is not None:
        outs += [sds((4 * CH, COLS), BF), sds((HALF, CELLS), F32)]
        ins += [scale]
    return call(
        functools.partial(close_kernel, scale is not None, flow),
        outs,
        ins,
        scratch=[pltpu.VMEM((CH, CELLS), F32), pltpu.VMEM((CH, 256), F32)],
        smem=(0, 1),
        flops=10**9,
        name="close",
    )


def weave_kernel(x_ref, out_ref):
    size = 256
    row = lax.broadcasted_iota(jnp.int32, (size, size), 0)
    col = lax.broadcasted_iota(jnp.int32, (size, size), 1)
    place = (col == 2 * (row % 128) + row // 128).astype(BF)
    for r in range(2):
        for t in range(3):
            lane = r * ROW + t * 128
            pair = jnp.concatenate(
                [x_ref[:, lane : lane + 128], x_ref[:, lane + COLS : lane + COLS + 128]], axis=1
            )
            hi, mid, low = split3(pair)
            woven = mm(hi, place) + (mm(mid, place) + mm(low, place))
            out_ref[0, :, r, t * size : (t + 1) * size] = woven


def weave(x):
    return call(weave_kernel, [sds((1, CH, 2, ROW), F32)], [x], name="weave")[0]


PARTS = ((0, IN_HALF), (224, TAP_HALF), (368, TAP_HALF), (512, TAP_HALF), (656, HALF))
FLOW_ROWS = 704
GROUP = 88


def merge_kernel(*refs):
    out_ref, total = refs[-2:]
    for k in range(2):
        own_in, own_out, own_small, got_in, got_out, got_small = refs[6 * k : 6 * k + 6]
        at = k * FLOW_ROWS
        total[at : at + IN_HALF] = own_in[...] + got_in[...]
        for a in range(3):
            start = at + IN_HALF + a * TAP_HALF
            total[start : start + TAP_HALF] = own_out[a] + got_out[a]
        small = own_small[...] + got_small[...]
        start = at + FLOW_ROWS - HALF
        total[start : start + HALF, :256] = small
        total[start : start + HALF, 256:] = small - small.astype(BF).astype(F32)
    for g in range(2 * FLOW_ROWS // GROUP):
        for lane in range(4):
            out_ref[4 * g + lane] = total[
                g * GROUP : (g + 1) * GROUP, lane * 128 : (lane + 1) * 128
            ].astype(BF)


def merge(own0, got0, own1, got1):
    shares = 2 * FLOW_ROWS // GROUP * 4
    return call(
        merge_kernel,
        [sds((shares, GROUP, 128), BF)],
        [*own0, *got0, *own1, *got1],
        scratch=[pltpu.VMEM((2 * FLOW_ROWS, HID), F32)],
        name="merge",
    )[0]


def total_kernel(cells, shares_ref, out_ref):
    total = shares_ref[0].astype(F32)
    for s in range(1, shares_ref.shape[0]):
        total += shares_ref[s].astype(F32)
    mean = (total * (1.0 / cells)).astype(BF)
    for s in range(shares_ref.shape[0]):
        out_ref[s] = mean


def totals(shares, cells):
    return call(
        functools.partial(total_kernel, cells), [sds(shares.shape, BF)], [shares], name="totals"
    )[0]


def unpack_kernel(core_ref, mine_ref, other_ref, win_ref, wout_ref, mix_ref, bin_ref, bout_ref, rows):
    mine_first = core_ref[0] == 0
    for half in range(2):
        for g in range(2 * FLOW_ROWS // GROUP):
            for lane in range(4):
                mine = mine_ref[4 * g + lane].astype(F32)
                other = other_ref[4 * g + lane].astype(F32)
                first, second = (mine, other) if half == 0 else (other, mine)
                rows[half, g * GROUP : (g + 1) * GROUP, lane * 128 : (lane + 1) * 128] = jnp.where(
                    mine_first, first, second
                )
    for k in range(2):
        at = k * FLOW_ROWS
        win_ref[k, :IN_HALF] = rows[0, at : at + IN_HALF]
        win_ref[k, IN_HALF:] = rows[1, at : at + 9 * HALF - IN_HALF]
        bin_ref[k : k + 1, :] = rows[1, at + 9 * HALF - IN_HALF : at + 9 * HALF - IN_HALF + 1]
        for a in range(3):
            start = at + IN_HALF + a * TAP_HALF
            wout_ref[k, 3 * a + 2] = rows[0, start : start + CH]
            wout_ref[k, 3 * a + 1, :HALF] = rows[0, start + CH : start + TAP_HALF]
            wout_ref[k, 3 * a + 1, HALF:] = rows[1, start : start + HALF]
            wout_ref[k, 3 * a] = rows[1, start + HALF : start + TAP_HALF]
        start = at + FLOW_ROWS - HALF
        for half in range(2):
            block = rows[half, start : start + HALF]
            mix_ref[k, half * HALF : (half + 1) * HALF] = block[:, :CH] + block[:, 256 : 256 + CH]
        block = rows[0, start : start + 8]
        bout_ref[k] = block[:, 128 : 128 + CH] + block[:, 384 : 384 + CH]


def unpack(core, mine, other):
    return call(
        unpack_kernel,
        [
            sds((2, 9 * HALF, HID), F32),
            sds((2, 9, CH, HID), F32),
            sds((2, CH, CH), F32),
            sds((2, HID), F32),
            sds((2, 8, CH), F32),
        ],
        [core, mine, other],
        scratch=[pltpu.VMEM((2, 2 * FLOW_ROWS, HID), F32)],
        smem=(0,),
        name="unpack",
    )


def local(passed_on, passed_grad, latent, mix_factors, in_kernel, in_bias, out_kernel, out_bias):
    lat_index = lax.axis_index(LAT)
    lat_count = lax.axis_size(LAT)
    forth = [(i, (i + 1) % lat_count) for i in range(lat_count)]
    back = [(t, s) for s, t in forth]
    swap = [(0, 1), (1, 0)]
    flags = jnp.stack([lat_index > 0, lat_index < lat_count - 1]).astype(F32)
    core = lax.axis_index("c").astype(jnp.int32).reshape(1)

    block = payload(
        jnp.transpose(passed_on[0], (1, 2, 0)), jnp.transpose(passed_grad[0], (1, 2, 0))
    )
    recv = lax.all_to_all(block, LAT, 0, 0, tiled=True)
    inv, lut, w1t, w2t, w2k, b2c = prep(mix_factors, in_kernel, out_kernel, in_bias, out_bias)
    w1 = in_kernel.reshape(2, 9 * HALF, HID)
    yb = latent.reshape(HALF, CELLS)

    above, mid, below, ya, ga = turn(recv)
    x1, rows1, slope1, next_mid, grad1, moved1, up, down = forward(
        flags, above, mid, below, w1t[1], w2k[1], b2c[1], inv[1], ya, yb, True
    )
    from_above = lax.ppermute(down, LAT, forth)
    from_below = lax.ppermute(up, LAT, back)
    keep_out1, give_out1, bias1 = out_weight(core, grad1, rows1)
    top1, above0 = from_above[: 2 * CH], from_above[2 * CH :]
    bottom1, below0 = from_below[: 2 * CH], from_below[2 * CH :]
    gpre1, up1, in1, down1 = backward(flags, top1, grad1, bottom1, w2t[1], slope1, w1, 1)
    low1 = lax.ppermute(down1, LAT, forth)
    high1 = lax.ppermute(up1, LAT, back)
    got_out1 = lax.ppermute(give_out1, "c", swap)
    x0, rows0, slope0, scale0 = forward(
        flags, above0, next_mid, below0, w1t[0], w2k[0], b2c[0], inv[0],
        x1[:HALF], x1[HALF:], False,
    )
    gx1, keep_small1, give_small1, grad0, moved0 = close(
        core, flags, in1, low1, high1, ga, moved1, lut[1], x1, mix_factors, 1, bias1, scale0
    )
    top0 = lax.ppermute(grad0[2 * CH :], LAT, forth)
    bottom0 = lax.ppermute(grad0[: 2 * CH], LAT, back)
    keep_in1, give_in1 = in_weight(core, flags, above, mid, below, gpre1)
    keep_out0, give_out0, bias0 = out_weight(core, grad0, rows0)
    got_in1 = lax.ppermute(give_in1, "c", swap)
    got_small1 = lax.ppermute(give_small1, "c", swap)
    got_out0 = lax.ppermute(give_out0, "c", swap)
    gpre0, up0, in0, down0 = backward(flags, top0, grad0, bottom0, w2t[0], slope0, w1, 0)
    low0 = lax.ppermute(down0, LAT, forth)
    high0 = lax.ppermute(up0, LAT, back)
    keep_in0, give_in0 = in_weight(core, flags, above0, next_mid, below0, gpre0)
    got_in0 = lax.ppermute(give_in0, "c", swap)
    gx0, keep_small0, give_small0 = close(
        core, flags, in0, low0, high0, gx1, moved0, lut[0], x0, mix_factors, 0, bias0
    )
    got_small0 = lax.ppermute(give_small0, "c", swap)

    shares = lax.all_to_all(
        merge(
            (keep_in0, keep_out0, keep_small0),
            (got_in0, got_out0, got_small0),
            (keep_in1, keep_out1, keep_small1),
            (got_in1, got_out1, got_small1),
        ),
        CHIPS, 0, 0, tiled=True,
    )
    cells = float(CELLS * lat_count * lax.axis_size(ENS))
    mine = lax.all_to_all(totals(shares, cells), CHIPS, 0, 0, tiled=True)
    other = lax.ppermute(mine, "c", swap)
    rebuilt = weave(x0)
    input_grad = weave(gx0)
    in_grad, out_grad, mix_grad, in_bias_grad, out_bias_grad = unpack(core, mine, other)
    return (
        rebuilt,
        input_grad,
        mix_grad,
        in_grad.reshape(2, 9, HALF, HID),
        in_bias_grad,
        out_grad,
        out_bias_grad[:, 0],
    )


def solution(mesh):
    split = Mesh(mesh.devices.reshape(4, 2, 2, 4, 2), ("y", "xl", "c", "z", "xh"))
    return jax.shard_map(
        local,
        mesh=split,
        in_specs=(
            P(ENS, None, None, LAT),
            P(ENS, None, None, LAT),
            P(ENS, None, LAT, None),
            P(),
            P(),
            P(),
            P(),
            P(),
        ),
        out_specs=(P(ENS, None, LAT, None), P(ENS, None, LAT, None), P(), P(), P(), P(), P()),
        check_vma=False,
    )
```

```python
import functools

import jax
import jax.numpy as jnp
from jax import lax
from jax.experimental import pallas as pl
from jax.experimental.pallas import tpu as pltpu
from jax.sharding import Mesh, PartitionSpec as P

BF = jnp.bfloat16
F32 = jnp.float32
HIGH = lax.Precision.HIGHEST
LAT = ("y", "xl", "c")
ENS = ("z", "xh")
CHIPS = ("y", "xl", "z", "xh")
HALF = 48
CH = 96
HID = 512
COLS = 384
ROW = 768
CELLS = 1536
IN_ROWS = 448
IN_HALF = 224
TAP_HALF = 144
MIB = 1024 * 1024


def mm(a, b):
    return lax.dot_general(a, b, (((1,), (0,)), ((), ())), preferred_element_type=F32)


def mm_nt(a, b):
    return lax.dot_general(a, b, (((1,), (1,)), ((), ())), preferred_element_type=F32)


def mm_high(a, b):
    return lax.dot_general(
        a, b, (((1,), (0,)), ((), ())), preferred_element_type=F32, precision=HIGH
    )


def split3(x):
    hi = x.astype(BF)
    rest = x - hi.astype(F32)
    mid = rest.astype(BF)
    low = (rest - mid.astype(F32)).astype(BF)
    return hi, mid, low


def from_left(x):
    lane = lax.broadcasted_iota(jnp.int32, x.shape, 1)
    return jnp.where(lane == 0, 0.0, pltpu.roll(x, 1, 1))


def from_right(x):
    width = x.shape[1]
    lane = lax.broadcasted_iota(jnp.int32, x.shape, 1)
    return jnp.where(lane == width - 1, 0.0, pltpu.roll(x, width - 1, 1))


def sds(shape, dtype):
    return jax.ShapeDtypeStruct(shape, dtype)


def call(body, outs, ins, scratch=(), smem=(), flops=0, name=None, limit=16):
    moved = sum(x.size * x.dtype.itemsize for x in list(ins) + list(outs))
    return pl.pallas_call(
        body,
        out_shape=outs,
        in_specs=[
            pl.BlockSpec(memory_space=pltpu.SMEM if i in smem else pltpu.VMEM)
            for i in range(len(ins))
        ],
        out_specs=[pl.BlockSpec(memory_space=pltpu.VMEM) for _ in outs],
        scratch_shapes=list(scratch),
        compiler_params=pltpu.CompilerParams(vmem_limit_bytes=limit * MIB),
        cost_estimate=pl.CostEstimate(flops=flops, bytes_accessed=moved, transcendentals=0),
        name=name,
    )(*ins)


def payload_kernel(on_ref, grad_ref, out_ref):
    bands, width = on_ref.shape[2], 2 * CH
    blank = jnp.zeros(on_ref.shape[1:], BF)
    for s in range(on_ref.shape[0]):
        on = on_ref[s]
        hi = on.astype(BF)
        grad = grad_ref[s]
        ghi = grad.astype(BF)
        out_ref[s, :, :width] = hi
        out_ref[s, :, width : 2 * width] = (on - hi.astype(F32)).astype(BF)
        if s + 1 < on_ref.shape[0]:
            out_ref[s + 1, :, 2 * width : 3 * width] = hi
        if s > 0:
            out_ref[s - 1, :, 3 * width : 4 * width] = hi
        out_ref[s, :, 4 * width : 5 * width] = ghi
        out_ref[s, :, 5 * width : 6 * width] = (grad - ghi.astype(F32)).astype(BF)
    out_ref[0, :, 2 * width : 3 * width] = blank
    out_ref[on_ref.shape[0] - 1, :, 3 * width : 4 * width] = blank


def payload(on, grad):
    bands, width, channels = on.shape
    return call(
        payload_kernel, [sds((bands, width, 6 * channels), BF)], [on, grad], name="payload", limit=56
    )[0]


def prep_kernel(
    mix_ref, w1_ref, w2_ref, b1_ref, b2_ref, *refs
):
    stage1, stage2 = refs[-2:]
    flows = mix_ref.shape[0]
    row = lax.broadcasted_iota(jnp.int32, (CH, CH), 0)
    col = lax.broadcasted_iota(jnp.int32, (CH, CH), 1)
    eye = (row == col).astype(F32)
    near = (row // 16) == (col // 16)
    units = []
    for k in range(flows):
        mix = mix_ref[k]
        units.append(jnp.where(row > col, mix, 0.0))
        units.append(jnp.where(row < col, mix, 0.0))
    inner = [jnp.where(near, u, 0.0) for u in units]
    outer = [u - i for u, i in zip(units, inner)]
    power = inner
    blocks = [eye - n for n in inner]
    for _ in range(3):
        power = [mm_high(p, p) for p in power]
        blocks = [mm_high(b, eye + p) for b, p in zip(blocks, power)]
    power = [mm_high(b, o) for b, o in zip(blocks, outer)]
    whole = [eye - p for p in power]
    for _ in range(2):
        power = [mm_high(p, p) for p in power]
        whole = [mm_high(w, eye + p) for w, p in zip(whole, power)]
    inverses = [mm_high(w, b) for w, b in zip(whole, blocks)]
    for k in range(flows):
        inv_ref, lut_ref, w1t_ref, w2t_ref, w2k_ref, w1k_ref, b2c_ref = refs[7 * k : 7 * k + 7]
        inv_ref[...] = mm_high(inverses[2 * k + 1], inverses[2 * k])
        lut_ref[...] = mm_high(units[2 * k] + eye, units[2 * k + 1] + eye).T
        for tap in range(9):
            stage1[tap * HALF : (tap + 1) * HALF, :] = 0.5 * w1_ref[k, tap].astype(F32)
            stage2[tap * CH : (tap + 1) * CH, :] = 0.5 * w2_ref[k, 8 - tap].astype(F32)
        hi, mid, low = split3(0.5 * b1_ref[k : k + 1, :])
        stage1[9 * HALF :, :] = jnp.zeros((IN_ROWS - 9 * HALF, HID), F32)
        for i, part in enumerate((hi, mid, low)):
            stage1[9 * HALF + i : 9 * HALF + i + 1, :] = part.astype(F32)
        w1t_ref[...] = stage1[...].T.astype(BF)
        w2t_ref[...] = stage2[...].T.astype(BF)
        for a in range(3):
            for b in range(3):
                w2k_ref[b * CH : (b + 1) * CH, a * HID : (a + 1) * HID] = w2_ref[k, 3 * a + b]
                w1k_ref[b * HALF : (b + 1) * HALF, a * HID : (a + 1) * HID] = w1_ref[
                    k, 3 * (2 - a) + b
                ]
        b2c_ref[...] = jnp.broadcast_to(b2_ref[k : k + 1, :], (8, CH)).T


def prep(mix_factors, in_kernel, out_kernel, in_bias, out_bias):
    flows = mix_factors.shape[0]
    outs = call(
        prep_kernel,
        [
            sds((CH, CH), F32),
            sds((CH, CH), F32),
            sds((HID, IN_ROWS), BF),
            sds((HID, 9 * CH), BF),
            sds((3 * CH, 3 * HID), BF),
            sds((3 * HALF, 3 * HID), BF),
            sds((CH, 8), F32),
        ]
        * flows,
        [mix_factors, in_kernel, out_kernel, in_bias, out_bias],
        scratch=[pltpu.VMEM((IN_ROWS, HID), F32), pltpu.VMEM((9 * CH, HID), F32)],
        name="prep",
        limit=56,
    )
    return [outs[i::7] for i in range(7)]


def turn_kernel(recv_ref, above_ref, mid_ref, below_ref, ya_ref, ga_ref, stage):
    width = 2 * CH
    row = lax.broadcasted_iota(jnp.int32, (width, width), 0)
    col = lax.broadcasted_iota(jnp.int32, (width, width), 1)
    pick = (col == 4 * (row % HALF) + row // HALF).astype(BF)
    none = jnp.zeros((width, width), BF)
    first = jnp.concatenate([pick, none], axis=1)
    second = jnp.concatenate([none, pick], axis=1)
    both = jnp.concatenate([pick, pick], axis=1)
    sources, count = recv_ref.shape[0], recv_ref.shape[1]
    for s in range(sources):
        stage[s * count : (s + 1) * count, :] = recv_ref[s].astype(F32)
    pair = stage[:, : 2 * width].astype(BF)
    kept = mm_nt(both, pair)
    mid_ref[...] = mm_nt(first, pair).astype(BF)
    pair = stage[:, 2 * width : 4 * width].astype(BF)
    above_ref[...] = mm_nt(first, pair).astype(BF)
    below_ref[...] = mm_nt(second, pair).astype(BF)
    grad = mm_nt(both, stage[:, 4 * width :].astype(BF))
    for k in range(4):
        ya_ref[:, k * COLS : (k + 1) * COLS] = kept[k * HALF : (k + 1) * HALF]
        ga_ref[:, k * COLS : (k + 1) * COLS] = grad[k * HALF : (k + 1) * HALF]


def turn(recv):
    return call(
        turn_kernel,
        [sds((2 * CH, COLS), BF)] * 3 + [sds((HALF, CELLS), F32)] * 2,
        [recv],
        scratch=[pltpu.VMEM((COLS, recv.shape[2]), F32)],
        name="turn",
    )


def stack_planes(even, odd, factor=None):
    if factor is not None:
        even = (even.astype(F32) * factor).astype(BF)
        odd = (odd.astype(F32) * factor).astype(BF)
    left = from_left(odd.astype(F32)).astype(BF)
    right = from_right(even.astype(F32)).astype(BF)
    return jnp.concatenate([left, even, odd, right], axis=0)


def fill_input_columns(flags_ref, above_ref, mid_ref, below_ref, columns, first, count):
    refs = {-2: (above_ref, 0), -1: (above_ref, CH), 0: (mid_ref, 0)}
    refs.update({1: (mid_ref, CH), 2: (below_ref, 0), 3: (below_ref, CH)})
    for source in range(first - 1, first + count + 1):
        ref, at = refs[source]
        factor = flags_ref[0] if source < 0 else flags_ref[1] if source > 1 else None
        stacked = stack_planes(ref[at : at + HALF], ref[at + HALF : at + CH], factor)
        for a in range(3):
            target = source - a + 1 - first
            if 0 <= target < count:
                for p in range(2):
                    lane = (2 * target + p) * COLS
                    columns[a * 144 : (a + 1) * 144, lane : lane + COLS] = stacked[
                        p * HALF : p * HALF + 144
                    ]
    extra = IN_ROWS - 9 * HALF
    row = lax.broadcasted_iota(jnp.int32, (extra, count * ROW), 0)
    columns[9 * HALF :, :] = jnp.where(row < 3, 1.0, 0.0).astype(BF)


def fill_grad_columns(flags_ref, above_ref, mid_ref, below_ref, columns):
    for source in range(-2, 4):
        ref = above_ref if source < 0 else below_ref if source > 1 else mid_ref
        factor = flags_ref[0] if source < 0 else flags_ref[1] if source > 1 else None
        at = (source % 2) * 2 * CH
        stacked = stack_planes(ref[at : at + CH], ref[at + CH : at + 2 * CH], factor)
        for a in range(3):
            target = source - a + 2
            if 0 <= target < 4:
                for p in range(2):
                    lane = (2 * target + p) * COLS
                    columns[a * 288 : (a + 1) * 288, lane : lane + COLS] = stacked[
                        p * CH : p * CH + 288
                    ]


def put_out_grad(raw, moved, out_ref):
    for r in range(2):
        for p in range(2):
            lane = (2 * r + p) * COLS
            at = (2 * r + p) * CH
            out_ref[at : at + HALF] = raw[:, lane : lane + COLS].astype(BF)
            out_ref[at + HALF : at + CH] = moved[:, lane : lane + COLS].astype(BF)


def forward_kernel(with_grad, flags_ref, *refs):
    above_ref, mid_ref, below_ref, w1t_ref, w2k_ref, b2_ref, inv_ref, ya_ref, yb_ref = refs[:9]
    columns, pre, outs = refs[-3:]
    if with_grad:
        x_ref, rows, slope_ref, next_ref, grad_ref, moved_ref = refs[9:-3]
    else:
        x_ref, rows, slope_ref, scale_ref = refs[9:-3]
    fill_input_columns(flags_ref, above_ref, mid_ref, below_ref, columns, -1, 4)
    for h in range(4):
        pre[h % 2] = mm(w1t_ref[...], columns[:, h * ROW : (h + 1) * ROW])
        inside = flags_ref[0] if h == 0 else flags_ref[1] if h == 3 else None

        def activate(step, carry):
            at = pl.multiple_of(step * 16, 16)
            half = pre[h % 2, pl.ds(at, 16), :]
            bent = jnp.tanh(half)
            more = 1.0 + bent
            hidden = half * more
            slope = more * (1.0 + half * (1.0 - bent))
            if inside is not None:
                hidden = hidden * inside
                slope = slope * inside
            rows[pl.ds(h * HID + at, 16), :] = hidden.astype(BF)
            slope_ref[pl.ds(h * HID + at, 16), :] = slope
            return carry

        lax.fori_loop(0, HID // 16, activate, 0, unroll=UNROLL)
    for r in range(2):
        taps = mm(w2k_ref[...], rows[r * HID : (r + 3) * HID, :])
        even, odd = taps[:, :COLS], taps[:, COLS:]
        lane = 2 * r * COLS
        outs[:, lane : lane + COLS] = from_left(odd[:CH]) + even[CH : 2 * CH] + odd[2 * CH :]
        outs[:, lane + COLS : lane + ROW] = even[:CH] + odd[CH : 2 * CH] + from_right(even[2 * CH :])
    raw = outs[:HALF] + b2_ref[:HALF, :1]
    shift = outs[HALF:] + b2_ref[HALF:, :1]
    inverse = 1.0 + jnp.exp(-(raw + 2.0))
    scale = 1.0 / inverse
    moved_in = yb_ref[...] * inverse - shift
    x = mm_high(inv_ref[...], jnp.concatenate([ya_ref[...], moved_in], axis=0))
    x_ref[...] = x
    if with_grad:
        moved_grad = yb_ref[...]
        moved = moved_grad * scale
        moved_ref[...] = moved
        put_out_grad((moved_grad * yb_ref[...] - 1.0) * (1.0 - scale), moved, grad_ref)
        for k in range(4):
            next_ref[k * HALF : (k + 1) * HALF] = x[:HALF, k * COLS : (k + 1) * COLS].astype(BF)
    else:
        scale_ref[...] = scale


UNROLL = 4


def forward(flags, above, mid, below, w1t, w2k, b2c, inv, ya, yb, with_grad):
    outs = [sds((CH, CELLS), F32), sds((4 * HID, ROW), BF), sds((4 * HID, ROW), F32)]
    if with_grad:
        outs += [
            sds((2 * CH, COLS), BF),
            sds((4 * CH, COLS), BF),
            sds((HALF, CELLS), F32),
        ]
    else:
        outs += [sds((HALF, CELLS), F32)]
    return call(
        functools.partial(forward_kernel, with_grad),
        outs,
        [flags, above, mid, below, w1t, w2k, b2c, inv, ya, yb],
        scratch=[
            pltpu.VMEM((IN_ROWS, 4 * ROW), BF),
            pltpu.VMEM((2, HID, ROW), F32),
            pltpu.VMEM((CH, CELLS), F32),
        ],
        smem=(0,),
        flops=4 * 10**9,
        name="forward",
    )


def backward_kernel(
    flags_ref, above_ref, mid_ref, below_ref, w2t_ref, slope_ref, w1k_ref, gpre_ref, in_ref,
    columns, hid_grad,
):
    fill_grad_columns(flags_ref, above_ref, mid_ref, below_ref, columns)
    for h in range(4):
        hid_grad[h % 2] = mm(w2t_ref[...], columns[:, h * ROW : (h + 1) * ROW])

        def slope(step, carry):
            at = pl.multiple_of(step * 16, 16)
            gpre_ref[pl.ds(h * HID + at, 16), :] = (
                hid_grad[h % 2, pl.ds(at, 16), :] * slope_ref[pl.ds(h * HID + at, 16), :]
            ).astype(BF)
            return carry

        lax.fori_loop(0, HID // 16, slope, 0, unroll=UNROLL)
    b0, b1, b2 = slice(0, HALF), slice(HALF, CH), slice(CH, 3 * HALF)
    for r in range(2):
        taps = mm(w1k_ref[...], gpre_ref[r * HID : (r + 3) * HID, :])
        even, odd = taps[:, :COLS], taps[:, COLS:]
        in_ref[r * CH : r * CH + HALF] = odd[b0] + even[b1] + from_left(odd[b2])
        in_ref[r * CH + HALF : (r + 1) * CH] = from_right(even[b0]) + odd[b1] + even[b2]


def backward(flags, above, mid, below, w2t, slope, w1k):
    return call(
        backward_kernel,
        [sds((4 * HID, ROW), BF), sds((2 * CH, COLS), F32)],
        [flags, above, mid, below, w2t, slope, w1k],
        scratch=[pltpu.VMEM((9 * CH, 4 * ROW), BF), pltpu.VMEM((2, HID, ROW), F32)],
        smem=(0,),
        flops=6 * 10**9,
        name="backward",
    )


def out_weight_kernel(core_ref, grad_ref, rows_ref, keep_ref, give_ref, bias_ref, left, right):
    for r in range(2):
        at = 2 * r * CH
        stacked = stack_planes(grad_ref[at : at + CH], grad_ref[at + CH : at + 2 * CH])
        left[r] = stacked[: 3 * CH]
        right[r] = stacked[CH:]
    for ref, core in ((keep_ref, core_ref[0]), (give_ref, 1 - core_ref[0])):
        at = pl.multiple_of(core * TAP_HALF, 16)
        part = [
            jnp.concatenate(
                [left[r, pl.ds(at, TAP_HALF), :], right[r, pl.ds(at, TAP_HALF), :]], axis=1
            )
            for r in range(2)
        ]
        for a in range(3):
            ref[a] = mm_nt(part[0], rows_ref[a * HID : (a + 1) * HID]) + mm_nt(
                part[1], rows_ref[(a + 1) * HID : (a + 2) * HID]
            )
    ones = jnp.ones((8, COLS), BF)
    total = mm_nt(ones, grad_ref[:CH]) + mm_nt(ones, grad_ref[CH : 2 * CH])
    bias_ref[...] = total + (
        mm_nt(ones, grad_ref[2 * CH : 3 * CH]) + mm_nt(ones, grad_ref[3 * CH :])
    )


def out_weight(core, grad, rows):
    return call(
        out_weight_kernel,
        [sds((3, TAP_HALF, HID), F32), sds((3, TAP_HALF, HID), F32), sds((8, CH), F32)],
        [core, grad, rows],
        scratch=[pltpu.VMEM((2, 3 * CH, COLS), BF), pltpu.VMEM((2, 3 * CH, COLS), BF)],
        smem=(0,),
        flops=2 * 10**9,
        name="out_weight",
    )


def in_weight_kernel(
    core_ref, flags_ref, above_ref, mid_ref, below_ref, gpre_ref, keep_ref, give_ref, columns
):
    fill_input_columns(flags_ref, above_ref, mid_ref, below_ref, columns, 0, 2)
    for ref, core in ((keep_ref, core_ref[0]), (give_ref, 1 - core_ref[0])):
        at = pl.multiple_of(core * IN_HALF, 16)
        part = columns[pl.ds(at, IN_HALF), :]
        ref[...] = mm_nt(part[:, :ROW], gpre_ref[HID : 2 * HID]) + mm_nt(
            part[:, ROW:], gpre_ref[2 * HID : 3 * HID]
        )


def in_weight(core, flags, above, mid, below, gpre):
    return call(
        in_weight_kernel,
        [sds((IN_HALF, HID), F32), sds((IN_HALF, HID), F32)],
        [core, flags, above, mid, below, gpre],
        scratch=[pltpu.VMEM((IN_ROWS, CELLS), BF)],
        smem=(0, 1),
        flops=10**9,
        name="in_weight",
    )


def close_kernel(next_step, flow, core_ref, *refs):
    in_ref, ga_ref, moved_ref, lut_ref, x_ref, mix_ref, bias_ref = refs[:7]
    whole, small = refs[-2:]
    if next_step:
        scale_ref, gx_ref, keep_ref, give_ref, grad_ref, nmoved_ref = refs[7:-2]
    else:
        gx_ref, keep_ref, give_ref = refs[7:-2]
    for k in range(4):
        lane = k * COLS
        whole[:HALF, lane : lane + COLS] = (
            ga_ref[:HALF, lane : lane + COLS] + in_ref[k * HALF : (k + 1) * HALF]
        )
    whole[HALF:] = moved_ref[...]
    gx = mm_high(lut_ref[...], whole[...])
    gx_ref[...] = gx
    if next_step:
        scale = scale_ref[...]
        moved_grad = gx[HALF:]
        moved = moved_grad * scale
        nmoved_ref[...] = moved
        put_out_grad((moved_grad * x_ref[HALF:] - 1.0) * (1.0 - scale), moved, grad_ref)
    ghi, gmid, _ = split3(whole[...])
    xhi, xmid, _ = split3(x_ref[...])
    outer = mm_nt(ghi, xhi) + (mm_nt(ghi, xmid) + mm_nt(gmid, xhi))
    row = lax.broadcasted_iota(jnp.int32, (CH, CH), 0)
    col = lax.broadcasted_iota(jnp.int32, (CH, CH), 1)
    eye = (row == col).astype(F32)
    mix = mix_ref[flow]
    lower = jnp.where(row > col, mix, 0.0) + eye
    upper = jnp.where(row < col, mix, 0.0) + eye
    by_upper = mm_high(outer, upper.T)
    by_lower = mm_high(lower.T, outer)
    small[:, :CH] = jnp.where(row > col, by_upper, jnp.where(row < col, by_lower, 0.0))
    small[:, CH:] = jnp.zeros((CH, 2 * 128 - CH), F32)
    small[:8, 128 : 128 + CH] = bias_ref[...]
    for ref, core in ((keep_ref, core_ref[0]), (give_ref, 1 - core_ref[0])):
        ref[...] = small[pl.ds(pl.multiple_of(core * HALF, 8), HALF), :]


def close(core, gin, ga, moved, lut, x, mix, flow, bias, scale=None):
    outs = [sds((CH, CELLS), F32), sds((HALF, 256), F32), sds((HALF, 256), F32)]
    ins = [core, gin, ga, moved, lut, x, mix, bias]
    if scale is not None:
        outs += [sds((4 * CH, COLS), BF), sds((HALF, CELLS), F32)]
        ins += [scale]
    return call(
        functools.partial(close_kernel, scale is not None, flow),
        outs,
        ins,
        scratch=[pltpu.VMEM((CH, CELLS), F32), pltpu.VMEM((CH, 256), F32)],
        smem=(0,),
        flops=10**9,
        name="close",
    )


def weave_kernel(x_ref, out_ref):
    size = 256
    row = lax.broadcasted_iota(jnp.int32, (size, size), 0)
    col = lax.broadcasted_iota(jnp.int32, (size, size), 1)
    place = (col == 2 * (row % 128) + row // 128).astype(BF)
    for r in range(2):
        for t in range(3):
            lane = r * ROW + t * 128
            pair = jnp.concatenate(
                [x_ref[:, lane : lane + 128], x_ref[:, lane + COLS : lane + COLS + 128]], axis=1
            )
            hi, mid, low = split3(pair)
            woven = mm(hi, place) + (mm(mid, place) + mm(low, place))
            out_ref[0, :, r, t * size : (t + 1) * size] = woven


def weave(x):
    return call(weave_kernel, [sds((1, CH, 2, ROW), F32)], [x], name="weave")[0]


PARTS = ((0, IN_HALF), (224, TAP_HALF), (368, TAP_HALF), (512, TAP_HALF), (656, HALF))
FLOW_ROWS = 704
GROUP = 88


def merge_kernel(*refs):
    out_ref, total = refs[-2:]
    for k in range(2):
        own_in, own_out, own_small, got_in, got_out, got_small = refs[6 * k : 6 * k + 6]
        at = k * FLOW_ROWS
        total[at : at + IN_HALF] = own_in[...] + got_in[...]
        for a in range(3):
            start = at + IN_HALF + a * TAP_HALF
            total[start : start + TAP_HALF] = own_out[a] + got_out[a]
        small = own_small[...] + got_small[...]
        start = at + FLOW_ROWS - HALF
        total[start : start + HALF, :256] = small
        total[start : start + HALF, 256:] = small - small.astype(BF).astype(F32)
    for g in range(2 * FLOW_ROWS // GROUP):
        for lane in range(4):
            out_ref[4 * g + lane] = total[
                g * GROUP : (g + 1) * GROUP, lane * 128 : (lane + 1) * 128
            ].astype(BF)


def merge(own0, got0, own1, got1):
    shares = 2 * FLOW_ROWS // GROUP * 4
    return call(
        merge_kernel,
        [sds((shares, GROUP, 128), BF)],
        [*own0, *got0, *own1, *got1],
        scratch=[pltpu.VMEM((2 * FLOW_ROWS, HID), F32)],
        name="merge",
    )[0]


def total_kernel(cells, shares_ref, out_ref):
    total = shares_ref[0].astype(F32)
    for s in range(1, shares_ref.shape[0]):
        total += shares_ref[s].astype(F32)
    mean = (total * (1.0 / cells)).astype(BF)
    for s in range(shares_ref.shape[0]):
        out_ref[s] = mean


def totals(shares, cells):
    return call(
        functools.partial(total_kernel, cells), [sds(shares.shape, BF)], [shares], name="totals"
    )[0]


def unpack_kernel(core_ref, mine_ref, other_ref, win_ref, wout_ref, mix_ref, bin_ref, bout_ref, rows):
    mine_first = core_ref[0] == 0
    for half in range(2):
        for g in range(2 * FLOW_ROWS // GROUP):
            for lane in range(4):
                mine = mine_ref[4 * g + lane].astype(F32)
                other = other_ref[4 * g + lane].astype(F32)
                first, second = (mine, other) if half == 0 else (other, mine)
                rows[half, g * GROUP : (g + 1) * GROUP, lane * 128 : (lane + 1) * 128] = jnp.where(
                    mine_first, first, second
                )
    for k in range(2):
        at = k * FLOW_ROWS
        win_ref[k, :IN_HALF] = rows[0, at : at + IN_HALF]
        win_ref[k, IN_HALF:] = rows[1, at : at + 9 * HALF - IN_HALF]
        bin_ref[k : k + 1, :] = rows[1, at + 9 * HALF - IN_HALF : at + 9 * HALF - IN_HALF + 1]
        for a in range(3):
            start = at + IN_HALF + a * TAP_HALF
            wout_ref[k, 3 * a + 2] = rows[0, start : start + CH]
            wout_ref[k, 3 * a + 1, :HALF] = rows[0, start + CH : start + TAP_HALF]
            wout_ref[k, 3 * a + 1, HALF:] = rows[1, start : start + HALF]
            wout_ref[k, 3 * a] = rows[1, start + HALF : start + TAP_HALF]
        start = at + FLOW_ROWS - HALF
        for half in range(2):
            block = rows[half, start : start + HALF]
            mix_ref[k, half * HALF : (half + 1) * HALF] = block[:, :CH] + block[:, 256 : 256 + CH]
        block = rows[0, start : start + 8]
        bout_ref[k] = block[:, 128 : 128 + CH] + block[:, 384 : 384 + CH]


def unpack(core, mine, other):
    return call(
        unpack_kernel,
        [
            sds((2, 9 * HALF, HID), F32),
            sds((2, 9, CH, HID), F32),
            sds((2, CH, CH), F32),
            sds((2, HID), F32),
            sds((2, 8, CH), F32),
        ],
        [core, mine, other],
        scratch=[pltpu.VMEM((2, 2 * FLOW_ROWS, HID), F32)],
        smem=(0,),
        name="unpack",
    )


def after(x, *others):
    return lax.optimization_barrier((x, *others))[0]


def local(passed_on, passed_grad, latent, mix_factors, in_kernel, in_bias, out_kernel, out_bias):
    lat_index = lax.axis_index(LAT)
    lat_count = lax.axis_size(LAT)
    forth = [(i, (i + 1) % lat_count) for i in range(lat_count)]
    back = [(t, s) for s, t in forth]
    swap = [(0, 1), (1, 0)]
    flags = jnp.stack([lat_index > 0, lat_index < lat_count - 1]).astype(F32)
    core = lax.axis_index("c").astype(jnp.int32).reshape(1)

    block = payload(
        jnp.transpose(passed_on[0], (1, 2, 0)), jnp.transpose(passed_grad[0], (1, 2, 0))
    )
    recv = lax.all_to_all(block, LAT, 0, 0, tiled=True)
    inv, lut, w1t, w2t, w2k, w1k, b2c = prep(mix_factors, in_kernel, out_kernel, in_bias, out_bias)
    w1 = in_kernel.reshape(2, 9 * HALF, HID)
    yb = latent.reshape(HALF, CELLS)

    above, mid, below, ya, ga = turn(recv)
    x1, rows1, slope1, next_mid, grad1, moved1 = forward(
        flags, above, mid, below, w1t[1], w2k[1], b2c[1], inv[1], ya, yb, True
    )
    above0 = lax.ppermute(next_mid, LAT, forth)
    below0 = lax.ppermute(next_mid, LAT, back)
    top1 = lax.ppermute(grad1, LAT, forth)
    bottom1 = lax.ppermute(grad1, LAT, back)
    keep_out1, give_out1, bias1 = out_weight(core, grad1, rows1)
    x0, rows0, slope0, scale0 = forward(
        after(flags, keep_out1), above0, next_mid, below0, w1t[0], w2k[0], b2c[0], inv[0],
        x1[:HALF], x1[HALF:], False,
    )
    got_out1 = lax.ppermute(give_out1, "c", swap)
    gpre1, in1 = backward(after(flags, x0), top1, grad1, bottom1, w2t[1], slope1, w1k[1])
    gx1, keep_small1, give_small1, grad0, moved0 = close(
        core, in1, ga, moved1, lut[1], x1, mix_factors, 1, bias1, scale0
    )
    top0 = lax.ppermute(grad0, LAT, forth)
    bottom0 = lax.ppermute(grad0, LAT, back)
    got_small1 = lax.ppermute(give_small1, "c", swap)
    keep_in1, give_in1 = in_weight(after(core, grad0), flags, above, mid, below, gpre1)
    got_in1 = lax.ppermute(give_in1, "c", swap)
    keep_out0, give_out0, bias0 = out_weight(after(core, keep_in1), grad0, rows0)
    rebuilt = weave(after(x0, keep_out0))
    gpre0, in0 = backward(after(flags, rebuilt), top0, grad0, bottom0, w2t[0], slope0, w1k[0])
    got_out0 = lax.ppermute(give_out0, "c", swap)
    keep_in0, give_in0 = in_weight(after(core, in0), flags, above0, next_mid, below0, gpre0)
    got_in0 = lax.ppermute(give_in0, "c", swap)
    gx0, keep_small0, give_small0 = close(
        after(core, keep_in0), in0, gx1, moved0, lut[0], x0, mix_factors, 0, bias0
    )
    got_small0 = lax.ppermute(give_small0, "c", swap)

    packed = merge(
        (keep_in0, keep_out0, keep_small0),
        (got_in0, got_out0, got_small0),
        (keep_in1, keep_out1, keep_small1),
        (got_in1, got_out1, got_small1),
    )
    shares = lax.all_to_all(packed, CHIPS, 0, 0, tiled=True)
    input_grad = weave(after(gx0, packed))
    cells = float(CELLS * lat_count * lax.axis_size(ENS))
    spread = totals(after(shares, input_grad), cells)
    mine = lax.all_to_all(spread, CHIPS, 0, 0, tiled=True)
    other = lax.ppermute(mine, "c", swap)
    in_grad, out_grad, mix_grad, in_bias_grad, out_bias_grad = unpack(core, mine, other)
    return (
        rebuilt,
        input_grad,
        mix_grad,
        in_grad.reshape(2, 9, HALF, HID),
        in_bias_grad,
        out_grad,
        out_bias_grad[:, 0],
    )


def solution(mesh):
    split = Mesh(mesh.devices.reshape(4, 2, 2, 4, 2), ("y", "xl", "c", "z", "xh"))
    return jax.shard_map(
        local,
        mesh=split,
        in_specs=(
            P(ENS, None, None, LAT),
            P(ENS, None, None, LAT),
            P(ENS, None, LAT, None),
            P(),
            P(),
            P(),
            P(),
            P(),
        ),
        out_specs=(P(ENS, None, LAT, None), P(ENS, None, LAT, None), P(), P(), P(), P(), P()),
        check_vma=False,
    )
```

```python
import functools

import jax
import jax.numpy as jnp
from jax import lax
from jax.experimental import pallas as pl
from jax.experimental.pallas import tpu as pltpu
from jax.sharding import Mesh, PartitionSpec as P

BF = jnp.bfloat16
F32 = jnp.float32
HIGH = lax.Precision.HIGHEST
LAT = ("y", "xl", "c")
ENS = ("z", "xh")
CHIPS = ("y", "xl", "z", "xh")
HALF = 48
CH = 96
HID = 512
COLS = 384
ROW = 768
CELLS = 1536
IN_ROWS = 448
IN_HALF = 224
TAP_HALF = 144
MIB = 1024 * 1024


def mm(a, b):
    return lax.dot_general(a, b, (((1,), (0,)), ((), ())), preferred_element_type=F32)


def mm_nt(a, b):
    return lax.dot_general(a, b, (((1,), (1,)), ((), ())), preferred_element_type=F32)


def mm_high(a, b):
    return lax.dot_general(
        a, b, (((1,), (0,)), ((), ())), preferred_element_type=F32, precision=HIGH
    )


def split3(x):
    hi = x.astype(BF)
    rest = x - hi.astype(F32)
    mid = rest.astype(BF)
    low = (rest - mid.astype(F32)).astype(BF)
    return hi, mid, low


def from_left(x):
    lane = lax.broadcasted_iota(jnp.int32, x.shape, 1)
    return jnp.where(lane == 0, 0.0, pltpu.roll(x, 1, 1))


def from_right(x):
    width = x.shape[1]
    lane = lax.broadcasted_iota(jnp.int32, x.shape, 1)
    return jnp.where(lane == width - 1, 0.0, pltpu.roll(x, width - 1, 1))


def sds(shape, dtype):
    return jax.ShapeDtypeStruct(shape, dtype)


def call(body, outs, ins, scratch=(), smem=(), hbm=(), flops=0, name=None, limit=16):
    moved = sum(x.size * x.dtype.itemsize for x in list(ins) + list(outs))
    return pl.pallas_call(
        body,
        out_shape=outs,
        in_specs=[
            pl.BlockSpec(
                memory_space=pltpu.SMEM if i in smem else pltpu.HBM if i in hbm else pltpu.VMEM
            )
            for i in range(len(ins))
        ],
        out_specs=[pl.BlockSpec(memory_space=pltpu.VMEM) for _ in outs],
        scratch_shapes=list(scratch),
        compiler_params=pltpu.CompilerParams(vmem_limit_bytes=limit * MIB),
        cost_estimate=pl.CostEstimate(flops=flops, bytes_accessed=moved, transcendentals=0),
        name=name,
    )(*ins)


def payload_kernel(on_ref, grad_ref, out_ref):
    bands, width = on_ref.shape[2], 2 * CH
    blank = jnp.zeros(on_ref.shape[1:], BF)
    for s in range(on_ref.shape[0]):
        on = on_ref[s]
        hi = on.astype(BF)
        grad = grad_ref[s]
        ghi = grad.astype(BF)
        out_ref[s, :, :width] = hi
        out_ref[s, :, width : 2 * width] = (on - hi.astype(F32)).astype(BF)
        if s + 1 < on_ref.shape[0]:
            out_ref[s + 1, :, 2 * width : 3 * width] = hi
        if s > 0:
            out_ref[s - 1, :, 3 * width : 4 * width] = hi
        out_ref[s, :, 4 * width : 5 * width] = ghi
        out_ref[s, :, 5 * width : 6 * width] = (grad - ghi.astype(F32)).astype(BF)
    out_ref[0, :, 2 * width : 3 * width] = blank
    out_ref[on_ref.shape[0] - 1, :, 3 * width : 4 * width] = blank


def payload(on, grad):
    bands, width, channels = on.shape
    return call(
        payload_kernel, [sds((bands, width, 6 * channels), BF)], [on, grad], name="payload", limit=56
    )[0]


def prep_kernel(
    mix_ref, w1_ref, w2_ref, b1_ref, b2_ref, *refs
):
    stage1, stage2 = refs[-2:]
    flows = mix_ref.shape[0]
    row = lax.broadcasted_iota(jnp.int32, (CH, CH), 0)
    col = lax.broadcasted_iota(jnp.int32, (CH, CH), 1)
    eye = (row == col).astype(F32)
    near = (row // 16) == (col // 16)
    units = []
    for k in range(flows):
        mix = mix_ref[k]
        units.append(jnp.where(row > col, mix, 0.0))
        units.append(jnp.where(row < col, mix, 0.0))
    inner = [jnp.where(near, u, 0.0) for u in units]
    outer = [u - i for u, i in zip(units, inner)]
    power = inner
    blocks = [eye - n for n in inner]
    for _ in range(3):
        power = [mm_high(p, p) for p in power]
        blocks = [mm_high(b, eye + p) for b, p in zip(blocks, power)]
    power = [mm_high(b, o) for b, o in zip(blocks, outer)]
    whole = [eye - p for p in power]
    for _ in range(2):
        power = [mm_high(p, p) for p in power]
        whole = [mm_high(w, eye + p) for w, p in zip(whole, power)]
    inverses = [mm_high(w, b) for w, b in zip(whole, blocks)]
    for k in range(flows):
        inv_ref, lut_ref, w1t_ref, w2t_ref, w2k_ref, w1k_ref, b2c_ref = refs[7 * k : 7 * k + 7]
        inv_ref[...] = mm_high(inverses[2 * k + 1], inverses[2 * k])
        lut_ref[...] = mm_high(units[2 * k] + eye, units[2 * k + 1] + eye).T
        for tap in range(9):
            stage1[tap * HALF : (tap + 1) * HALF, :] = 0.5 * w1_ref[k, tap].astype(F32)
            stage2[tap * CH : (tap + 1) * CH, :] = 0.5 * w2_ref[k, 8 - tap].astype(F32)
        hi, mid, low = split3(0.5 * b1_ref[k : k + 1, :])
        stage1[9 * HALF :, :] = jnp.zeros((IN_ROWS - 9 * HALF, HID), F32)
        for i, part in enumerate((hi, mid, low)):
            stage1[9 * HALF + i : 9 * HALF + i + 1, :] = part.astype(F32)
        w1t_ref[...] = stage1[...].T.astype(BF)
        w2t_ref[...] = stage2[...].T.astype(BF)
        for a in range(3):
            for b in range(3):
                w2k_ref[b * CH : (b + 1) * CH, a * HID : (a + 1) * HID] = w2_ref[k, 3 * a + b]
                w1k_ref[b * HALF : (b + 1) * HALF, a * HID : (a + 1) * HID] = w1_ref[
                    k, 3 * (2 - a) + b
                ]
        b2c_ref[...] = jnp.broadcast_to(b2_ref[k : k + 1, :], (8, CH)).T


def prep(mix_factors, in_kernel, out_kernel, in_bias, out_bias):
    flows = mix_factors.shape[0]
    outs = call(
        prep_kernel,
        [
            sds((CH, CH), F32),
            sds((CH, CH), F32),
            sds((HID, IN_ROWS), BF),
            sds((HID, 9 * CH), BF),
            sds((3 * CH, 3 * HID), BF),
            sds((3 * HALF, 3 * HID), BF),
            sds((CH, 8), F32),
        ]
        * flows,
        [mix_factors, in_kernel, out_kernel, in_bias, out_bias],
        scratch=[pltpu.VMEM((IN_ROWS, HID), F32), pltpu.VMEM((9 * CH, HID), F32)],
        name="prep",
        limit=56,
    )
    return [outs[i::7] for i in range(7)]


def turn_kernel(recv_ref, above_ref, mid_ref, below_ref, ya_ref, ga_ref, stage):
    width = 2 * CH
    row = lax.broadcasted_iota(jnp.int32, (width, width), 0)
    col = lax.broadcasted_iota(jnp.int32, (width, width), 1)
    pick = (col == 4 * (row % HALF) + row // HALF).astype(BF)
    none = jnp.zeros((width, width), BF)
    first = jnp.concatenate([pick, none], axis=1)
    second = jnp.concatenate([none, pick], axis=1)
    both = jnp.concatenate([pick, pick], axis=1)
    sources, count = recv_ref.shape[0], recv_ref.shape[1]
    for s in range(sources):
        stage[s * count : (s + 1) * count, :] = recv_ref[s].astype(F32)
    pair = stage[:, : 2 * width].astype(BF)
    kept = mm_nt(both, pair)
    mid_ref[...] = mm_nt(first, pair).astype(BF)
    pair = stage[:, 2 * width : 4 * width].astype(BF)
    above_ref[...] = mm_nt(first, pair).astype(BF)
    below_ref[...] = mm_nt(second, pair).astype(BF)
    grad = mm_nt(both, stage[:, 4 * width :].astype(BF))
    for k in range(4):
        ya_ref[:, k * COLS : (k + 1) * COLS] = kept[k * HALF : (k + 1) * HALF]
        ga_ref[:, k * COLS : (k + 1) * COLS] = grad[k * HALF : (k + 1) * HALF]


def turn(recv):
    return call(
        turn_kernel,
        [sds((2 * CH, COLS), BF)] * 3 + [sds((HALF, CELLS), F32)] * 2,
        [recv],
        scratch=[pltpu.VMEM((COLS, recv.shape[2]), F32)],
        flops=4 * 10**9,
        name="turn",
    )


def stack_planes(even, odd, factor=None):
    if factor is not None:
        even = (even.astype(F32) * factor).astype(BF)
        odd = (odd.astype(F32) * factor).astype(BF)
    left = from_left(odd.astype(F32)).astype(BF)
    right = from_right(even.astype(F32)).astype(BF)
    return jnp.concatenate([left, even, odd, right], axis=0)


def fill_input_columns(flags_ref, above_ref, mid_ref, below_ref, columns, first, count):
    refs = {-2: (above_ref, 0), -1: (above_ref, CH), 0: (mid_ref, 0)}
    refs.update({1: (mid_ref, CH), 2: (below_ref, 0), 3: (below_ref, CH)})
    for source in range(first - 1, first + count + 1):
        ref, at = refs[source]
        factor = flags_ref[0] if source < 0 else flags_ref[1] if source > 1 else None
        stacked = stack_planes(ref[at : at + HALF], ref[at + HALF : at + CH], factor)
        for a in range(3):
            target = source - a + 1 - first
            if 0 <= target < count:
                for p in range(2):
                    lane = (2 * target + p) * COLS
                    columns[a * 144 : (a + 1) * 144, lane : lane + COLS] = stacked[
                        p * HALF : p * HALF + 144
                    ]
    extra = IN_ROWS - 9 * HALF
    row = lax.broadcasted_iota(jnp.int32, (extra, count * ROW), 0)
    columns[9 * HALF :, :] = jnp.where(row < 3, 1.0, 0.0).astype(BF)


def fill_grad_columns(flags_ref, above_ref, mid_ref, below_ref, columns):
    for source in range(-2, 4):
        ref = above_ref if source < 0 else below_ref if source > 1 else mid_ref
        factor = flags_ref[0] if source < 0 else flags_ref[1] if source > 1 else None
        at = (source % 2) * 2 * CH
        stacked = stack_planes(ref[at : at + CH], ref[at + CH : at + 2 * CH], factor)
        for a in range(3):
            target = source - a + 2
            if 0 <= target < 4:
                for p in range(2):
                    lane = (2 * target + p) * COLS
                    columns[a * 288 : (a + 1) * 288, lane : lane + COLS] = stacked[
                        p * CH : p * CH + 288
                    ]


def put_out_grad(raw, moved, out_ref):
    for r in range(2):
        for p in range(2):
            lane = (2 * r + p) * COLS
            at = (2 * r + p) * CH
            out_ref[at : at + HALF] = raw[:, lane : lane + COLS].astype(BF)
            out_ref[at + HALF : at + CH] = moved[:, lane : lane + COLS].astype(BF)


def forward_kernel(with_grad, flags_ref, *refs):
    above_ref, mid_ref, below_ref, *weights, ya_ref, yb_ref = refs[:9]
    columns, pre, outs, *held, sems = refs[-8:]
    w1t_ref, w2k_ref, b2_ref, inv_ref = held
    copies = [
        pltpu.make_async_copy(source, target, sems.at[i])
        for i, (source, target) in enumerate(zip(weights, held))
    ]
    for copy in copies:
        copy.start()
    if with_grad:
        x_ref, rows, slope_ref, next_ref, grad_ref, moved_ref = refs[9:-8]
    else:
        x_ref, rows, slope_ref, scale_ref = refs[9:-8]
    fill_input_columns(flags_ref, above_ref, mid_ref, below_ref, columns, -1, 4)
    for copy in copies:
        copy.wait()
    for h in range(4):
        pre[h % 2] = mm(w1t_ref[...], columns[:, h * ROW : (h + 1) * ROW])
        inside = flags_ref[0] if h == 0 else flags_ref[1] if h == 3 else None

        def activate(step, carry):
            at = pl.multiple_of(step * 16, 16)
            half = pre[h % 2, pl.ds(at, 16), :]
            bent = jnp.tanh(half)
            more = 1.0 + bent
            hidden = half * more
            slope = more * (1.0 + half * (1.0 - bent))
            if inside is not None:
                hidden = hidden * inside
                slope = slope * inside
            rows[pl.ds(h * HID + at, 16), :] = hidden.astype(BF)
            slope_ref[pl.ds(h * HID + at, 16), :] = slope
            return carry

        lax.fori_loop(0, HID // 16, activate, 0, unroll=True)
    for r in range(2):
        taps = mm(w2k_ref[...], rows[r * HID : (r + 3) * HID, :])
        even, odd = taps[:, :COLS], taps[:, COLS:]
        lane = 2 * r * COLS
        outs[:, lane : lane + COLS] = from_left(odd[:CH]) + even[CH : 2 * CH] + odd[2 * CH :]
        outs[:, lane + COLS : lane + ROW] = even[:CH] + odd[CH : 2 * CH] + from_right(even[2 * CH :])
    raw = outs[:HALF] + b2_ref[:HALF, :1]
    shift = outs[HALF:] + b2_ref[HALF:, :1]
    inverse = 1.0 + jnp.exp(-(raw + 2.0))
    scale = 1.0 / inverse
    moved_in = yb_ref[...] * inverse - shift
    x = mm_high(inv_ref[...], jnp.concatenate([ya_ref[...], moved_in], axis=0))
    x_ref[...] = x
    if with_grad:
        moved_grad = yb_ref[...]
        moved = moved_grad * scale
        moved_ref[...] = moved
        put_out_grad((moved_grad * yb_ref[...] - 1.0) * (1.0 - scale), moved, grad_ref)
        for k in range(4):
            next_ref[k * HALF : (k + 1) * HALF] = x[:HALF, k * COLS : (k + 1) * COLS].astype(BF)
    else:
        scale_ref[...] = scale


def forward(flags, above, mid, below, w1t, w2k, b2c, inv, ya, yb, with_grad):
    outs = [sds((CH, CELLS), F32), sds((4 * HID, ROW), BF), sds((4 * HID, ROW), F32)]
    if with_grad:
        outs += [
            sds((2 * CH, COLS), BF),
            sds((4 * CH, COLS), BF),
            sds((HALF, CELLS), F32),
        ]
    else:
        outs += [sds((HALF, CELLS), F32)]
    return call(
        functools.partial(forward_kernel, with_grad),
        outs,
        [flags, above, mid, below, w1t, w2k, b2c, inv, ya, yb],
        scratch=[
            pltpu.VMEM((IN_ROWS, 4 * ROW), BF),
            pltpu.VMEM((2, HID, ROW), F32),
            pltpu.VMEM((CH, CELLS), F32),
            pltpu.VMEM((HID, IN_ROWS), BF),
            pltpu.VMEM((3 * CH, 3 * HID), BF),
            pltpu.VMEM((CH, 8), F32),
            pltpu.VMEM((CH, CH), F32),
            pltpu.SemaphoreType.DMA((4,)),
        ],
        smem=(0,),
        hbm=(4, 5, 6, 7),
        limit=24,
        flops=4 * 10**9,
        name="forward",
    )


def backward_kernel(
    flags_ref, above_ref, mid_ref, below_ref, w2t_ref, slope_ref, w1k_ref, gpre_ref, in_ref,
    columns, hid_grad,
):
    fill_grad_columns(flags_ref, above_ref, mid_ref, below_ref, columns)
    for h in range(4):
        hid_grad[h % 2] = mm(w2t_ref[...], columns[:, h * ROW : (h + 1) * ROW])

        def slope(step, carry):
            at = pl.multiple_of(step * 16, 16)
            gpre_ref[pl.ds(h * HID + at, 16), :] = (
                hid_grad[h % 2, pl.ds(at, 16), :] * slope_ref[pl.ds(h * HID + at, 16), :]
            ).astype(BF)
            return carry

        lax.fori_loop(0, HID // 16, slope, 0, unroll=True)
    b0, b1, b2 = slice(0, HALF), slice(HALF, CH), slice(CH, 3 * HALF)
    for r in range(2):
        taps = mm(w1k_ref[...], gpre_ref[r * HID : (r + 3) * HID, :])
        even, odd = taps[:, :COLS], taps[:, COLS:]
        in_ref[r * CH : r * CH + HALF] = odd[b0] + even[b1] + from_left(odd[b2])
        in_ref[r * CH + HALF : (r + 1) * CH] = from_right(even[b0]) + odd[b1] + even[b2]


def backward(flags, above, mid, below, w2t, slope, w1k):
    return call(
        backward_kernel,
        [sds((4 * HID, ROW), BF), sds((2 * CH, COLS), F32)],
        [flags, above, mid, below, w2t, slope, w1k],
        scratch=[pltpu.VMEM((9 * CH, 4 * ROW), BF), pltpu.VMEM((2, HID, ROW), F32)],
        smem=(0,),
        flops=6 * 10**9,
        limit=20,
        name="backward",
    )


def out_weight_kernel(core_ref, grad_ref, rows_ref, keep_ref, give_ref, bias_ref, left, right, whole):
    for r in range(2):
        at = 2 * r * CH
        stacked = stack_planes(grad_ref[at : at + CH], grad_ref[at + CH : at + 2 * CH])
        left[r] = stacked[: 3 * CH]
        right[r] = stacked[CH:]
    part = [jnp.concatenate([left[r], right[r]], axis=1) for r in range(2)]
    for a in range(3):
        whole[...] = mm_nt(part[0], rows_ref[a * HID : (a + 1) * HID]) + mm_nt(
            part[1], rows_ref[(a + 1) * HID : (a + 2) * HID]
        )
        for ref, core in ((keep_ref, core_ref[0]), (give_ref, 1 - core_ref[0])):
            ref[a] = whole[pl.ds(pl.multiple_of(core * TAP_HALF, 8), TAP_HALF), :]
    ones = jnp.ones((8, COLS), BF)
    total = mm_nt(ones, grad_ref[:CH]) + mm_nt(ones, grad_ref[CH : 2 * CH])
    bias_ref[...] = total + (
        mm_nt(ones, grad_ref[2 * CH : 3 * CH]) + mm_nt(ones, grad_ref[3 * CH :])
    )


def out_weight(core, grad, rows):
    return call(
        out_weight_kernel,
        [sds((3, TAP_HALF, HID), F32), sds((3, TAP_HALF, HID), F32), sds((8, CH), F32)],
        [core, grad, rows],
        scratch=[
            pltpu.VMEM((2, 3 * CH, COLS), BF),
            pltpu.VMEM((2, 3 * CH, COLS), BF),
            pltpu.VMEM((3 * CH, HID), F32),
        ],
        smem=(0,),
        flops=2 * 10**9,
        name="out_weight",
    )


def in_weight_kernel(
    core_ref, flags_ref, above_ref, mid_ref, below_ref, gpre_ref, keep_ref, give_ref, columns,
    whole,
):
    fill_input_columns(flags_ref, above_ref, mid_ref, below_ref, columns, 0, 2)
    whole[...] = mm_nt(columns[:, :ROW], gpre_ref[HID : 2 * HID]) + mm_nt(
        columns[:, ROW:], gpre_ref[2 * HID : 3 * HID]
    )
    for ref, core in ((keep_ref, core_ref[0]), (give_ref, 1 - core_ref[0])):
        ref[...] = whole[pl.ds(pl.multiple_of(core * IN_HALF, 8), IN_HALF), :]


def in_weight(core, flags, above, mid, below, gpre):
    return call(
        in_weight_kernel,
        [sds((IN_HALF, HID), F32), sds((IN_HALF, HID), F32)],
        [core, flags, above, mid, below, gpre],
        scratch=[pltpu.VMEM((IN_ROWS, CELLS), BF), pltpu.VMEM((IN_ROWS, HID), F32)],
        smem=(0, 1),
        flops=10**9,
        name="in_weight",
    )


def close_kernel(next_step, flow, core_ref, *refs):
    in_ref, ga_ref, moved_ref, lut_ref, x_ref, mix_ref, bias_ref = refs[:7]
    whole, small = refs[-2:]
    if next_step:
        scale_ref, gx_ref, keep_ref, give_ref, grad_ref, nmoved_ref = refs[7:-2]
    else:
        gx_ref, keep_ref, give_ref = refs[7:-2]
    for k in range(4):
        lane = k * COLS
        whole[:HALF, lane : lane + COLS] = (
            ga_ref[:HALF, lane : lane + COLS] + in_ref[k * HALF : (k + 1) * HALF]
        )
    whole[HALF:] = moved_ref[...]
    gx = mm_high(lut_ref[...], whole[...])
    gx_ref[...] = gx
    if next_step:
        scale = scale_ref[...]
        moved_grad = gx[HALF:]
        moved = moved_grad * scale
        nmoved_ref[...] = moved
        put_out_grad((moved_grad * x_ref[HALF:] - 1.0) * (1.0 - scale), moved, grad_ref)
    ghi, gmid, _ = split3(whole[...])
    xhi, xmid, _ = split3(x_ref[...])
    outer = mm_nt(ghi, xhi) + (mm_nt(ghi, xmid) + mm_nt(gmid, xhi))
    row = lax.broadcasted_iota(jnp.int32, (CH, CH), 0)
    col = lax.broadcasted_iota(jnp.int32, (CH, CH), 1)
    eye = (row == col).astype(F32)
    mix = mix_ref[flow]
    lower = jnp.where(row > col, mix, 0.0) + eye
    upper = jnp.where(row < col, mix, 0.0) + eye
    by_upper = mm_high(outer, upper.T)
    by_lower = mm_high(lower.T, outer)
    small[:, :CH] = jnp.where(row > col, by_upper, jnp.where(row < col, by_lower, 0.0))
    small[:, CH:] = jnp.zeros((CH, 2 * 128 - CH), F32)
    small[:8, 128 : 128 + CH] = bias_ref[...]
    for ref, core in ((keep_ref, core_ref[0]), (give_ref, 1 - core_ref[0])):
        ref[...] = small[pl.ds(pl.multiple_of(core * HALF, 8), HALF), :]


def close(core, gin, ga, moved, lut, x, mix, flow, bias, scale=None):
    outs = [sds((CH, CELLS), F32), sds((HALF, 256), F32), sds((HALF, 256), F32)]
    ins = [core, gin, ga, moved, lut, x, mix, bias]
    if scale is not None:
        outs += [sds((4 * CH, COLS), BF), sds((HALF, CELLS), F32)]
        ins += [scale]
    return call(
        functools.partial(close_kernel, scale is not None, flow),
        outs,
        ins,
        scratch=[pltpu.VMEM((CH, CELLS), F32), pltpu.VMEM((CH, 256), F32)],
        smem=(0,),
        flops=10**9,
        name="close",
    )


def weave_kernel(x_ref, out_ref):
    size = 256
    row = lax.broadcasted_iota(jnp.int32, (size, size), 0)
    col = lax.broadcasted_iota(jnp.int32, (size, size), 1)
    place = (col == 2 * (row % 128) + row // 128).astype(BF)
    for r in range(2):
        for t in range(3):
            lane = r * ROW + t * 128
            pair = jnp.concatenate(
                [x_ref[:, lane : lane + 128], x_ref[:, lane + COLS : lane + COLS + 128]], axis=1
            )
            hi, mid, low = split3(pair)
            woven = mm(hi, place) + (mm(mid, place) + mm(low, place))
            out_ref[0, :, r, t * size : (t + 1) * size] = woven


def weave(x):
    return call(weave_kernel, [sds((1, CH, 2, ROW), F32)], [x], name="weave")[0]


PARTS = ((0, IN_HALF), (224, TAP_HALF), (368, TAP_HALF), (512, TAP_HALF), (656, HALF))
FLOW_ROWS = 704
GROUP = 88


def merge_kernel(*refs):
    out_ref, total = refs[-2:]
    for k in range(2):
        own_in, own_out, own_small, got_in, got_out, got_small = refs[6 * k : 6 * k + 6]
        at = k * FLOW_ROWS
        total[at : at + IN_HALF] = own_in[...] + got_in[...]
        for a in range(3):
            start = at + IN_HALF + a * TAP_HALF
            total[start : start + TAP_HALF] = own_out[a] + got_out[a]
        small = own_small[...] + got_small[...]
        start = at + FLOW_ROWS - HALF
        total[start : start + HALF, :256] = small
        total[start : start + HALF, 256:] = small - small.astype(BF).astype(F32)
    for g in range(2 * FLOW_ROWS // GROUP):
        for lane in range(4):
            out_ref[4 * g + lane] = total[
                g * GROUP : (g + 1) * GROUP, lane * 128 : (lane + 1) * 128
            ].astype(BF)


def merge(own0, got0, own1, got1):
    shares = 2 * FLOW_ROWS // GROUP * 4
    return call(
        merge_kernel,
        [sds((shares, GROUP, 128), BF)],
        [*own0, *got0, *own1, *got1],
        scratch=[pltpu.VMEM((2 * FLOW_ROWS, HID), F32)],
        name="merge",
    )[0]


def total_kernel(cells, shares_ref, out_ref):
    total = shares_ref[0].astype(F32)
    for s in range(1, shares_ref.shape[0]):
        total += shares_ref[s].astype(F32)
    mean = (total * (1.0 / cells)).astype(BF)
    for s in range(shares_ref.shape[0]):
        out_ref[s] = mean


def totals(shares, cells):
    return call(
        functools.partial(total_kernel, cells), [sds(shares.shape, BF)], [shares], name="totals"
    )[0]


def unpack_kernel(core_ref, mine_ref, other_ref, win_ref, wout_ref, mix_ref, bin_ref, bout_ref, rows):
    mine_first = core_ref[0] == 0
    for half in range(2):
        for g in range(2 * FLOW_ROWS // GROUP):
            for lane in range(4):
                mine = mine_ref[4 * g + lane].astype(F32)
                other = other_ref[4 * g + lane].astype(F32)
                first, second = (mine, other) if half == 0 else (other, mine)
                rows[half, g * GROUP : (g + 1) * GROUP, lane * 128 : (lane + 1) * 128] = jnp.where(
                    mine_first, first, second
                )
    for k in range(2):
        at = k * FLOW_ROWS
        win_ref[k, :IN_HALF] = rows[0, at : at + IN_HALF]
        win_ref[k, IN_HALF:] = rows[1, at : at + 9 * HALF - IN_HALF]
        bin_ref[k : k + 1, :] = rows[1, at + 9 * HALF - IN_HALF : at + 9 * HALF - IN_HALF + 1]
        for a in range(3):
            start = at + IN_HALF + a * TAP_HALF
            wout_ref[k, 3 * a + 2] = rows[0, start : start + CH]
            wout_ref[k, 3 * a + 1, :HALF] = rows[0, start + CH : start + TAP_HALF]
            wout_ref[k, 3 * a + 1, HALF:] = rows[1, start : start + HALF]
            wout_ref[k, 3 * a] = rows[1, start + HALF : start + TAP_HALF]
        start = at + FLOW_ROWS - HALF
        for half in range(2):
            block = rows[half, start : start + HALF]
            mix_ref[k, half * HALF : (half + 1) * HALF] = block[:, :CH] + block[:, 256 : 256 + CH]
        block = rows[0, start : start + 8]
        bout_ref[k] = block[:, 128 : 128 + CH] + block[:, 384 : 384 + CH]


def unpack(core, mine, other):
    return call(
        unpack_kernel,
        [
            sds((2, 9 * HALF, HID), F32),
            sds((2, 9, CH, HID), F32),
            sds((2, CH, CH), F32),
            sds((2, HID), F32),
            sds((2, 8, CH), F32),
        ],
        [core, mine, other],
        scratch=[pltpu.VMEM((2, 2 * FLOW_ROWS, HID), F32)],
        smem=(0,),
        name="unpack",
    )


def after(x, *others):
    return lax.optimization_barrier((x, *others))[0]


def local(passed_on, passed_grad, latent, mix_factors, in_kernel, in_bias, out_kernel, out_bias):
    lat_index = lax.axis_index(LAT)
    lat_count = lax.axis_size(LAT)
    forth = [(i, (i + 1) % lat_count) for i in range(lat_count)]
    back = [(t, s) for s, t in forth]
    swap = [(0, 1), (1, 0)]
    flags = jnp.stack([lat_index > 0, lat_index < lat_count - 1]).astype(F32)
    core = lax.axis_index("c").astype(jnp.int32).reshape(1)

    block = payload(
        jnp.transpose(passed_on[0], (1, 2, 0)), jnp.transpose(passed_grad[0], (1, 2, 0))
    )
    recv = lax.all_to_all(block, LAT, 0, 0, tiled=True)
    inv, lut, w1t, w2t, w2k, w1k, b2c = prep(mix_factors, in_kernel, out_kernel, in_bias, out_bias)
    w1 = in_kernel.reshape(2, 9 * HALF, HID)
    yb = latent.reshape(HALF, CELLS)

    above, mid, below, ya, ga = turn(recv)
    x1, rows1, slope1, next_mid, grad1, moved1 = forward(
        flags, above, mid, below, w1t[1], w2k[1], b2c[1], inv[1], ya, yb, True
    )
    above0 = lax.ppermute(next_mid, LAT, forth)
    below0 = lax.ppermute(next_mid, LAT, back)
    top1 = lax.ppermute(grad1, LAT, forth)
    bottom1 = lax.ppermute(grad1, LAT, back)
    keep_out1, give_out1, bias1 = out_weight(core, grad1, rows1)
    x0, rows0, slope0, scale0 = forward(
        after(flags, keep_out1), above0, next_mid, below0, w1t[0], w2k[0], b2c[0], inv[0],
        x1[:HALF], x1[HALF:], False,
    )
    got_out1 = lax.ppermute(give_out1, "c", swap)
    gpre1, in1 = backward(after(flags, x0), top1, grad1, bottom1, w2t[1], slope1, w1k[1])
    gx1, keep_small1, give_small1, grad0, moved0 = close(
        core, in1, ga, moved1, lut[1], x1, mix_factors, 1, bias1, scale0
    )
    top0 = lax.ppermute(grad0, LAT, forth)
    bottom0 = lax.ppermute(grad0, LAT, back)
    got_small1 = lax.ppermute(give_small1, "c", swap)
    keep_in1, give_in1 = in_weight(after(core, grad0), flags, above, mid, below, gpre1)
    got_in1 = lax.ppermute(give_in1, "c", swap)
    keep_out0, give_out0, bias0 = out_weight(after(core, keep_in1), grad0, rows0)
    rebuilt = weave(after(x0, keep_out0))
    gpre0, in0 = backward(after(flags, rebuilt), top0, grad0, bottom0, w2t[0], slope0, w1k[0])
    got_out0 = lax.ppermute(give_out0, "c", swap)
    keep_in0, give_in0 = in_weight(after(core, in0), flags, above0, next_mid, below0, gpre0)
    got_in0 = lax.ppermute(give_in0, "c", swap)
    gx0, keep_small0, give_small0 = close(
        after(core, keep_in0), in0, gx1, moved0, lut[0], x0, mix_factors, 0, bias0
    )
    got_small0 = lax.ppermute(give_small0, "c", swap)

    packed = merge(
        (keep_in0, keep_out0, keep_small0),
        (got_in0, got_out0, got_small0),
        (keep_in1, keep_out1, keep_small1),
        (got_in1, got_out1, got_small1),
    )
    shares = lax.all_to_all(packed, CHIPS, 0, 0, tiled=True)
    input_grad = weave(after(gx0, packed))
    cells = float(CELLS * lat_count * lax.axis_size(ENS))
    spread = totals(after(shares, input_grad), cells)
    mine = lax.all_to_all(spread, CHIPS, 0, 0, tiled=True)
    other = lax.ppermute(mine, "c", swap)
    in_grad, out_grad, mix_grad, in_bias_grad, out_bias_grad = unpack(core, mine, other)
    return (
        rebuilt,
        input_grad,
        mix_grad,
        in_grad.reshape(2, 9, HALF, HID),
        in_bias_grad,
        out_grad,
        out_bias_grad[:, 0],
    )


def solution(mesh):
    split = Mesh(mesh.devices.reshape(4, 2, 2, 4, 2), ("y", "xl", "c", "z", "xh"))
    return jax.shard_map(
        local,
        mesh=split,
        in_specs=(
            P(ENS, None, None, LAT),
            P(ENS, None, None, LAT),
            P(ENS, None, LAT, None),
            P(),
            P(),
            P(),
            P(),
            P(),
        ),
        out_specs=(P(ENS, None, LAT, None), P(ENS, None, LAT, None), P(), P(), P(), P(), P()),
        check_vma=False,
    )
```

```python
import functools

import jax
import jax.numpy as jnp
from jax import lax
from jax.experimental import pallas as pl
from jax.experimental.pallas import tpu as pltpu
from jax.sharding import Mesh, PartitionSpec as P

BF = jnp.bfloat16
F32 = jnp.float32
HIGH = lax.Precision.HIGHEST
LAT = ("y", "xl", "c")
ENS = ("z", "xh")
CHIPS = ("y", "xl", "z", "xh")
HALF = 48
CH = 96
HID = 512
COLS = 384
ROW = 768
CELLS = 1536
IN_ROWS = 448
IN_HALF = 224
TAP_HALF = 144
MIB = 1024 * 1024


def mm(a, b):
    return lax.dot_general(a, b, (((1,), (0,)), ((), ())), preferred_element_type=F32)


def mm_nt(a, b):
    return lax.dot_general(a, b, (((1,), (1,)), ((), ())), preferred_element_type=F32)


def mm_high(a, b):
    return lax.dot_general(
        a, b, (((1,), (0,)), ((), ())), preferred_element_type=F32, precision=HIGH
    )


def split3(x):
    hi = x.astype(BF)
    rest = x - hi.astype(F32)
    mid = rest.astype(BF)
    low = (rest - mid.astype(F32)).astype(BF)
    return hi, mid, low


def from_left(x):
    lane = lax.broadcasted_iota(jnp.int32, x.shape, 1)
    return jnp.where(lane == 0, 0.0, pltpu.roll(x, 1, 1))


def from_right(x):
    width = x.shape[1]
    lane = lax.broadcasted_iota(jnp.int32, x.shape, 1)
    return jnp.where(lane == width - 1, 0.0, pltpu.roll(x, width - 1, 1))


def sds(shape, dtype):
    return jax.ShapeDtypeStruct(shape, dtype)


def call(body, outs, ins, scratch=(), smem=(), flops=0, name=None, limit=16):
    moved = sum(x.size * x.dtype.itemsize for x in list(ins) + list(outs))
    return pl.pallas_call(
        body,
        out_shape=outs,
        in_specs=[
            pl.BlockSpec(memory_space=pltpu.SMEM if i in smem else pltpu.VMEM)
            for i in range(len(ins))
        ],
        out_specs=[pl.BlockSpec(memory_space=pltpu.VMEM) for _ in outs],
        scratch_shapes=list(scratch),
        compiler_params=pltpu.CompilerParams(vmem_limit_bytes=limit * MIB),
        cost_estimate=pl.CostEstimate(flops=flops, bytes_accessed=moved, transcendentals=0),
        name=name,
    )(*ins)


def payload_kernel(on_ref, grad_ref, out_ref):
    width = on_ref.shape[2]
    blank = jnp.zeros(on_ref.shape[1:], BF)
    for s in range(on_ref.shape[0]):
        on = on_ref[s]
        hi = on.astype(BF)
        grad = grad_ref[s]
        out_ref[s, :, :width] = hi
        out_ref[s, :, width : 2 * width] = (on - hi.astype(F32)).astype(BF)
        if s + 1 < on_ref.shape[0]:
            out_ref[s + 1, :, 2 * width : 3 * width] = hi
        if s > 0:
            out_ref[s - 1, :, 3 * width : 4 * width] = hi
        out_ref[s, :, 4 * width :] = grad.astype(BF)
    out_ref[0, :, 2 * width : 3 * width] = blank
    out_ref[on_ref.shape[0] - 1, :, 3 * width : 4 * width] = blank


def payload(on, grad):
    bands, width, channels = on.shape
    return call(
        payload_kernel, [sds((bands, width, 5 * channels), BF)], [on, grad], name="payload", limit=56
    )[0]


def prep_kernel(
    mix_ref, w1_ref, w2_ref, b1_ref, b2_ref, *refs
):
    stage1, stage2 = refs[-2:]
    flows = mix_ref.shape[0]
    row = lax.broadcasted_iota(jnp.int32, (CH, CH), 0)
    col = lax.broadcasted_iota(jnp.int32, (CH, CH), 1)
    eye = (row == col).astype(F32)
    near = (row // 16) == (col // 16)
    units = []
    for k in range(flows):
        mix = mix_ref[k]
        units.append(jnp.where(row > col, mix, 0.0))
        units.append(jnp.where(row < col, mix, 0.0))
    inner = [jnp.where(near, u, 0.0) for u in units]
    outer = [u - i for u, i in zip(units, inner)]
    power = inner
    blocks = [eye - n for n in inner]
    for _ in range(3):
        power = [mm_high(p, p) for p in power]
        blocks = [mm_high(b, eye + p) for b, p in zip(blocks, power)]
    power = [mm_high(b, o) for b, o in zip(blocks, outer)]
    whole = [eye - p for p in power]
    for _ in range(2):
        power = [mm_high(p, p) for p in power]
        whole = [mm_high(w, eye + p) for w, p in zip(whole, power)]
    inverses = [mm_high(w, b) for w, b in zip(whole, blocks)]
    for k in range(flows):
        inv_ref, lut_ref, w1t_ref, w2t_ref, w2k_ref, w1k_ref, b2c_ref = refs[7 * k : 7 * k + 7]
        inv_ref[...] = mm_high(inverses[2 * k + 1], inverses[2 * k])
        lut_ref[...] = mm_high(units[2 * k] + eye, units[2 * k + 1] + eye).T
        for tap in range(9):
            stage1[tap * HALF : (tap + 1) * HALF, :] = 0.5 * w1_ref[k, tap].astype(F32)
            stage2[tap * CH : (tap + 1) * CH, :] = 0.5 * w2_ref[k, 8 - tap].astype(F32)
        hi, mid, low = split3(0.5 * b1_ref[k : k + 1, :])
        stage1[9 * HALF :, :] = jnp.zeros((IN_ROWS - 9 * HALF, HID), F32)
        for i, part in enumerate((hi, mid, low)):
            stage1[9 * HALF + i : 9 * HALF + i + 1, :] = part.astype(F32)
        w1t_ref[...] = stage1[...].T.astype(BF)
        w2t_ref[...] = stage2[...].T.astype(BF)
        for a in range(3):
            for b in range(3):
                w2k_ref[b * CH : (b + 1) * CH, a * HID : (a + 1) * HID] = w2_ref[k, 3 * a + b]
                w1k_ref[b * HALF : (b + 1) * HALF, a * HID : (a + 1) * HID] = w1_ref[
                    k, 3 * (2 - a) + b
                ]
        b2c_ref[...] = jnp.broadcast_to(b2_ref[k : k + 1, :], (8, CH)).T


def prep(mix_factors, in_kernel, out_kernel, in_bias, out_bias):
    flows = mix_factors.shape[0]
    outs = call(
        prep_kernel,
        [
            sds((CH, CH), F32),
            sds((CH, CH), F32),
            sds((HID, IN_ROWS), BF),
            sds((HID, 9 * CH), BF),
            sds((3 * CH, 3 * HID), BF),
            sds((3 * HALF, 3 * HID), BF),
            sds((CH, 8), F32),
        ]
        * flows,
        [mix_factors, in_kernel, out_kernel, in_bias, out_bias],
        scratch=[pltpu.VMEM((IN_ROWS, HID), F32), pltpu.VMEM((9 * CH, HID), F32)],
        name="prep",
        limit=56,
    )
    return [outs[i::7] for i in range(7)]


def turn_kernel(recv_ref, above_ref, mid_ref, below_ref, ya_ref, ga_ref, stage):
    width = 2 * CH
    row = lax.broadcasted_iota(jnp.int32, (width, width), 0)
    col = lax.broadcasted_iota(jnp.int32, (width, width), 1)
    pick = (col == 4 * (row % HALF) + row // HALF).astype(BF)
    none = jnp.zeros((width, width), BF)
    first = jnp.concatenate([pick, none], axis=1)
    second = jnp.concatenate([none, pick], axis=1)
    both = jnp.concatenate([pick, pick], axis=1)
    sources, count = recv_ref.shape[0], recv_ref.shape[1]
    for s in range(sources):
        stage[s * count : (s + 1) * count, :] = recv_ref[s].astype(F32)
    pair = stage[:, : 2 * width].astype(BF)
    kept = mm_nt(both, pair)
    mid_ref[...] = mm_nt(first, pair).astype(BF)
    pair = stage[:, 2 * width : 4 * width].astype(BF)
    above_ref[...] = mm_nt(first, pair).astype(BF)
    below_ref[...] = mm_nt(second, pair).astype(BF)
    grad = mm_nt(pick, stage[:, 4 * width :].astype(BF))
    for k in range(4):
        ya_ref[:, k * COLS : (k + 1) * COLS] = kept[k * HALF : (k + 1) * HALF]
        ga_ref[:, k * COLS : (k + 1) * COLS] = grad[k * HALF : (k + 1) * HALF]


def turn(recv):
    return call(
        turn_kernel,
        [sds((2 * CH, COLS), BF)] * 3 + [sds((HALF, CELLS), F32)] * 2,
        [recv],
        scratch=[pltpu.VMEM((COLS, recv.shape[2]), F32)],
        flops=4 * 10**9,
        name="turn",
    )


def stack_planes(even, odd, factor=None):
    if factor is not None:
        even = (even.astype(F32) * factor).astype(BF)
        odd = (odd.astype(F32) * factor).astype(BF)
    left = from_left(odd.astype(F32)).astype(BF)
    right = from_right(even.astype(F32)).astype(BF)
    return jnp.concatenate([left, even, odd, right], axis=0)


def fill_input_columns(flags_ref, above_ref, mid_ref, below_ref, columns, first, count):
    refs = {-2: (above_ref, 0), -1: (above_ref, CH), 0: (mid_ref, 0)}
    refs.update({1: (mid_ref, CH), 2: (below_ref, 0), 3: (below_ref, CH)})
    for source in range(first - 1, first + count + 1):
        ref, at = refs[source]
        factor = flags_ref[0] if source < 0 else flags_ref[1] if source > 1 else None
        stacked = stack_planes(ref[at : at + HALF], ref[at + HALF : at + CH], factor)
        for a in range(3):
            target = source - a + 1 - first
            if 0 <= target < count:
                for p in range(2):
                    lane = (2 * target + p) * COLS
                    columns[a * 144 : (a + 1) * 144, lane : lane + COLS] = stacked[
                        p * HALF : p * HALF + 144
                    ]
    extra = IN_ROWS - 9 * HALF
    row = lax.broadcasted_iota(jnp.int32, (extra, count * ROW), 0)
    columns[9 * HALF :, :] = jnp.where(row < 3, 1.0, 0.0).astype(BF)


def fill_grad_columns(flags_ref, above_ref, mid_ref, below_ref, columns):
    for source in range(-2, 4):
        ref = above_ref if source < 0 else below_ref if source > 1 else mid_ref
        factor = flags_ref[0] if source < 0 else flags_ref[1] if source > 1 else None
        at = (source % 2) * 2 * CH
        stacked = stack_planes(ref[at : at + CH], ref[at + CH : at + 2 * CH], factor)
        for a in range(3):
            target = source - a + 2
            if 0 <= target < 4:
                for p in range(2):
                    lane = (2 * target + p) * COLS
                    columns[a * 288 : (a + 1) * 288, lane : lane + COLS] = stacked[
                        p * CH : p * CH + 288
                    ]


def put_out_grad(raw, moved, out_ref):
    for r in range(2):
        for p in range(2):
            lane = (2 * r + p) * COLS
            at = (2 * r + p) * CH
            out_ref[at : at + HALF] = raw[:, lane : lane + COLS].astype(BF)
            out_ref[at + HALF : at + CH] = moved[:, lane : lane + COLS].astype(BF)


def forward_kernel(with_grad, flags_ref, *refs):
    above_ref, mid_ref, below_ref, w1t_ref, w2k_ref, b2_ref, inv_ref, ya_ref, yb_ref = refs[:9]
    columns, pre, outs = refs[-3:]
    if with_grad:
        x_ref, rows, slope_ref, next_ref, grad_ref, moved_ref = refs[9:-3]
    else:
        x_ref, rows, slope_ref, scale_ref = refs[9:-3]
    fill_input_columns(flags_ref, above_ref, mid_ref, below_ref, columns, -1, 4)
    for h in range(4):
        pre[h % 2] = mm(w1t_ref[...], columns[:, h * ROW : (h + 1) * ROW])
        inside = flags_ref[0] if h == 0 else flags_ref[1] if h == 3 else None

        def activate(step, carry):
            at = pl.multiple_of(step * 16, 16)
            half = pre[h % 2, pl.ds(at, 16), :]
            bent = jnp.tanh(half)
            more = 1.0 + bent
            hidden = half * more
            slope = more * (1.0 + half * (1.0 - bent))
            if inside is not None:
                hidden = hidden * inside
                slope = slope * inside
            rows[pl.ds(h * HID + at, 16), :] = hidden.astype(BF)
            slope_ref[pl.ds(h * HID + at, 16), :] = slope
            return carry

        lax.fori_loop(0, HID // 16, activate, 0, unroll=True)
    for r in range(2):
        taps = mm(w2k_ref[...], rows[r * HID : (r + 3) * HID, :])
        even, odd = taps[:, :COLS], taps[:, COLS:]
        lane = 2 * r * COLS
        outs[:, lane : lane + COLS] = from_left(odd[:CH]) + even[CH : 2 * CH] + odd[2 * CH :]
        outs[:, lane + COLS : lane + ROW] = even[:CH] + odd[CH : 2 * CH] + from_right(even[2 * CH :])
    raw = outs[:HALF] + b2_ref[:HALF, :1]
    shift = outs[HALF:] + b2_ref[HALF:, :1]
    inverse = 1.0 + jnp.exp(-(raw + 2.0))
    scale = 1.0 / inverse
    moved_in = yb_ref[...] * inverse - shift
    x = mm_high(inv_ref[...], jnp.concatenate([ya_ref[...], moved_in], axis=0))
    x_ref[...] = x
    if with_grad:
        moved_grad = yb_ref[...]
        moved = moved_grad * scale
        moved_ref[...] = moved
        put_out_grad((moved_grad * yb_ref[...] - 1.0) * (1.0 - scale), moved, grad_ref)
        for k in range(4):
            next_ref[k * HALF : (k + 1) * HALF] = x[:HALF, k * COLS : (k + 1) * COLS].astype(BF)
    else:
        scale_ref[...] = scale


def forward(flags, above, mid, below, w1t, w2k, b2c, inv, ya, yb, with_grad):
    outs = [sds((CH, CELLS), F32), sds((4 * HID, ROW), BF), sds((4 * HID, ROW), F32)]
    if with_grad:
        outs += [
            sds((2 * CH, COLS), BF),
            sds((4 * CH, COLS), BF),
            sds((HALF, CELLS), F32),
        ]
    else:
        outs += [sds((HALF, CELLS), F32)]
    return call(
        functools.partial(forward_kernel, with_grad),
        outs,
        [flags, above, mid, below, w1t, w2k, b2c, inv, ya, yb],
        scratch=[
            pltpu.VMEM((IN_ROWS, 4 * ROW), BF),
            pltpu.VMEM((2, HID, ROW), F32),
            pltpu.VMEM((CH, CELLS), F32),
        ],
        smem=(0,),
        limit=24,
        flops=4 * 10**9,
        name="forward",
    )


def backward_kernel(
    flags_ref, above_ref, mid_ref, below_ref, w2t_ref, slope_ref, w1k_ref, gpre_ref, in_ref,
    columns, hid_grad,
):
    fill_grad_columns(flags_ref, above_ref, mid_ref, below_ref, columns)
    for h in range(4):
        hid_grad[h % 2] = mm(w2t_ref[...], columns[:, h * ROW : (h + 1) * ROW])

        def slope(step, carry):
            at = pl.multiple_of(step * 16, 16)
            gpre_ref[pl.ds(h * HID + at, 16), :] = (
                hid_grad[h % 2, pl.ds(at, 16), :] * slope_ref[pl.ds(h * HID + at, 16), :]
            ).astype(BF)
            return carry

        lax.fori_loop(0, HID // 16, slope, 0, unroll=True)
    b0, b1, b2 = slice(0, HALF), slice(HALF, CH), slice(CH, 3 * HALF)
    for r in range(2):
        taps = mm(w1k_ref[...], gpre_ref[r * HID : (r + 3) * HID, :])
        even, odd = taps[:, :COLS], taps[:, COLS:]
        in_ref[r * CH : r * CH + HALF] = odd[b0] + even[b1] + from_left(odd[b2])
        in_ref[r * CH + HALF : (r + 1) * CH] = from_right(even[b0]) + odd[b1] + even[b2]


def backward(flags, above, mid, below, w2t, slope, w1k):
    return call(
        backward_kernel,
        [sds((4 * HID, ROW), BF), sds((2 * CH, COLS), F32)],
        [flags, above, mid, below, w2t, slope, w1k],
        scratch=[pltpu.VMEM((9 * CH, 4 * ROW), BF), pltpu.VMEM((2, HID, ROW), F32)],
        smem=(0,),
        flops=6 * 10**9,
        limit=20,
        name="backward",
    )


def out_weight_kernel(core_ref, grad_ref, rows_ref, keep_ref, give_ref, bias_ref, left, right, whole):
    for r in range(2):
        at = 2 * r * CH
        stacked = stack_planes(grad_ref[at : at + CH], grad_ref[at + CH : at + 2 * CH])
        left[r] = stacked[: 3 * CH]
        right[r] = stacked[CH:]
    part = [jnp.concatenate([left[r], right[r]], axis=1) for r in range(2)]
    for a in range(3):
        whole[...] = mm_nt(part[0], rows_ref[a * HID : (a + 1) * HID]) + mm_nt(
            part[1], rows_ref[(a + 1) * HID : (a + 2) * HID]
        )
        for ref, core in ((keep_ref, core_ref[0]), (give_ref, 1 - core_ref[0])):
            ref[a] = whole[pl.ds(pl.multiple_of(core * TAP_HALF, 8), TAP_HALF), :]
    ones = jnp.ones((8, COLS), BF)
    total = mm_nt(ones, grad_ref[:CH]) + mm_nt(ones, grad_ref[CH : 2 * CH])
    bias_ref[...] = total + (
        mm_nt(ones, grad_ref[2 * CH : 3 * CH]) + mm_nt(ones, grad_ref[3 * CH :])
    )


def out_weight(core, grad, rows):
    return call(
        out_weight_kernel,
        [sds((3, TAP_HALF, HID), F32), sds((3, TAP_HALF, HID), F32), sds((8, CH), F32)],
        [core, grad, rows],
        scratch=[
            pltpu.VMEM((2, 3 * CH, COLS), BF),
            pltpu.VMEM((2, 3 * CH, COLS), BF),
            pltpu.VMEM((3 * CH, HID), F32),
        ],
        smem=(0,),
        flops=2 * 10**9,
        name="out_weight",
    )


def in_weight_kernel(
    core_ref, flags_ref, above_ref, mid_ref, below_ref, gpre_ref, keep_ref, give_ref, columns,
    whole,
):
    fill_input_columns(flags_ref, above_ref, mid_ref, below_ref, columns, 0, 2)
    whole[...] = mm_nt(columns[:, :ROW], gpre_ref[HID : 2 * HID]) + mm_nt(
        columns[:, ROW:], gpre_ref[2 * HID : 3 * HID]
    )
    for ref, core in ((keep_ref, core_ref[0]), (give_ref, 1 - core_ref[0])):
        ref[...] = whole[pl.ds(pl.multiple_of(core * IN_HALF, 8), IN_HALF), :]


def in_weight(core, flags, above, mid, below, gpre):
    return call(
        in_weight_kernel,
        [sds((IN_HALF, HID), F32), sds((IN_HALF, HID), F32)],
        [core, flags, above, mid, below, gpre],
        scratch=[pltpu.VMEM((IN_ROWS, CELLS), BF), pltpu.VMEM((IN_ROWS, HID), F32)],
        smem=(0, 1),
        flops=10**9,
        name="in_weight",
    )


def close_kernel(next_step, flow, *refs):
    in_ref, ga_ref, moved_ref, lut_ref, x_ref, mix_ref, bias_ref = refs[:7]
    whole = refs[-1]
    if next_step:
        scale_ref, gx_ref, small, grad_ref, nmoved_ref = refs[7:-1]
    else:
        gx_ref, small = refs[7:-1]
    for k in range(4):
        lane = k * COLS
        whole[:HALF, lane : lane + COLS] = (
            ga_ref[:HALF, lane : lane + COLS] + in_ref[k * HALF : (k + 1) * HALF]
        )
    whole[HALF:] = moved_ref[...]
    gx = mm_high(lut_ref[...], whole[...])
    gx_ref[...] = gx
    if next_step:
        scale = scale_ref[...]
        moved_grad = gx[HALF:]
        moved = moved_grad * scale
        nmoved_ref[...] = moved
        put_out_grad((moved_grad * x_ref[HALF:] - 1.0) * (1.0 - scale), moved, grad_ref)
    ghi, gmid, _ = split3(whole[...])
    xhi, xmid, _ = split3(x_ref[...])
    outer = mm_nt(ghi, xhi) + (mm_nt(ghi, xmid) + mm_nt(gmid, xhi))
    row = lax.broadcasted_iota(jnp.int32, (CH, CH), 0)
    col = lax.broadcasted_iota(jnp.int32, (CH, CH), 1)
    eye = (row == col).astype(F32)
    mix = mix_ref[flow]
    lower = jnp.where(row > col, mix, 0.0) + eye
    upper = jnp.where(row < col, mix, 0.0) + eye
    by_upper = mm_high(outer, upper.T)
    by_lower = mm_high(lower.T, outer)
    small[:, :CH] = jnp.where(row > col, by_upper, jnp.where(row < col, by_lower, 0.0))
    small[:, CH:] = jnp.zeros((CH, 2 * 128 - CH), F32)
    small[:8, 128 : 128 + CH] = bias_ref[...]


def close(gin, ga, moved, lut, x, mix, flow, bias, scale=None):
    outs = [sds((CH, CELLS), F32), sds((CH, 256), F32)]
    ins = [gin, ga, moved, lut, x, mix, bias]
    if scale is not None:
        outs += [sds((4 * CH, COLS), BF), sds((HALF, CELLS), F32)]
        ins += [scale]
    return call(
        functools.partial(close_kernel, scale is not None, flow),
        outs,
        ins,
        scratch=[pltpu.VMEM((CH, CELLS), F32)],
        flops=10**9,
        name="close",
    )


def weave_kernel(x_ref, out_ref):
    size = 256
    row = lax.broadcasted_iota(jnp.int32, (size, size), 0)
    col = lax.broadcasted_iota(jnp.int32, (size, size), 1)
    place = (col == 2 * (row % 128) + row // 128).astype(BF)
    for r in range(2):
        for t in range(3):
            lane = r * ROW + t * 128
            pair = jnp.concatenate(
                [x_ref[:, lane : lane + 128], x_ref[:, lane + COLS : lane + COLS + 128]], axis=1
            )
            hi, mid, low = split3(pair)
            woven = mm(hi, place) + (mm(mid, place) + mm(low, place))
            out_ref[0, :, r, t * size : (t + 1) * size] = woven


def weave(x):
    return call(weave_kernel, [sds((1, CH, 2, ROW), F32)], [x], name="weave")[0]


FLOW_ROWS = 704
GROUP = 88


def merge_kernel(*refs):
    out_ref, total = refs[-2:]
    for k in range(2):
        own_in, own_out, got_in, got_out, small = refs[5 * k : 5 * k + 5]
        at = k * FLOW_ROWS
        total[at : at + IN_HALF] = own_in[...] + got_in[...]
        for a in range(3):
            start = at + IN_HALF + a * TAP_HALF
            total[start : start + TAP_HALF] = own_out[a] + got_out[a]
        start = at + FLOW_ROWS - HALF
        total[start : start + HALF, :256] = small[:HALF]
        total[start : start + HALF, 256:] = small[HALF:]
    for g in range(2 * FLOW_ROWS // GROUP):
        for lane in range(4):
            out_ref[4 * g + lane] = total[
                g * GROUP : (g + 1) * GROUP, lane * 128 : (lane + 1) * 128
            ].astype(BF)


def merge(first, second):
    shares = 2 * FLOW_ROWS // GROUP * 4
    return call(
        merge_kernel,
        [sds((shares, GROUP, 128), BF)],
        [*first, *second],
        scratch=[pltpu.VMEM((2 * FLOW_ROWS, HID), F32)],
        name="merge",
    )[0]


def total_kernel(cells, shares_ref, out_ref):
    total = shares_ref[0].astype(F32)
    for s in range(1, shares_ref.shape[0]):
        total += shares_ref[s].astype(F32)
    mean = (total * (1.0 / cells)).astype(BF)
    for s in range(shares_ref.shape[0]):
        out_ref[s] = mean


def totals(shares, cells):
    return call(
        functools.partial(total_kernel, cells), [sds(shares.shape, BF)], [shares], name="totals"
    )[0]


def unpack_kernel(core_ref, mine_ref, other_ref, win_ref, wout_ref, mix_ref, bin_ref, bout_ref, rows):
    mine_first = core_ref[0] == 0
    for half in range(2):
        for g in range(2 * FLOW_ROWS // GROUP):
            for lane in range(4):
                mine = mine_ref[4 * g + lane].astype(F32)
                other = other_ref[4 * g + lane].astype(F32)
                first, second = (mine, other) if half == 0 else (other, mine)
                rows[half, g * GROUP : (g + 1) * GROUP, lane * 128 : (lane + 1) * 128] = jnp.where(
                    mine_first, first, second
                )
    for k in range(2):
        at = k * FLOW_ROWS
        win_ref[k, :IN_HALF] = rows[0, at : at + IN_HALF]
        win_ref[k, IN_HALF:] = rows[1, at : at + 9 * HALF - IN_HALF]
        bin_ref[k : k + 1, :] = rows[1, at + 9 * HALF - IN_HALF : at + 9 * HALF - IN_HALF + 1]
        for a in range(3):
            start = at + IN_HALF + a * TAP_HALF
            wout_ref[k, 3 * a + 2] = rows[0, start : start + CH]
            wout_ref[k, 3 * a + 1, :HALF] = rows[0, start + CH : start + TAP_HALF]
            wout_ref[k, 3 * a + 1, HALF:] = rows[1, start : start + HALF]
            wout_ref[k, 3 * a] = rows[1, start + HALF : start + TAP_HALF]
        start = at + FLOW_ROWS - HALF
        block = rows[0, start : start + HALF] + rows[1, start : start + HALF]
        mix_ref[k, :HALF] = block[:, :CH]
        mix_ref[k, HALF:] = block[:, 256 : 256 + CH]
        bout_ref[k : k + 1, :] = block[:1, 128 : 128 + CH]


def unpack(core, mine, other):
    return call(
        unpack_kernel,
        [
            sds((2, 9 * HALF, HID), F32),
            sds((2, 9, CH, HID), F32),
            sds((2, CH, CH), F32),
            sds((2, HID), F32),
            sds((2, CH), F32),
        ],
        [core, mine, other],
        scratch=[pltpu.VMEM((2, 2 * FLOW_ROWS, HID), F32)],
        smem=(0,),
        name="unpack",
    )


def after(x, *others):
    return lax.optimization_barrier((x, *others))[0]


def local(passed_on, passed_grad, latent, mix_factors, in_kernel, in_bias, out_kernel, out_bias):
    lat_index = lax.axis_index(LAT)
    lat_count = lax.axis_size(LAT)
    forth = [(i, (i + 1) % lat_count) for i in range(lat_count)]
    back = [(t, s) for s, t in forth]
    swap = [(0, 1), (1, 0)]
    flags = jnp.stack([lat_index > 0, lat_index < lat_count - 1]).astype(F32)
    core = lax.axis_index("c").astype(jnp.int32).reshape(1)

    block = payload(
        jnp.transpose(passed_on[0], (1, 2, 0)), jnp.transpose(passed_grad[0], (1, 2, 0))
    )
    recv = lax.all_to_all(block, LAT, 0, 0, tiled=True)
    inv, lut, w1t, w2t, w2k, w1k, b2c = prep(mix_factors, in_kernel, out_kernel, in_bias, out_bias)
    w1 = in_kernel.reshape(2, 9 * HALF, HID)
    yb = latent.reshape(HALF, CELLS)

    above, mid, below, ya, ga = turn(recv)
    x1, rows1, slope1, next_mid, grad1, moved1 = forward(
        flags, above, mid, below, w1t[1], w2k[1], b2c[1], inv[1], ya, yb, True
    )
    above0 = lax.ppermute(next_mid, LAT, forth)
    below0 = lax.ppermute(next_mid, LAT, back)
    top1 = lax.ppermute(grad1, LAT, forth)
    bottom1 = lax.ppermute(grad1, LAT, back)
    keep_out1, give_out1, bias1 = out_weight(core, grad1, rows1)
    x0, rows0, slope0, scale0 = forward(
        after(flags, keep_out1), above0, next_mid, below0, w1t[0], w2k[0], b2c[0], inv[0],
        x1[:HALF], x1[HALF:], False,
    )
    got_out1 = lax.ppermute(give_out1, "c", swap)
    gpre1, in1 = backward(after(flags, x0), top1, grad1, bottom1, w2t[1], slope1, w1k[1])
    gx1, small1, grad0, moved0 = close(
        in1, ga, moved1, lut[1], x1, mix_factors, 1, bias1, scale0
    )
    top0 = lax.ppermute(grad0, LAT, forth)
    bottom0 = lax.ppermute(grad0, LAT, back)
    keep_in1, give_in1 = in_weight(after(core, grad0), flags, above, mid, below, gpre1)
    got_in1 = lax.ppermute(give_in1, "c", swap)
    keep_out0, give_out0, bias0 = out_weight(after(core, keep_in1), grad0, rows0)
    rebuilt = weave(after(x0, keep_out0))
    gpre0, in0 = backward(after(flags, rebuilt), top0, grad0, bottom0, w2t[0], slope0, w1k[0])
    got_out0 = lax.ppermute(give_out0, "c", swap)
    keep_in0, give_in0 = in_weight(after(core, in0), flags, above0, next_mid, below0, gpre0)
    got_in0 = lax.ppermute(give_in0, "c", swap)
    gx0, small0 = close(
        after(in0, keep_in0), gx1, moved0, lut[0], x0, mix_factors, 0, bias0
    )

    packed = merge(
        (keep_in0, keep_out0, got_in0, got_out0, small0),
        (keep_in1, keep_out1, got_in1, got_out1, small1),
    )
    shares = lax.all_to_all(packed, CHIPS, 0, 0, tiled=True)
    input_grad = weave(after(gx0, packed))
    cells = float(CELLS * lat_count * lax.axis_size(ENS))
    spread = totals(after(shares, input_grad), cells)
    mine = lax.all_to_all(spread, CHIPS, 0, 0, tiled=True)
    other = lax.ppermute(mine, "c", swap)
    in_grad, out_grad, mix_grad, in_bias_grad, out_bias_grad = unpack(core, mine, other)
    return (
        rebuilt,
        input_grad,
        mix_grad,
        in_grad.reshape(2, 9, HALF, HID),
        in_bias_grad,
        out_grad,
        out_bias_grad,
    )


def solution(mesh):
    split = Mesh(mesh.devices.reshape(4, 2, 2, 4, 2), ("y", "xl", "c", "z", "xh"))
    return jax.shard_map(
        local,
        mesh=split,
        in_specs=(
            P(ENS, None, None, LAT),
            P(ENS, None, None, LAT),
            P(ENS, None, LAT, None),
            P(),
            P(),
            P(),
            P(),
            P(),
        ),
        out_specs=(P(ENS, None, LAT, None), P(ENS, None, LAT, None), P(), P(), P(), P(), P()),
        check_vma=False,
    )
```

```python
import functools

import jax
import jax.numpy as jnp
from jax import lax
from jax.experimental import pallas as pl
from jax.experimental.pallas import tpu as pltpu
from jax.sharding import Mesh, PartitionSpec as P

BF = jnp.bfloat16
F32 = jnp.float32
HIGH = lax.Precision.HIGHEST
LAT = ("y", "xl", "c")
ENS = ("z", "xh")
CHIPS = ("y", "xl", "z", "xh")
HALF = 48
CH = 96
HID = 512
COLS = 384
ROW = 768
CELLS = 1536
IN_ROWS = 448
IN_HALF = 224
TAP_HALF = 144
MIB = 1024 * 1024


def mm(a, b):
    return lax.dot_general(a, b, (((1,), (0,)), ((), ())), preferred_element_type=F32)


def mm_nt(a, b):
    return lax.dot_general(a, b, (((1,), (1,)), ((), ())), preferred_element_type=F32)


def mm_high(a, b):
    return lax.dot_general(
        a, b, (((1,), (0,)), ((), ())), preferred_element_type=F32, precision=HIGH
    )


def split3(x):
    hi = x.astype(BF)
    rest = x - hi.astype(F32)
    mid = rest.astype(BF)
    low = (rest - mid.astype(F32)).astype(BF)
    return hi, mid, low


def from_left(x):
    lane = lax.broadcasted_iota(jnp.int32, x.shape, 1)
    return jnp.where(lane == 0, 0.0, pltpu.roll(x, 1, 1))


def from_right(x):
    width = x.shape[1]
    lane = lax.broadcasted_iota(jnp.int32, x.shape, 1)
    return jnp.where(lane == width - 1, 0.0, pltpu.roll(x, width - 1, 1))


def sds(shape, dtype):
    return jax.ShapeDtypeStruct(shape, dtype)


def call(
    body, outs, ins, scratch=(), smem=(), hbm=(), hbm_outs=(), alias=None, flops=0, name=None, limit=16
):
    moved = sum(x.size * x.dtype.itemsize for x in list(ins) + list(outs))
    return pl.pallas_call(
        body,
        out_shape=outs,
        in_specs=[
            pl.BlockSpec(
                memory_space=pltpu.SMEM if i in smem else pltpu.HBM if i in hbm else pltpu.VMEM
            )
            for i in range(len(ins))
        ],
        out_specs=[
            pl.BlockSpec(memory_space=pltpu.HBM if i in hbm_outs else pltpu.VMEM)
            for i in range(len(outs))
        ],
        scratch_shapes=list(scratch),
        input_output_aliases=alias or {},
        compiler_params=pltpu.CompilerParams(vmem_limit_bytes=limit * MIB),
        cost_estimate=pl.CostEstimate(flops=flops, bytes_accessed=moved, transcendentals=0),
        name=name,
    )(*ins)


def payload_kernel(on_ref, grad_ref, out_ref):
    width = on_ref.shape[2]
    blank = jnp.zeros(on_ref.shape[1:], BF)
    for s in range(on_ref.shape[0]):
        on = on_ref[s]
        hi = on.astype(BF)
        grad = grad_ref[s]
        out_ref[s, :, :width] = hi
        out_ref[s, :, width : 2 * width] = (on - hi.astype(F32)).astype(BF)
        if s + 1 < on_ref.shape[0]:
            out_ref[s + 1, :, 2 * width : 3 * width] = hi
        if s > 0:
            out_ref[s - 1, :, 3 * width : 4 * width] = hi
        out_ref[s, :, 4 * width :] = grad.astype(BF)
    out_ref[0, :, 2 * width : 3 * width] = blank
    out_ref[on_ref.shape[0] - 1, :, 3 * width : 4 * width] = blank


def payload(on, grad):
    bands, width, channels = on.shape
    return call(
        payload_kernel, [sds((bands, width, 5 * channels), BF)], [on, grad], name="payload", limit=56
    )[0]


def prep_kernel(
    mix_ref, w1_ref, w2_ref, b1_ref, b2_ref, *refs
):
    stage1, stage2 = refs[-2:]
    flows = mix_ref.shape[0]
    row = lax.broadcasted_iota(jnp.int32, (CH, CH), 0)
    col = lax.broadcasted_iota(jnp.int32, (CH, CH), 1)
    eye = (row == col).astype(F32)
    near = (row // 16) == (col // 16)
    units = []
    for k in range(flows):
        mix = mix_ref[k]
        units.append(jnp.where(row > col, mix, 0.0))
        units.append(jnp.where(row < col, mix, 0.0))
    inner = [jnp.where(near, u, 0.0) for u in units]
    outer = [u - i for u, i in zip(units, inner)]
    power = inner
    blocks = [eye - n for n in inner]
    for _ in range(3):
        power = [mm_high(p, p) for p in power]
        blocks = [mm_high(b, eye + p) for b, p in zip(blocks, power)]
    power = [mm_high(b, o) for b, o in zip(blocks, outer)]
    whole = [eye - p for p in power]
    for _ in range(2):
        power = [mm_high(p, p) for p in power]
        whole = [mm_high(w, eye + p) for w, p in zip(whole, power)]
    inverses = [mm_high(w, b) for w, b in zip(whole, blocks)]
    for k in range(flows):
        inv_ref, lut_ref, w1t_ref, w2t_ref, w2k_ref, w1k_ref, b2c_ref = refs[7 * k : 7 * k + 7]
        inv_ref[...] = mm_high(inverses[2 * k + 1], inverses[2 * k])
        lut_ref[...] = mm_high(units[2 * k] + eye, units[2 * k + 1] + eye).T
        for tap in range(9):
            stage1[tap * HALF : (tap + 1) * HALF, :] = 0.5 * w1_ref[k, tap].astype(F32)
            stage2[tap * CH : (tap + 1) * CH, :] = 0.5 * w2_ref[k, 8 - tap].astype(F32)
        hi, mid, low = split3(0.5 * b1_ref[k : k + 1, :])
        stage1[9 * HALF :, :] = jnp.zeros((IN_ROWS - 9 * HALF, HID), F32)
        for i, part in enumerate((hi, mid, low)):
            stage1[9 * HALF + i : 9 * HALF + i + 1, :] = part.astype(F32)
        w1t_ref[...] = stage1[...].T.astype(BF)
        w2t_ref[...] = stage2[...].T.astype(BF)
        for a in range(3):
            for b in range(3):
                w2k_ref[b * CH : (b + 1) * CH, a * HID : (a + 1) * HID] = w2_ref[k, 3 * a + b]
                w1k_ref[b * HALF : (b + 1) * HALF, a * HID : (a + 1) * HID] = w1_ref[
                    k, 3 * (2 - a) + b
                ]
        b2c_ref[...] = jnp.broadcast_to(b2_ref[k : k + 1, :], (8, CH)).T


def prep(mix_factors, in_kernel, out_kernel, in_bias, out_bias):
    flows = mix_factors.shape[0]
    outs = call(
        prep_kernel,
        [
            sds((CH, CH), F32),
            sds((CH, CH), F32),
            sds((HID, IN_ROWS), BF),
            sds((HID, 9 * CH), BF),
            sds((3 * CH, 3 * HID), BF),
            sds((3 * HALF, 3 * HID), BF),
            sds((CH, 8), F32),
        ]
        * flows,
        [mix_factors, in_kernel, out_kernel, in_bias, out_bias],
        scratch=[pltpu.VMEM((IN_ROWS, HID), F32), pltpu.VMEM((9 * CH, HID), F32)],
        name="prep",
        limit=56,
    )
    return [outs[i::7] for i in range(7)]


def turn_kernel(recv_ref, above_ref, mid_ref, below_ref, ya_ref, ga_ref, stage):
    width = 2 * CH
    row = lax.broadcasted_iota(jnp.int32, (width, width), 0)
    col = lax.broadcasted_iota(jnp.int32, (width, width), 1)
    pick = (col == 4 * (row % HALF) + row // HALF).astype(BF)
    none = jnp.zeros((width, width), BF)
    first = jnp.concatenate([pick, none], axis=1)
    second = jnp.concatenate([none, pick], axis=1)
    both = jnp.concatenate([pick, pick], axis=1)
    sources, count = recv_ref.shape[0], recv_ref.shape[1]
    for s in range(sources):
        stage[s * count : (s + 1) * count, :] = recv_ref[s].astype(F32)
    pair = stage[:, : 2 * width].astype(BF)
    kept = mm_nt(both, pair)
    mid_ref[...] = mm_nt(first, pair).astype(BF)
    pair = stage[:, 2 * width : 4 * width].astype(BF)
    above_ref[...] = mm_nt(first, pair).astype(BF)
    below_ref[...] = mm_nt(second, pair).astype(BF)
    grad = mm_nt(pick, stage[:, 4 * width :].astype(BF))
    for k in range(4):
        ya_ref[:, k * COLS : (k + 1) * COLS] = kept[k * HALF : (k + 1) * HALF]
        ga_ref[:, k * COLS : (k + 1) * COLS] = grad[k * HALF : (k + 1) * HALF]


def turn(recv):
    return call(
        turn_kernel,
        [sds((2 * CH, COLS), BF)] * 3 + [sds((HALF, CELLS), F32)] * 2,
        [recv],
        scratch=[pltpu.VMEM((COLS, recv.shape[2]), F32)],
        flops=4 * 10**9,
        name="turn",
    )


def stack_planes(even, odd, factor=None):
    if factor is not None:
        even = (even.astype(F32) * factor).astype(BF)
        odd = (odd.astype(F32) * factor).astype(BF)
    left = from_left(odd.astype(F32)).astype(BF)
    right = from_right(even.astype(F32)).astype(BF)
    return jnp.concatenate([left, even, odd, right], axis=0)


def fill_input_columns(flags_ref, above_ref, mid_ref, below_ref, columns, first, count):
    refs = {-2: (above_ref, 0), -1: (above_ref, CH), 0: (mid_ref, 0)}
    refs.update({1: (mid_ref, CH), 2: (below_ref, 0), 3: (below_ref, CH)})
    for source in range(first - 1, first + count + 1):
        ref, at = refs[source]
        factor = flags_ref[0] if source < 0 else flags_ref[1] if source > 1 else None
        stacked = stack_planes(ref[at : at + HALF], ref[at + HALF : at + CH], factor)
        for a in range(3):
            target = source - a + 1 - first
            if 0 <= target < count:
                for p in range(2):
                    lane = (2 * target + p) * COLS
                    columns[a * 144 : (a + 1) * 144, lane : lane + COLS] = stacked[
                        p * HALF : p * HALF + 144
                    ]
    extra = IN_ROWS - 9 * HALF
    row = lax.broadcasted_iota(jnp.int32, (extra, count * ROW), 0)
    columns[9 * HALF :, :] = jnp.where(row < 3, 1.0, 0.0).astype(BF)


def fill_grad_columns(flags_ref, above_ref, mid_ref, below_ref, columns):
    for source in range(-2, 4):
        ref = above_ref if source < 0 else below_ref if source > 1 else mid_ref
        factor = flags_ref[0] if source < 0 else flags_ref[1] if source > 1 else None
        at = (source % 2) * 2 * CH
        stacked = stack_planes(ref[at : at + CH], ref[at + CH : at + 2 * CH], factor)
        for a in range(3):
            target = source - a + 2
            if 0 <= target < 4:
                for p in range(2):
                    lane = (2 * target + p) * COLS
                    columns[a * 288 : (a + 1) * 288, lane : lane + COLS] = stacked[
                        p * CH : p * CH + 288
                    ]


def put_out_grad(raw, moved, out_ref):
    for r in range(2):
        for p in range(2):
            lane = (2 * r + p) * COLS
            at = (2 * r + p) * CH
            out_ref[at : at + HALF] = raw[:, lane : lane + COLS].astype(BF)
            out_ref[at + HALF : at + CH] = moved[:, lane : lane + COLS].astype(BF)


def forward_kernel(with_grad, flags_ref, *refs):
    above_ref, mid_ref, below_ref, w1t_ref, w2k_ref, b2_ref, inv_ref, ya_ref, yb_ref = refs[:9]
    columns, pre, outs = refs[-3:]
    if with_grad:
        x_ref, rows, slope_ref, next_ref, grad_ref, moved_ref = refs[9:-3]
    else:
        x_ref, rows, slope_ref, scale_ref = refs[9:-3]
    fill_input_columns(flags_ref, above_ref, mid_ref, below_ref, columns, -1, 4)
    for h in range(4):
        pre[h % 2] = mm(w1t_ref[...], columns[:, h * ROW : (h + 1) * ROW])
        inside = flags_ref[0] if h == 0 else flags_ref[1] if h == 3 else None

        def activate(step, carry):
            at = pl.multiple_of(step * 16, 16)
            half = pre[h % 2, pl.ds(at, 16), :]
            bent = jnp.tanh(half)
            more = 1.0 + bent
            hidden = half * more
            slope = more * (1.0 + half * (1.0 - bent))
            if inside is not None:
                hidden = hidden * inside
                slope = slope * inside
            rows[pl.ds(h * HID + at, 16), :] = hidden.astype(BF)
            slope_ref[pl.ds(h * HID + at, 16), :] = slope
            return carry

        lax.fori_loop(0, HID // 16, activate, 0, unroll=True)
    for r in range(2):
        taps = mm(w2k_ref[...], rows[r * HID : (r + 3) * HID, :])
        even, odd = taps[:, :COLS], taps[:, COLS:]
        lane = 2 * r * COLS
        outs[:, lane : lane + COLS] = from_left(odd[:CH]) + even[CH : 2 * CH] + odd[2 * CH :]
        outs[:, lane + COLS : lane + ROW] = even[:CH] + odd[CH : 2 * CH] + from_right(even[2 * CH :])
    raw = outs[:HALF] + b2_ref[:HALF, :1]
    shift = outs[HALF:] + b2_ref[HALF:, :1]
    inverse = 1.0 + jnp.exp(-(raw + 2.0))
    scale = 1.0 / inverse
    moved_in = yb_ref[...] * inverse - shift
    x = mm_high(inv_ref[...], jnp.concatenate([ya_ref[...], moved_in], axis=0))
    x_ref[...] = x
    if with_grad:
        moved_grad = yb_ref[...]
        moved = moved_grad * scale
        moved_ref[...] = moved
        put_out_grad((moved_grad * yb_ref[...] - 1.0) * (1.0 - scale), moved, grad_ref)
        for k in range(4):
            next_ref[k * HALF : (k + 1) * HALF] = x[:HALF, k * COLS : (k + 1) * COLS].astype(BF)
    else:
        scale_ref[...] = scale


def forward(flags, above, mid, below, w1t, w2k, b2c, inv, ya, yb, with_grad):
    outs = [sds((CH, CELLS), F32), sds((4 * HID, ROW), BF), sds((4 * HID, ROW), F32)]
    if with_grad:
        outs += [
            sds((2 * CH, COLS), BF),
            sds((4 * CH, COLS), BF),
            sds((HALF, CELLS), F32),
        ]
    else:
        outs += [sds((HALF, CELLS), F32)]
    return call(
        functools.partial(forward_kernel, with_grad),
        outs,
        [flags, above, mid, below, w1t, w2k, b2c, inv, ya, yb],
        scratch=[
            pltpu.VMEM((IN_ROWS, 4 * ROW), BF),
            pltpu.VMEM((2, HID, ROW), F32),
            pltpu.VMEM((CH, CELLS), F32),
        ],
        smem=(0,),
        limit=24,
        flops=4 * 10**9,
        name="forward",
    )


def backward_kernel(
    flags_ref, above_ref, mid_ref, below_ref, w2t_ref, slope_ref, w1k_ref, gpre_ref, in_ref,
    columns, hid_grad,
):
    fill_grad_columns(flags_ref, above_ref, mid_ref, below_ref, columns)
    for h in range(4):
        hid_grad[h % 2] = mm(w2t_ref[...], columns[:, h * ROW : (h + 1) * ROW])

        def slope(step, carry):
            at = pl.multiple_of(step * 16, 16)
            gpre_ref[pl.ds(h * HID + at, 16), :] = (
                hid_grad[h % 2, pl.ds(at, 16), :] * slope_ref[pl.ds(h * HID + at, 16), :]
            ).astype(BF)
            return carry

        lax.fori_loop(0, HID // 16, slope, 0, unroll=True)
    b0, b1, b2 = slice(0, HALF), slice(HALF, CH), slice(CH, 3 * HALF)
    for r in range(2):
        taps = mm(w1k_ref[...], gpre_ref[r * HID : (r + 3) * HID, :])
        even, odd = taps[:, :COLS], taps[:, COLS:]
        in_ref[r * CH : r * CH + HALF] = odd[b0] + even[b1] + from_left(odd[b2])
        in_ref[r * CH + HALF : (r + 1) * CH] = from_right(even[b0]) + odd[b1] + even[b2]


def backward(flags, above, mid, below, w2t, slope, w1k):
    return call(
        backward_kernel,
        [sds((4 * HID, ROW), BF), sds((2 * CH, COLS), F32)],
        [flags, above, mid, below, w2t, slope, w1k],
        scratch=[pltpu.VMEM((9 * CH, 4 * ROW), BF), pltpu.VMEM((2, HID, ROW), F32)],
        smem=(0,),
        flops=6 * 10**9,
        limit=20,
        name="backward",
    )


def out_weight_kernel(core_ref, grad_ref, rows_ref, keep_ref, give_ref, bias_ref, left, right, whole):
    for r in range(2):
        at = 2 * r * CH
        stacked = stack_planes(grad_ref[at : at + CH], grad_ref[at + CH : at + 2 * CH])
        left[r] = stacked[: 3 * CH]
        right[r] = stacked[CH:]
    part = [jnp.concatenate([left[r], right[r]], axis=1) for r in range(2)]
    for a in range(3):
        whole[...] = mm_nt(part[0], rows_ref[a * HID : (a + 1) * HID]) + mm_nt(
            part[1], rows_ref[(a + 1) * HID : (a + 2) * HID]
        )
        for ref, core in ((keep_ref, core_ref[0]), (give_ref, 1 - core_ref[0])):
            ref[a] = whole[pl.ds(pl.multiple_of(core * TAP_HALF, 8), TAP_HALF), :]
    ones = jnp.ones((8, COLS), BF)
    total = mm_nt(ones, grad_ref[:CH]) + mm_nt(ones, grad_ref[CH : 2 * CH])
    bias_ref[...] = total + (
        mm_nt(ones, grad_ref[2 * CH : 3 * CH]) + mm_nt(ones, grad_ref[3 * CH :])
    )


def out_weight(core, grad, rows):
    return call(
        out_weight_kernel,
        [sds((3, TAP_HALF, HID), F32), sds((3, TAP_HALF, HID), F32), sds((8, CH), F32)],
        [core, grad, rows],
        scratch=[
            pltpu.VMEM((2, 3 * CH, COLS), BF),
            pltpu.VMEM((2, 3 * CH, COLS), BF),
            pltpu.VMEM((3 * CH, HID), F32),
        ],
        smem=(0,),
        flops=2 * 10**9,
        name="out_weight",
    )


def in_weight_kernel(
    core_ref, flags_ref, above_ref, mid_ref, below_ref, gpre_ref, keep_ref, give_ref, columns,
    whole,
):
    fill_input_columns(flags_ref, above_ref, mid_ref, below_ref, columns, 0, 2)
    whole[...] = mm_nt(columns[:, :ROW], gpre_ref[HID : 2 * HID]) + mm_nt(
        columns[:, ROW:], gpre_ref[2 * HID : 3 * HID]
    )
    for ref, core in ((keep_ref, core_ref[0]), (give_ref, 1 - core_ref[0])):
        ref[...] = whole[pl.ds(pl.multiple_of(core * IN_HALF, 8), IN_HALF), :]


def in_weight(core, flags, above, mid, below, gpre):
    return call(
        in_weight_kernel,
        [sds((IN_HALF, HID), F32), sds((IN_HALF, HID), F32)],
        [core, flags, above, mid, below, gpre],
        scratch=[pltpu.VMEM((IN_ROWS, CELLS), BF), pltpu.VMEM((IN_ROWS, HID), F32)],
        smem=(0, 1),
        flops=10**9,
        name="in_weight",
    )


def close_kernel(next_step, flow, *refs):
    in_ref, ga_ref, moved_ref, lut_ref, x_ref, mix_ref, bias_ref = refs[:7]
    whole = refs[-1]
    if next_step:
        scale_ref, gx_ref, small, grad_ref, nmoved_ref = refs[7:-1]
    else:
        gx_ref, small = refs[7:-1]
    for k in range(4):
        lane = k * COLS
        whole[:HALF, lane : lane + COLS] = (
            ga_ref[:HALF, lane : lane + COLS] + in_ref[k * HALF : (k + 1) * HALF]
        )
    whole[HALF:] = moved_ref[...]
    gx = mm_high(lut_ref[...], whole[...])
    gx_ref[...] = gx
    if next_step:
        scale = scale_ref[...]
        moved_grad = gx[HALF:]
        moved = moved_grad * scale
        nmoved_ref[...] = moved
        put_out_grad((moved_grad * x_ref[HALF:] - 1.0) * (1.0 - scale), moved, grad_ref)
    ghi, gmid, _ = split3(whole[...])
    xhi, xmid, _ = split3(x_ref[...])
    outer = mm_nt(ghi, xhi) + (mm_nt(ghi, xmid) + mm_nt(gmid, xhi))
    row = lax.broadcasted_iota(jnp.int32, (CH, CH), 0)
    col = lax.broadcasted_iota(jnp.int32, (CH, CH), 1)
    eye = (row == col).astype(F32)
    mix = mix_ref[flow]
    lower = jnp.where(row > col, mix, 0.0) + eye
    upper = jnp.where(row < col, mix, 0.0) + eye
    by_upper = mm_high(outer, upper.T)
    by_lower = mm_high(lower.T, outer)
    small[:, :CH] = jnp.where(row > col, by_upper, jnp.where(row < col, by_lower, 0.0))
    small[:, CH:] = jnp.zeros((CH, 2 * 128 - CH), F32)
    small[:8, 128 : 128 + CH] = bias_ref[...]


def close(gin, ga, moved, lut, x, mix, flow, bias, scale=None):
    outs = [sds((CH, CELLS), F32), sds((CH, 256), F32)]
    ins = [gin, ga, moved, lut, x, mix, bias]
    if scale is not None:
        outs += [sds((4 * CH, COLS), BF), sds((HALF, CELLS), F32)]
        ins += [scale]
    return call(
        functools.partial(close_kernel, scale is not None, flow),
        outs,
        ins,
        scratch=[pltpu.VMEM((CH, CELLS), F32)],
        flops=10**9,
        name="close",
    )


def weave_kernel(x_ref, out_ref):
    size = 256
    row = lax.broadcasted_iota(jnp.int32, (size, size), 0)
    col = lax.broadcasted_iota(jnp.int32, (size, size), 1)
    place = (col == 2 * (row % 128) + row // 128).astype(BF)
    for r in range(2):
        for t in range(3):
            lane = r * ROW + t * 128
            pair = jnp.concatenate(
                [x_ref[:, lane : lane + 128], x_ref[:, lane + COLS : lane + COLS + 128]], axis=1
            )
            hi, mid, low = split3(pair)
            woven = mm(hi, place) + (mm(mid, place) + mm(low, place))
            out_ref[0, :, r, t * size : (t + 1) * size] = woven


def weave(x):
    return call(weave_kernel, [sds((1, CH, 2, ROW), F32)], [x], name="weave")[0]


FLOW_ROWS = 704
GROUP = 88


def merge_kernel(*refs):
    out_ref, total = refs[-2:]
    for k in range(2):
        own_in, own_out, got_in, got_out, small = refs[5 * k : 5 * k + 5]
        at = k * FLOW_ROWS
        total[at : at + IN_HALF] = own_in[...] + got_in[...]
        for a in range(3):
            start = at + IN_HALF + a * TAP_HALF
            total[start : start + TAP_HALF] = own_out[a] + got_out[a]
        start = at + FLOW_ROWS - HALF
        total[start : start + HALF, :256] = small[:HALF]
        total[start : start + HALF, 256:] = small[HALF:]
    for g in range(2 * FLOW_ROWS // GROUP):
        for lane in range(4):
            out_ref[4 * g + lane] = total[
                g * GROUP : (g + 1) * GROUP, lane * 128 : (lane + 1) * 128
            ].astype(BF)


def merge(first, second):
    shares = 2 * FLOW_ROWS // GROUP * 4
    return call(
        merge_kernel,
        [sds((shares, GROUP, 128), BF)],
        [*first, *second],
        scratch=[pltpu.VMEM((2 * FLOW_ROWS, HID), F32)],
        name="merge",
    )[0]


def total_kernel(cells, shares_ref, out_ref):
    total = shares_ref[0].astype(F32)
    for s in range(1, shares_ref.shape[0]):
        total += shares_ref[s].astype(F32)
    mean = (total * (1.0 / cells)).astype(BF)
    for s in range(shares_ref.shape[0]):
        out_ref[s] = mean


def totals(shares, cells):
    return call(
        functools.partial(total_kernel, cells), [sds(shares.shape, BF)], [shares], name="totals"
    )[0]


def half_copies(half, k, rows, win_ref, wout_ref, sems):
    at = k * FLOW_ROWS
    count = IN_HALF if half == 0 else 9 * HALF - IN_HALF
    pairs = [(at, count, win_ref.at[k, pl.ds(half * IN_HALF, count), :])]
    for a in range(3):
        start = at + IN_HALF + a * TAP_HALF
        if half == 0:
            pairs.append((start, CH, wout_ref.at[k, 3 * a + 2]))
            pairs.append((start + CH, HALF, wout_ref.at[k, 3 * a + 1, pl.ds(0, HALF), :]))
        else:
            pairs.append((start, HALF, wout_ref.at[k, 3 * a + 1, pl.ds(HALF, HALF), :]))
            pairs.append((start + HALF, CH, wout_ref.at[k, 3 * a]))
    return [
        pltpu.make_async_copy(rows.at[pl.ds(first, size), :], target, sems.at[7 * k + i])
        for i, (first, size, target) in enumerate(pairs)
    ]


def put_half(half_now, shares_ref, rows, win_ref, wout_ref, sems):
    groups = FLOW_ROWS // GROUP
    for k in range(2):
        for g in range(k * groups, (k + 1) * groups):
            for lane in range(4):
                rows[g * GROUP : (g + 1) * GROUP, lane * 128 : (lane + 1) * 128] = shares_ref[
                    4 * g + lane
                ].astype(F32)
        for half in range(2):

            @pl.when(half_now == half)
            def _():
                for copy in half_copies(half, k, rows, win_ref, wout_ref, sems):
                    copy.start()


def wait_half(half_now, rows, win_ref, wout_ref, sems):
    for half in range(2):

        @pl.when(half_now == half)
        def _():
            for k in range(2):
                for copy in half_copies(half, k, rows, win_ref, wout_ref, sems):
                    copy.wait()


def unpack_own_kernel(core_ref, mine_ref, win_ref, wout_ref, rows, sems):
    put_half(core_ref[0], mine_ref, rows, win_ref, wout_ref, sems)
    wait_half(core_ref[0], rows, win_ref, wout_ref, sems)


def unpack_other_kernel(
    core_ref, mine_ref, other_ref, _win, _wout, win_ref, wout_ref, mix_ref, bin_ref, bout_ref,
    rows, sems,
):
    put_half(1 - core_ref[0], other_ref, rows, win_ref, wout_ref, sems)
    groups = FLOW_ROWS // GROUP
    for k in range(2):
        last = 4 * ((k + 1) * groups - 1)
        parts = [
            mine_ref[last + lane][GROUP - HALF :].astype(F32)
            + other_ref[last + lane][GROUP - HALF :].astype(F32)
            for lane in range(4)
        ]
        mix_ref[k, :HALF] = parts[0][:, :CH]
        mix_ref[k, HALF:] = parts[2][:, :CH]
        bout_ref[k : k + 1, :] = parts[1][:1, :CH]
        row = 9 * HALF - IN_HALF
        share, row = 4 * (k * groups + row // GROUP), row % GROUP
        for lane in range(4):
            mine = mine_ref[share + lane].astype(F32)[row : row + 1]
            other = other_ref[share + lane].astype(F32)[row : row + 1]
            bin_ref[k : k + 1, lane * 128 : (lane + 1) * 128] = jnp.where(
                core_ref[0] == 1, mine, other
            )
    wait_half(1 - core_ref[0], rows, win_ref, wout_ref, sems)


KERNEL_GRADS = [((2, 9 * HALF, HID), F32), ((2, 9, CH, HID), F32)]


def unpack_own(core, mine):
    return call(
        unpack_own_kernel,
        [sds(*x) for x in KERNEL_GRADS],
        [core, mine],
        scratch=[pltpu.VMEM((2 * FLOW_ROWS, HID), F32), pltpu.SemaphoreType.DMA((14,))],
        smem=(0,),
        hbm_outs=(0, 1),
        name="unpack_own",
    )


def unpack_other(core, mine, other, win, wout):
    return call(
        unpack_other_kernel,
        [sds(*x) for x in KERNEL_GRADS]
        + [sds((2, CH, CH), F32), sds((2, HID), F32), sds((2, CH), F32)],
        [core, mine, other, win, wout],
        scratch=[pltpu.VMEM((2 * FLOW_ROWS, HID), F32), pltpu.SemaphoreType.DMA((14,))],
        smem=(0,),
        hbm=(3, 4),
        hbm_outs=(0, 1),
        alias={3: 0, 4: 1},
        name="unpack_other",
    )


def after(x, *others):
    return lax.optimization_barrier((x, *others))[0]


def local(passed_on, passed_grad, latent, mix_factors, in_kernel, in_bias, out_kernel, out_bias):
    lat_index = lax.axis_index(LAT)
    lat_count = lax.axis_size(LAT)
    forth = [(i, (i + 1) % lat_count) for i in range(lat_count)]
    back = [(t, s) for s, t in forth]
    swap = [(0, 1), (1, 0)]
    flags = jnp.stack([lat_index > 0, lat_index < lat_count - 1]).astype(F32)
    core = lax.axis_index("c").astype(jnp.int32).reshape(1)

    block = payload(
        jnp.transpose(passed_on[0], (1, 2, 0)), jnp.transpose(passed_grad[0], (1, 2, 0))
    )
    recv = lax.all_to_all(block, LAT, 0, 0, tiled=True)
    inv, lut, w1t, w2t, w2k, w1k, b2c = prep(mix_factors, in_kernel, out_kernel, in_bias, out_bias)
    w1 = in_kernel.reshape(2, 9 * HALF, HID)
    yb = latent.reshape(HALF, CELLS)

    above, mid, below, ya, ga = turn(recv)
    x1, rows1, slope1, next_mid, grad1, moved1 = forward(
        flags, above, mid, below, w1t[1], w2k[1], b2c[1], inv[1], ya, yb, True
    )
    above0 = lax.ppermute(next_mid, LAT, forth)
    below0 = lax.ppermute(next_mid, LAT, back)
    top1 = lax.ppermute(grad1, LAT, forth)
    bottom1 = lax.ppermute(grad1, LAT, back)
    keep_out1, give_out1, bias1 = out_weight(core, grad1, rows1)
    x0, rows0, slope0, scale0 = forward(
        after(flags, keep_out1), above0, next_mid, below0, w1t[0], w2k[0], b2c[0], inv[0],
        x1[:HALF], x1[HALF:], False,
    )
    got_out1 = lax.ppermute(give_out1, "c", swap)
    gpre1, in1 = backward(after(flags, x0), top1, grad1, bottom1, w2t[1], slope1, w1k[1])
    gx1, small1, grad0, moved0 = close(
        in1, ga, moved1, lut[1], x1, mix_factors, 1, bias1, scale0
    )
    top0 = lax.ppermute(grad0, LAT, forth)
    bottom0 = lax.ppermute(grad0, LAT, back)
    keep_in1, give_in1 = in_weight(after(core, grad0), flags, above, mid, below, gpre1)
    got_in1 = lax.ppermute(give_in1, "c", swap)
    keep_out0, give_out0, bias0 = out_weight(after(core, keep_in1), grad0, rows0)
    rebuilt = weave(after(x0, keep_out0))
    gpre0, in0 = backward(after(flags, rebuilt), top0, grad0, bottom0, w2t[0], slope0, w1k[0])
    got_out0 = lax.ppermute(give_out0, "c", swap)
    keep_in0, give_in0 = in_weight(after(core, in0), flags, above0, next_mid, below0, gpre0)
    got_in0 = lax.ppermute(give_in0, "c", swap)
    gx0, small0 = close(
        after(in0, keep_in0), gx1, moved0, lut[0], x0, mix_factors, 0, bias0
    )

    packed = merge(
        (keep_in0, keep_out0, got_in0, got_out0, small0),
        (keep_in1, keep_out1, got_in1, got_out1, small1),
    )
    shares = lax.all_to_all(packed, CHIPS, 0, 0, tiled=True)
    cells = float(CELLS * lat_count * lax.axis_size(ENS))
    spread = totals(shares, cells)
    mine = lax.all_to_all(spread, CHIPS, 0, 0, tiled=True)
    other = lax.ppermute(mine, "c", swap)
    win, wout = unpack_own(core, mine)
    input_grad = weave(after(gx0, mine))
    in_grad, out_grad, mix_grad, in_bias_grad, out_bias_grad = unpack_other(
        core, mine, other, win, wout
    )
    return (
        rebuilt,
        input_grad,
        mix_grad,
        in_grad.reshape(2, 9, HALF, HID),
        in_bias_grad,
        out_grad,
        out_bias_grad,
    )


def solution(mesh):
    split = Mesh(mesh.devices.reshape(4, 2, 2, 4, 2), ("y", "xl", "c", "z", "xh"))
    return jax.shard_map(
        local,
        mesh=split,
        in_specs=(
            P(ENS, None, None, LAT),
            P(ENS, None, None, LAT),
            P(ENS, None, LAT, None),
            P(),
            P(),
            P(),
            P(),
            P(),
        ),
        out_specs=(P(ENS, None, LAT, None), P(ENS, None, LAT, None), P(), P(), P(), P(), P()),
        check_vma=False,
    )
```

```python
import functools

import jax
import jax.numpy as jnp
from jax import lax
from jax.experimental import pallas as pl
from jax.experimental.pallas import tpu as pltpu
from jax.sharding import Mesh, PartitionSpec as P

BF = jnp.bfloat16
F32 = jnp.float32
HIGH = lax.Precision.HIGHEST
LAT = ("y", "xl", "c")
ENS = ("z", "xh")
CHIPS = ("y", "xl", "z", "xh")
HALF = 48
CH = 96
HID = 512
COLS = 384
ROW = 768
CELLS = 1536
IN_ROWS = 448
IN_HALF = 224
TAP_HALF = 144
MIB = 1024 * 1024


def mm(a, b):
    return lax.dot_general(a, b, (((1,), (0,)), ((), ())), preferred_element_type=F32)


def mm_nt(a, b):
    return lax.dot_general(a, b, (((1,), (1,)), ((), ())), preferred_element_type=F32)


def mm_high(a, b):
    return lax.dot_general(
        a, b, (((1,), (0,)), ((), ())), preferred_element_type=F32, precision=HIGH
    )


def split3(x):
    hi = x.astype(BF)
    rest = x - hi.astype(F32)
    mid = rest.astype(BF)
    low = (rest - mid.astype(F32)).astype(BF)
    return hi, mid, low


def from_left(x):
    lane = lax.broadcasted_iota(jnp.int32, x.shape, 1)
    return jnp.where(lane == 0, 0.0, pltpu.roll(x, 1, 1))


def from_right(x):
    width = x.shape[1]
    lane = lax.broadcasted_iota(jnp.int32, x.shape, 1)
    return jnp.where(lane == width - 1, 0.0, pltpu.roll(x, width - 1, 1))


def sds(shape, dtype):
    return jax.ShapeDtypeStruct(shape, dtype)


def call(
    body, outs, ins, scratch=(), smem=(), hbm=(), hbm_outs=(), alias=None, flops=0, name=None, limit=16
):
    moved = sum(x.size * x.dtype.itemsize for x in list(ins) + list(outs))
    return pl.pallas_call(
        body,
        out_shape=outs,
        in_specs=[
            pl.BlockSpec(
                memory_space=pltpu.SMEM if i in smem else pltpu.HBM if i in hbm else pltpu.VMEM
            )
            for i in range(len(ins))
        ],
        out_specs=[
            pl.BlockSpec(memory_space=pltpu.HBM if i in hbm_outs else pltpu.VMEM)
            for i in range(len(outs))
        ],
        scratch_shapes=list(scratch),
        input_output_aliases=alias or {},
        compiler_params=pltpu.CompilerParams(vmem_limit_bytes=limit * MIB),
        cost_estimate=pl.CostEstimate(flops=flops, bytes_accessed=moved, transcendentals=0),
        name=name,
    )(*ins)


def payload_kernel(on_ref, grad_ref, out_ref):
    width = on_ref.shape[2]
    blank = jnp.zeros(on_ref.shape[1:], BF)
    for s in range(on_ref.shape[0]):
        on = on_ref[s]
        hi = on.astype(BF)
        grad = grad_ref[s]
        out_ref[s, :, :width] = hi
        out_ref[s, :, width : 2 * width] = (on - hi.astype(F32)).astype(BF)
        if s + 1 < on_ref.shape[0]:
            out_ref[s + 1, :, 2 * width : 3 * width] = hi
        if s > 0:
            out_ref[s - 1, :, 3 * width : 4 * width] = hi
        out_ref[s, :, 4 * width :] = grad.astype(BF)
    out_ref[0, :, 2 * width : 3 * width] = blank
    out_ref[on_ref.shape[0] - 1, :, 3 * width : 4 * width] = blank


def payload(on, grad):
    bands, width, channels = on.shape
    return call(
        payload_kernel, [sds((bands, width, 5 * channels), BF)], [on, grad], name="payload", limit=56
    )[0]


def prep_kernel(
    mix_ref, w1_ref, w2_ref, b1_ref, b2_ref, *refs
):
    stage1, stage2 = refs[-2:]
    flows = mix_ref.shape[0]
    row = lax.broadcasted_iota(jnp.int32, (CH, CH), 0)
    col = lax.broadcasted_iota(jnp.int32, (CH, CH), 1)
    eye = (row == col).astype(F32)
    near = (row // 16) == (col // 16)
    units = []
    for k in range(flows):
        mix = mix_ref[k]
        units.append(jnp.where(row > col, mix, 0.0))
        units.append(jnp.where(row < col, mix, 0.0))
    inner = [jnp.where(near, u, 0.0) for u in units]
    outer = [u - i for u, i in zip(units, inner)]
    power = inner
    blocks = [eye - n for n in inner]
    for _ in range(3):
        power = [mm_high(p, p) for p in power]
        blocks = [mm_high(b, eye + p) for b, p in zip(blocks, power)]
    power = [mm_high(b, o) for b, o in zip(blocks, outer)]
    whole = [eye - p for p in power]
    for _ in range(2):
        power = [mm_high(p, p) for p in power]
        whole = [mm_high(w, eye + p) for w, p in zip(whole, power)]
    inverses = [mm_high(w, b) for w, b in zip(whole, blocks)]
    for k in range(flows):
        inv_ref, lut_ref, w1t_ref, w2t_ref, w2k_ref, w1k_ref, b2c_ref = refs[7 * k : 7 * k + 7]
        inv_ref[...] = mm_high(inverses[2 * k + 1], inverses[2 * k])
        lut_ref[...] = mm_high(units[2 * k] + eye, units[2 * k + 1] + eye).T
        for tap in range(9):
            stage1[tap * HALF : (tap + 1) * HALF, :] = 0.5 * w1_ref[k, tap].astype(F32)
            stage2[tap * CH : (tap + 1) * CH, :] = 0.5 * w2_ref[k, 8 - tap].astype(F32)
        hi, mid, low = split3(0.5 * b1_ref[k : k + 1, :])
        stage1[9 * HALF :, :] = jnp.zeros((IN_ROWS - 9 * HALF, HID), F32)
        for i, part in enumerate((hi, mid, low)):
            stage1[9 * HALF + i : 9 * HALF + i + 1, :] = part.astype(F32)
        w1t_ref[...] = stage1[...].T.astype(BF)
        w2t_ref[...] = stage2[...].T.astype(BF)
        for a in range(3):
            for b in range(3):
                w2k_ref[b * CH : (b + 1) * CH, a * HID : (a + 1) * HID] = w2_ref[k, 3 * a + b]
                w1k_ref[b * HALF : (b + 1) * HALF, a * HID : (a + 1) * HID] = w1_ref[
                    k, 3 * (2 - a) + b
                ]
        b2c_ref[...] = jnp.broadcast_to(b2_ref[k : k + 1, :], (8, CH)).T


def prep(mix_factors, in_kernel, out_kernel, in_bias, out_bias):
    flows = mix_factors.shape[0]
    outs = call(
        prep_kernel,
        [
            sds((CH, CH), F32),
            sds((CH, CH), F32),
            sds((HID, IN_ROWS), BF),
            sds((HID, 9 * CH), BF),
            sds((3 * CH, 3 * HID), BF),
            sds((3 * HALF, 3 * HID), BF),
            sds((CH, 8), F32),
        ]
        * flows,
        [mix_factors, in_kernel, out_kernel, in_bias, out_bias],
        scratch=[pltpu.VMEM((IN_ROWS, HID), F32), pltpu.VMEM((9 * CH, HID), F32)],
        name="prep",
        limit=56,
    )
    return [outs[i::7] for i in range(7)]


def turn_kernel(recv_ref, above_ref, mid_ref, below_ref, ya_ref, ga_ref, stage):
    width = 2 * CH
    row = lax.broadcasted_iota(jnp.int32, (width, width), 0)
    col = lax.broadcasted_iota(jnp.int32, (width, width), 1)
    pick = (col == 4 * (row % HALF) + row // HALF).astype(BF)
    none = jnp.zeros((width, width), BF)
    first = jnp.concatenate([pick, none], axis=1)
    second = jnp.concatenate([none, pick], axis=1)
    both = jnp.concatenate([pick, pick], axis=1)
    sources, count = recv_ref.shape[0], recv_ref.shape[1]
    for s in range(sources):
        stage[s * count : (s + 1) * count, :] = recv_ref[s].astype(F32)
    pair = stage[:, : 2 * width].astype(BF)
    kept = mm_nt(both, pair)
    mid_ref[...] = mm_nt(first, pair).astype(BF)
    pair = stage[:, 2 * width : 4 * width].astype(BF)
    above_ref[...] = mm_nt(first, pair).astype(BF)
    below_ref[...] = mm_nt(second, pair).astype(BF)
    grad = mm_nt(pick, stage[:, 4 * width :].astype(BF))
    for k in range(4):
        ya_ref[:, k * COLS : (k + 1) * COLS] = kept[k * HALF : (k + 1) * HALF]
        ga_ref[:, k * COLS : (k + 1) * COLS] = grad[k * HALF : (k + 1) * HALF]


def turn(recv):
    return call(
        turn_kernel,
        [sds((2 * CH, COLS), BF)] * 3 + [sds((HALF, CELLS), F32)] * 2,
        [recv],
        scratch=[pltpu.VMEM((COLS, recv.shape[2]), F32)],
        flops=4 * 10**9,
        name="turn",
    )


def stack_planes(even, odd, factor=None):
    if factor is not None:
        even = (even.astype(F32) * factor).astype(BF)
        odd = (odd.astype(F32) * factor).astype(BF)
    left = from_left(odd.astype(F32)).astype(BF)
    right = from_right(even.astype(F32)).astype(BF)
    return jnp.concatenate([left, even, odd, right], axis=0)


def fill_input_columns(flags_ref, above_ref, mid_ref, below_ref, columns, first, count):
    refs = {-2: (above_ref, 0), -1: (above_ref, CH), 0: (mid_ref, 0)}
    refs.update({1: (mid_ref, CH), 2: (below_ref, 0), 3: (below_ref, CH)})
    for source in range(first - 1, first + count + 1):
        ref, at = refs[source]
        factor = flags_ref[0] if source < 0 else flags_ref[1] if source > 1 else None
        stacked = stack_planes(ref[at : at + HALF], ref[at + HALF : at + CH], factor)
        for a in range(3):
            target = source - a + 1 - first
            if 0 <= target < count:
                for p in range(2):
                    lane = (2 * target + p) * COLS
                    columns[a * 144 : (a + 1) * 144, lane : lane + COLS] = stacked[
                        p * HALF : p * HALF + 144
                    ]
    extra = IN_ROWS - 9 * HALF
    row = lax.broadcasted_iota(jnp.int32, (extra, count * ROW), 0)
    columns[9 * HALF :, :] = jnp.where(row < 3, 1.0, 0.0).astype(BF)


def fill_grad_columns(flags_ref, above_ref, mid_ref, below_ref, columns):
    for source in range(-2, 4):
        ref = above_ref if source < 0 else below_ref if source > 1 else mid_ref
        factor = flags_ref[0] if source < 0 else flags_ref[1] if source > 1 else None
        at = (source % 2) * 2 * CH
        stacked = stack_planes(ref[at : at + CH], ref[at + CH : at + 2 * CH], factor)
        for a in range(3):
            target = source - a + 2
            if 0 <= target < 4:
                for p in range(2):
                    lane = (2 * target + p) * COLS
                    columns[a * 288 : (a + 1) * 288, lane : lane + COLS] = stacked[
                        p * CH : p * CH + 288
                    ]


def put_out_grad(raw, moved, out_ref):
    for r in range(2):
        for p in range(2):
            lane = (2 * r + p) * COLS
            at = (2 * r + p) * CH
            out_ref[at : at + HALF] = raw[:, lane : lane + COLS].astype(BF)
            out_ref[at + HALF : at + CH] = moved[:, lane : lane + COLS].astype(BF)


def forward_kernel(with_grad, flags_ref, *refs):
    above_ref, mid_ref, below_ref, w1t_ref, w2k_ref, b2_ref, inv_ref, ya_ref, yb_ref = refs[:9]
    columns, pre, outs = refs[-3:]
    if with_grad:
        x_ref, rows, slope_ref, next_ref, grad_ref, moved_ref = refs[9:-3]
    else:
        x_ref, rows, slope_ref, scale_ref = refs[9:-3]
    fill_input_columns(flags_ref, above_ref, mid_ref, below_ref, columns, -1, 4)
    for h in range(4):
        pre[h % 2] = mm(w1t_ref[...], columns[:, h * ROW : (h + 1) * ROW])
        inside = flags_ref[0] if h == 0 else flags_ref[1] if h == 3 else None

        def activate(step, carry):
            at = pl.multiple_of(step * 16, 16)
            half = pre[h % 2, pl.ds(at, 16), :]
            bent = jnp.tanh(half)
            more = 1.0 + bent
            hidden = half * more
            slope = more * (1.0 + half * (1.0 - bent))
            if inside is not None:
                hidden = hidden * inside
                slope = slope * inside
            rows[pl.ds(h * HID + at, 16), :] = hidden.astype(BF)
            slope_ref[pl.ds(h * HID + at, 16), :] = slope
            return carry

        lax.fori_loop(0, HID // 16, activate, 0, unroll=True)
    for r in range(2):
        taps = mm(w2k_ref[...], rows[r * HID : (r + 3) * HID, :])
        even, odd = taps[:, :COLS], taps[:, COLS:]
        lane = 2 * r * COLS
        outs[:, lane : lane + COLS] = from_left(odd[:CH]) + even[CH : 2 * CH] + odd[2 * CH :]
        outs[:, lane + COLS : lane + ROW] = even[:CH] + odd[CH : 2 * CH] + from_right(even[2 * CH :])
    raw = outs[:HALF] + b2_ref[:HALF, :1]
    shift = outs[HALF:] + b2_ref[HALF:, :1]
    inverse = 1.0 + jnp.exp(-(raw + 2.0))
    scale = 1.0 / inverse
    moved_in = yb_ref[...] * inverse - shift
    x = mm_high(inv_ref[...], jnp.concatenate([ya_ref[...], moved_in], axis=0))
    x_ref[...] = x
    if with_grad:
        moved_grad = yb_ref[...]
        moved = moved_grad * scale
        moved_ref[...] = moved
        put_out_grad((moved_grad * yb_ref[...] - 1.0) * (1.0 - scale), moved, grad_ref)
        for k in range(4):
            next_ref[k * HALF : (k + 1) * HALF] = x[:HALF, k * COLS : (k + 1) * COLS].astype(BF)
    else:
        scale_ref[...] = scale


def forward(flags, above, mid, below, w1t, w2k, b2c, inv, ya, yb, with_grad):
    outs = [sds((CH, CELLS), F32), sds((4 * HID, ROW), BF), sds((4 * HID, ROW), F32)]
    if with_grad:
        outs += [
            sds((2 * CH, COLS), BF),
            sds((4 * CH, COLS), BF),
            sds((HALF, CELLS), F32),
        ]
    else:
        outs += [sds((HALF, CELLS), F32)]
    return call(
        functools.partial(forward_kernel, with_grad),
        outs,
        [flags, above, mid, below, w1t, w2k, b2c, inv, ya, yb],
        scratch=[
            pltpu.VMEM((IN_ROWS, 4 * ROW), BF),
            pltpu.VMEM((2, HID, ROW), F32),
            pltpu.VMEM((CH, CELLS), F32),
        ],
        smem=(0,),
        limit=24,
        flops=4 * 10**9,
        name="forward",
    )


def backward_kernel(
    flags_ref, above_ref, mid_ref, below_ref, w2t_ref, slope_ref, w1k_ref, gpre_ref, in_ref,
    columns, hid_grad,
):
    fill_grad_columns(flags_ref, above_ref, mid_ref, below_ref, columns)
    for h in range(4):
        hid_grad[h % 2] = mm(w2t_ref[...], columns[:, h * ROW : (h + 1) * ROW])

        def slope(step, carry):
            at = pl.multiple_of(step * 16, 16)
            gpre_ref[pl.ds(h * HID + at, 16), :] = (
                hid_grad[h % 2, pl.ds(at, 16), :] * slope_ref[pl.ds(h * HID + at, 16), :]
            ).astype(BF)
            return carry

        lax.fori_loop(0, HID // 16, slope, 0, unroll=True)
    b0, b1, b2 = slice(0, HALF), slice(HALF, CH), slice(CH, 3 * HALF)
    for r in range(2):
        taps = mm(w1k_ref[...], gpre_ref[r * HID : (r + 3) * HID, :])
        even, odd = taps[:, :COLS], taps[:, COLS:]
        in_ref[r * CH : r * CH + HALF] = odd[b0] + even[b1] + from_left(odd[b2])
        in_ref[r * CH + HALF : (r + 1) * CH] = from_right(even[b0]) + odd[b1] + even[b2]


def backward(flags, above, mid, below, w2t, slope, w1k):
    return call(
        backward_kernel,
        [sds((4 * HID, ROW), BF), sds((2 * CH, COLS), F32)],
        [flags, above, mid, below, w2t, slope, w1k],
        scratch=[pltpu.VMEM((9 * CH, 4 * ROW), BF), pltpu.VMEM((2, HID, ROW), F32)],
        smem=(0,),
        flops=6 * 10**9,
        limit=20,
        name="backward",
    )


def out_weight_kernel(core_ref, grad_ref, rows_ref, keep_ref, give_ref, bias_ref, left, right, whole):
    for r in range(2):
        at = 2 * r * CH
        stacked = stack_planes(grad_ref[at : at + CH], grad_ref[at + CH : at + 2 * CH])
        left[r] = stacked[: 3 * CH]
        right[r] = stacked[CH:]
    part = [jnp.concatenate([left[r], right[r]], axis=1) for r in range(2)]
    for a in range(3):
        whole[...] = mm_nt(part[0], rows_ref[a * HID : (a + 1) * HID]) + mm_nt(
            part[1], rows_ref[(a + 1) * HID : (a + 2) * HID]
        )
        for ref, core in ((keep_ref, core_ref[0]), (give_ref, 1 - core_ref[0])):
            ref[a] = whole[pl.ds(pl.multiple_of(core * TAP_HALF, 8), TAP_HALF), :]
    ones = jnp.ones((8, COLS), BF)
    total = mm_nt(ones, grad_ref[:CH]) + mm_nt(ones, grad_ref[CH : 2 * CH])
    bias_ref[...] = total + (
        mm_nt(ones, grad_ref[2 * CH : 3 * CH]) + mm_nt(ones, grad_ref[3 * CH :])
    )


def out_weight(core, grad, rows):
    return call(
        out_weight_kernel,
        [sds((3, TAP_HALF, HID), F32), sds((3, TAP_HALF, HID), F32), sds((8, CH), F32)],
        [core, grad, rows],
        scratch=[
            pltpu.VMEM((2, 3 * CH, COLS), BF),
            pltpu.VMEM((2, 3 * CH, COLS), BF),
            pltpu.VMEM((3 * CH, HID), F32),
        ],
        smem=(0,),
        flops=2 * 10**9,
        name="out_weight",
    )


def in_weight_kernel(
    core_ref, flags_ref, above_ref, mid_ref, below_ref, gpre_ref, keep_ref, give_ref, columns,
    whole,
):
    fill_input_columns(flags_ref, above_ref, mid_ref, below_ref, columns, 0, 2)
    whole[...] = mm_nt(columns[:, :ROW], gpre_ref[HID : 2 * HID]) + mm_nt(
        columns[:, ROW:], gpre_ref[2 * HID : 3 * HID]
    )
    for ref, core in ((keep_ref, core_ref[0]), (give_ref, 1 - core_ref[0])):
        ref[...] = whole[pl.ds(pl.multiple_of(core * IN_HALF, 8), IN_HALF), :]


def in_weight(core, flags, above, mid, below, gpre):
    return call(
        in_weight_kernel,
        [sds((IN_HALF, HID), F32), sds((IN_HALF, HID), F32)],
        [core, flags, above, mid, below, gpre],
        scratch=[pltpu.VMEM((IN_ROWS, CELLS), BF), pltpu.VMEM((IN_ROWS, HID), F32)],
        smem=(0, 1),
        flops=10**9,
        name="in_weight",
    )


def close_kernel(next_step, flow, *refs):
    in_ref, ga_ref, moved_ref, lut_ref, x_ref, mix_ref, bias_ref = refs[:7]
    whole = refs[-1]
    if next_step:
        scale_ref, gx_ref, small, grad_ref, nmoved_ref = refs[7:-1]
    else:
        gx_ref, small = refs[7:-1]
    for k in range(4):
        lane = k * COLS
        whole[:HALF, lane : lane + COLS] = (
            ga_ref[:HALF, lane : lane + COLS] + in_ref[k * HALF : (k + 1) * HALF]
        )
    whole[HALF:] = moved_ref[...]
    gx = mm_high(lut_ref[...], whole[...])
    gx_ref[...] = gx
    if next_step:
        scale = scale_ref[...]
        moved_grad = gx[HALF:]
        moved = moved_grad * scale
        nmoved_ref[...] = moved
        put_out_grad((moved_grad * x_ref[HALF:] - 1.0) * (1.0 - scale), moved, grad_ref)
    ghi, gmid, _ = split3(whole[...])
    xhi, xmid, _ = split3(x_ref[...])
    outer = mm_nt(ghi, xhi) + (mm_nt(ghi, xmid) + mm_nt(gmid, xhi))
    row = lax.broadcasted_iota(jnp.int32, (CH, CH), 0)
    col = lax.broadcasted_iota(jnp.int32, (CH, CH), 1)
    eye = (row == col).astype(F32)
    mix = mix_ref[flow]
    lower = jnp.where(row > col, mix, 0.0) + eye
    upper = jnp.where(row < col, mix, 0.0) + eye
    by_upper = mm_high(outer, upper.T)
    by_lower = mm_high(lower.T, outer)
    small[:, :CH] = jnp.where(row > col, by_upper, jnp.where(row < col, by_lower, 0.0))
    small[:, CH:] = jnp.zeros((CH, 2 * 128 - CH), F32)
    small[:8, 128 : 128 + CH] = bias_ref[...]


def close(gin, ga, moved, lut, x, mix, flow, bias, scale=None):
    outs = [sds((CH, CELLS), F32), sds((CH, 256), F32)]
    ins = [gin, ga, moved, lut, x, mix, bias]
    if scale is not None:
        outs += [sds((4 * CH, COLS), BF), sds((HALF, CELLS), F32)]
        ins += [scale]
    return call(
        functools.partial(close_kernel, scale is not None, flow),
        outs,
        ins,
        scratch=[pltpu.VMEM((CH, CELLS), F32)],
        flops=10**9,
        name="close",
    )


def weave_kernel(x_ref, out_ref):
    size = 256
    row = lax.broadcasted_iota(jnp.int32, (size, size), 0)
    col = lax.broadcasted_iota(jnp.int32, (size, size), 1)
    place = (col == 2 * (row % 128) + row // 128).astype(BF)
    for r in range(2):
        for t in range(3):
            lane = r * ROW + t * 128
            pair = jnp.concatenate(
                [x_ref[:, lane : lane + 128], x_ref[:, lane + COLS : lane + COLS + 128]], axis=1
            )
            hi, mid, low = split3(pair)
            woven = mm(hi, place) + (mm(mid, place) + mm(low, place))
            out_ref[0, :, r, t * size : (t + 1) * size] = woven


def weave(x):
    return call(weave_kernel, [sds((1, CH, 2, ROW), F32)], [x], name="weave")[0]


FLOW_ROWS = 704
GROUP = 88


def merge_kernel(*refs):
    out_ref, total = refs[-2:]
    for k in range(2):
        own_in, own_out, got_in, got_out, small = refs[5 * k : 5 * k + 5]
        at = k * FLOW_ROWS
        total[at : at + IN_HALF] = own_in[...] + got_in[...]
        for a in range(3):
            start = at + IN_HALF + a * TAP_HALF
            total[start : start + TAP_HALF] = own_out[a] + got_out[a]
        start = at + FLOW_ROWS - HALF
        total[start : start + HALF, :256] = small[:HALF]
        total[start : start + HALF, 256:] = small[HALF:]
    for g in range(2 * FLOW_ROWS // GROUP):
        for lane in range(4):
            out_ref[4 * g + lane] = total[
                g * GROUP : (g + 1) * GROUP, lane * 128 : (lane + 1) * 128
            ].astype(BF)


def merge(first, second):
    shares = 2 * FLOW_ROWS // GROUP * 4
    return call(
        merge_kernel,
        [sds((shares, GROUP, 128), BF)],
        [*first, *second],
        scratch=[pltpu.VMEM((2 * FLOW_ROWS, HID), F32)],
        name="merge",
    )[0]


def total_kernel(cells, shares_ref, out_ref):
    total = shares_ref[0].astype(F32)
    for s in range(1, shares_ref.shape[0]):
        total += shares_ref[s].astype(F32)
    mean = (total * (1.0 / cells)).astype(BF)
    for s in range(shares_ref.shape[0]):
        out_ref[s] = mean


def totals(shares, cells):
    return call(
        functools.partial(total_kernel, cells), [sds(shares.shape, BF)], [shares], name="totals"
    )[0]


def half_copies(half, k, rows, win_ref, wout_ref, sems):
    at = k * FLOW_ROWS
    count = IN_HALF if half == 0 else 9 * HALF - IN_HALF
    pairs = [(at, count, win_ref.at[k, pl.ds(half * IN_HALF, count), :])]
    for a in range(3):
        start = at + IN_HALF + a * TAP_HALF
        if half == 0:
            pairs.append((start, CH, wout_ref.at[k, 3 * a + 2]))
            pairs.append((start + CH, HALF, wout_ref.at[k, 3 * a + 1, pl.ds(0, HALF), :]))
        else:
            pairs.append((start, HALF, wout_ref.at[k, 3 * a + 1, pl.ds(HALF, HALF), :]))
            pairs.append((start + HALF, CH, wout_ref.at[k, 3 * a]))
    return [
        pltpu.make_async_copy(rows.at[pl.ds(first, size), :], target, sems.at[7 * k + i])
        for i, (first, size, target) in enumerate(pairs)
    ]


def put_half(half_now, shares_ref, rows, win_ref, wout_ref, sems):
    groups = FLOW_ROWS // GROUP
    for k in range(2):
        for g in range(k * groups, (k + 1) * groups):
            for lane in range(4):
                rows[g * GROUP : (g + 1) * GROUP, lane * 128 : (lane + 1) * 128] = shares_ref[
                    4 * g + lane
                ].astype(F32)
        for half in range(2):

            @pl.when(half_now == half)
            def _():
                for copy in half_copies(half, k, rows, win_ref, wout_ref, sems):
                    copy.start()


def wait_half(half_now, rows, win_ref, wout_ref, sems):
    for half in range(2):

        @pl.when(half_now == half)
        def _():
            for k in range(2):
                for copy in half_copies(half, k, rows, win_ref, wout_ref, sems):
                    copy.wait()


def unpack_own_kernel(core_ref, mine_ref, win_ref, wout_ref, rows, sems):
    put_half(core_ref[0], mine_ref, rows, win_ref, wout_ref, sems)
    wait_half(core_ref[0], rows, win_ref, wout_ref, sems)


def unpack_other_kernel(
    core_ref, mine_ref, other_ref, _win, _wout, win_ref, wout_ref, mix_ref, bin_ref, bout_ref,
    rows, sems,
):
    put_half(1 - core_ref[0], other_ref, rows, win_ref, wout_ref, sems)
    groups = FLOW_ROWS // GROUP
    for k in range(2):
        last = 4 * ((k + 1) * groups - 1)
        parts = [
            mine_ref[last + lane].astype(F32)[GROUP - HALF :]
            + other_ref[last + lane].astype(F32)[GROUP - HALF :]
            for lane in range(4)
        ]
        mix_ref[k, :HALF] = parts[0][:, :CH]
        mix_ref[k, HALF:] = parts[2][:, :CH]
        bout_ref[k : k + 1, :] = parts[1][:1, :CH]
        row = 9 * HALF - IN_HALF
        share, row = 4 * (k * groups + row // GROUP), row % GROUP
        for lane in range(4):
            mine = mine_ref[share + lane].astype(F32)[row : row + 1]
            other = other_ref[share + lane].astype(F32)[row : row + 1]
            bin_ref[k : k + 1, lane * 128 : (lane + 1) * 128] = jnp.where(
                core_ref[0] == 1, mine, other
            )
    wait_half(1 - core_ref[0], rows, win_ref, wout_ref, sems)


KERNEL_GRADS = [((2, 9 * HALF, HID), F32), ((2, 9, CH, HID), F32)]


def unpack_own(core, mine):
    return call(
        unpack_own_kernel,
        [sds(*x) for x in KERNEL_GRADS],
        [core, mine],
        scratch=[pltpu.VMEM((2 * FLOW_ROWS, HID), F32), pltpu.SemaphoreType.DMA((14,))],
        smem=(0,),
        hbm_outs=(0, 1),
        name="unpack_own",
    )


def unpack_other(core, mine, other, win, wout):
    return call(
        unpack_other_kernel,
        [sds(*x) for x in KERNEL_GRADS]
        + [sds((2, CH, CH), F32), sds((2, HID), F32), sds((2, CH), F32)],
        [core, mine, other, win, wout],
        scratch=[pltpu.VMEM((2 * FLOW_ROWS, HID), F32), pltpu.SemaphoreType.DMA((14,))],
        smem=(0,),
        hbm=(3, 4),
        hbm_outs=(0, 1),
        alias={3: 0, 4: 1},
        name="unpack_other",
    )


def after(x, *others):
    return lax.optimization_barrier((x, *others))[0]


def local(passed_on, passed_grad, latent, mix_factors, in_kernel, in_bias, out_kernel, out_bias):
    lat_index = lax.axis_index(LAT)
    lat_count = lax.axis_size(LAT)
    forth = [(i, (i + 1) % lat_count) for i in range(lat_count)]
    back = [(t, s) for s, t in forth]
    swap = [(0, 1), (1, 0)]
    flags = jnp.stack([lat_index > 0, lat_index < lat_count - 1]).astype(F32)
    core = lax.axis_index("c").astype(jnp.int32).reshape(1)

    block = payload(
        jnp.transpose(passed_on[0], (1, 2, 0)), jnp.transpose(passed_grad[0], (1, 2, 0))
    )
    recv = lax.all_to_all(block, LAT, 0, 0, tiled=True)
    inv, lut, w1t, w2t, w2k, w1k, b2c = prep(mix_factors, in_kernel, out_kernel, in_bias, out_bias)
    w1 = in_kernel.reshape(2, 9 * HALF, HID)
    yb = latent.reshape(HALF, CELLS)

    above, mid, below, ya, ga = turn(recv)
    x1, rows1, slope1, next_mid, grad1, moved1 = forward(
        flags, above, mid, below, w1t[1], w2k[1], b2c[1], inv[1], ya, yb, True
    )
    above0 = lax.ppermute(next_mid, LAT, forth)
    below0 = lax.ppermute(next_mid, LAT, back)
    top1 = lax.ppermute(grad1, LAT, forth)
    bottom1 = lax.ppermute(grad1, LAT, back)
    keep_out1, give_out1, bias1 = out_weight(core, grad1, rows1)
    x0, rows0, slope0, scale0 = forward(
        after(flags, keep_out1), above0, next_mid, below0, w1t[0], w2k[0], b2c[0], inv[0],
        x1[:HALF], x1[HALF:], False,
    )
    got_out1 = lax.ppermute(give_out1, "c", swap)
    gpre1, in1 = backward(after(flags, x0), top1, grad1, bottom1, w2t[1], slope1, w1k[1])
    gx1, small1, grad0, moved0 = close(
        in1, ga, moved1, lut[1], x1, mix_factors, 1, bias1, scale0
    )
    top0 = lax.ppermute(grad0, LAT, forth)
    bottom0 = lax.ppermute(grad0, LAT, back)
    keep_in1, give_in1 = in_weight(after(core, grad0), flags, above, mid, below, gpre1)
    got_in1 = lax.ppermute(give_in1, "c", swap)
    keep_out0, give_out0, bias0 = out_weight(after(core, keep_in1), grad0, rows0)
    rebuilt = weave(after(x0, keep_out0))
    gpre0, in0 = backward(after(flags, rebuilt), top0, grad0, bottom0, w2t[0], slope0, w1k[0])
    got_out0 = lax.ppermute(give_out0, "c", swap)
    keep_in0, give_in0 = in_weight(after(core, in0), flags, above0, next_mid, below0, gpre0)
    got_in0 = lax.ppermute(give_in0, "c", swap)
    gx0, small0 = close(
        after(in0, keep_in0), gx1, moved0, lut[0], x0, mix_factors, 0, bias0
    )

    packed = merge(
        (keep_in0, keep_out0, got_in0, got_out0, small0),
        (keep_in1, keep_out1, got_in1, got_out1, small1),
    )
    shares = lax.all_to_all(packed, CHIPS, 0, 0, tiled=True)
    cells = float(CELLS * lat_count * lax.axis_size(ENS))
    spread = totals(shares, cells)
    mine = lax.all_to_all(spread, CHIPS, 0, 0, tiled=True)
    other = lax.ppermute(mine, "c", swap)
    win, wout = unpack_own(core, mine)
    input_grad = weave(after(gx0, mine))
    in_grad, out_grad, mix_grad, in_bias_grad, out_bias_grad = unpack_other(
        core, mine, other, win, wout
    )
    return (
        rebuilt,
        input_grad,
        mix_grad,
        in_grad.reshape(2, 9, HALF, HID),
        in_bias_grad,
        out_grad,
        out_bias_grad,
    )


def solution(mesh):
    split = Mesh(mesh.devices.reshape(4, 2, 2, 4, 2), ("y", "xl", "c", "z", "xh"))
    return jax.shard_map(
        local,
        mesh=split,
        in_specs=(
            P(ENS, None, None, LAT),
            P(ENS, None, None, LAT),
            P(ENS, None, LAT, None),
            P(),
            P(),
            P(),
            P(),
            P(),
        ),
        out_specs=(P(ENS, None, LAT, None), P(ENS, None, LAT, None), P(), P(), P(), P(), P()),
        check_vma=False,
    )
```

```python
import functools

import jax
import jax.numpy as jnp
from jax import lax
from jax.experimental import pallas as pl
from jax.experimental.pallas import tpu as pltpu
from jax.sharding import Mesh, PartitionSpec as P

BF = jnp.bfloat16
F32 = jnp.float32
HIGH = lax.Precision.HIGHEST
LAT = ("y", "xl", "c")
ENS = ("z", "xh")
CHIPS = ("y", "xl", "z", "xh")
HALF = 48
CH = 96
HID = 512
COLS = 384
ROW = 768
CELLS = 1536
IN_ROWS = 448
IN_HALF = 224
TAP_HALF = 144
MIB = 1024 * 1024


def mm(a, b):
    return lax.dot_general(a, b, (((1,), (0,)), ((), ())), preferred_element_type=F32)


def mm_nt(a, b):
    return lax.dot_general(a, b, (((1,), (1,)), ((), ())), preferred_element_type=F32)


def mm_high(a, b):
    return lax.dot_general(
        a, b, (((1,), (0,)), ((), ())), preferred_element_type=F32, precision=HIGH
    )


def split3(x):
    hi = x.astype(BF)
    rest = x - hi.astype(F32)
    mid = rest.astype(BF)
    low = (rest - mid.astype(F32)).astype(BF)
    return hi, mid, low


def stack_left(m):
    hi, mid, low = split3(m)
    return jnp.concatenate([hi, hi, mid, hi, low, mid], axis=1)


def mm_six(left, x):
    hi, mid, low = split3(x)
    return mm(left, jnp.concatenate([hi, mid, hi, low, hi, mid], axis=0))


def from_left(x):
    lane = lax.broadcasted_iota(jnp.int32, x.shape, 1)
    return jnp.where(lane == 0, 0.0, pltpu.roll(x, 1, 1))


def from_right(x):
    width = x.shape[1]
    lane = lax.broadcasted_iota(jnp.int32, x.shape, 1)
    return jnp.where(lane == width - 1, 0.0, pltpu.roll(x, width - 1, 1))


def sds(shape, dtype):
    return jax.ShapeDtypeStruct(shape, dtype)


def call(
    body, outs, ins, scratch=(), smem=(), hbm=(), hbm_outs=(), alias=None, flops=0, name=None, limit=16
):
    moved = sum(x.size * x.dtype.itemsize for x in list(ins) + list(outs))
    return pl.pallas_call(
        body,
        out_shape=outs,
        in_specs=[
            pl.BlockSpec(
                memory_space=pltpu.SMEM if i in smem else pltpu.HBM if i in hbm else pltpu.VMEM
            )
            for i in range(len(ins))
        ],
        out_specs=[
            pl.BlockSpec(memory_space=pltpu.HBM if i in hbm_outs else pltpu.VMEM)
            for i in range(len(outs))
        ],
        scratch_shapes=list(scratch),
        input_output_aliases=alias or {},
        compiler_params=pltpu.CompilerParams(vmem_limit_bytes=limit * MIB),
        cost_estimate=pl.CostEstimate(flops=flops, bytes_accessed=moved, transcendentals=0),
        name=name,
    )(*ins)


def payload_kernel(on_ref, grad_ref, out_ref):
    width = on_ref.shape[2]
    blank = jnp.zeros(on_ref.shape[1:], BF)
    for s in range(on_ref.shape[0]):
        on = on_ref[s]
        hi = on.astype(BF)
        grad = grad_ref[s]
        out_ref[s, :, :width] = hi
        out_ref[s, :, width : 2 * width] = (on - hi.astype(F32)).astype(BF)
        if s + 1 < on_ref.shape[0]:
            out_ref[s + 1, :, 2 * width : 3 * width] = hi
        if s > 0:
            out_ref[s - 1, :, 3 * width : 4 * width] = hi
        out_ref[s, :, 4 * width :] = grad.astype(BF)
    out_ref[0, :, 2 * width : 3 * width] = blank
    out_ref[on_ref.shape[0] - 1, :, 3 * width : 4 * width] = blank


def payload(on, grad):
    bands, width, channels = on.shape
    return call(
        payload_kernel, [sds((bands, width, 5 * channels), BF)], [on, grad], name="payload", limit=56
    )[0]


def prep_kernel(
    mix_ref, w1_ref, w2_ref, b1_ref, b2_ref, *refs
):
    stage1, stage2 = refs[-2:]
    flows = mix_ref.shape[0]
    row = lax.broadcasted_iota(jnp.int32, (CH, CH), 0)
    col = lax.broadcasted_iota(jnp.int32, (CH, CH), 1)
    eye = (row == col).astype(F32)
    near = (row // 16) == (col // 16)
    units = []
    for k in range(flows):
        mix = mix_ref[k]
        units.append(jnp.where(row > col, mix, 0.0))
        units.append(jnp.where(row < col, mix, 0.0))
    inner = [jnp.where(near, u, 0.0) for u in units]
    outer = [u - i for u, i in zip(units, inner)]
    power = inner
    blocks = [eye - n for n in inner]
    for _ in range(3):
        power = [mm_high(p, p) for p in power]
        blocks = [mm_high(b, eye + p) for b, p in zip(blocks, power)]
    power = [mm_high(b, o) for b, o in zip(blocks, outer)]
    whole = [eye - p for p in power]
    for _ in range(2):
        power = [mm_high(p, p) for p in power]
        whole = [mm_high(w, eye + p) for w, p in zip(whole, power)]
    inverses = [mm_high(w, b) for w, b in zip(whole, blocks)]
    for k in range(flows):
        inv_ref, lut_ref, w1t_ref, w2t_ref, w2k_ref, w1k_ref, b2c_ref = refs[7 * k : 7 * k + 7]
        inv_ref[...] = stack_left(mm_high(inverses[2 * k + 1], inverses[2 * k]))
        lut_ref[...] = stack_left(mm_high(units[2 * k] + eye, units[2 * k + 1] + eye).T)
        for tap in range(9):
            stage1[tap * HALF : (tap + 1) * HALF, :] = 0.5 * w1_ref[k, tap].astype(F32)
            stage2[tap * CH : (tap + 1) * CH, :] = 0.5 * w2_ref[k, 8 - tap].astype(F32)
        hi, mid, low = split3(0.5 * b1_ref[k : k + 1, :])
        stage1[9 * HALF :, :] = jnp.zeros((IN_ROWS - 9 * HALF, HID), F32)
        for i, part in enumerate((hi, mid, low)):
            stage1[9 * HALF + i : 9 * HALF + i + 1, :] = part.astype(F32)
        w1t_ref[...] = stage1[...].T.astype(BF)
        w2t_ref[...] = stage2[...].T.astype(BF)
        for a in range(3):
            for b in range(3):
                w2k_ref[b * CH : (b + 1) * CH, a * HID : (a + 1) * HID] = w2_ref[k, 3 * a + b]
                w1k_ref[b * HALF : (b + 1) * HALF, a * HID : (a + 1) * HID] = w1_ref[
                    k, 3 * (2 - a) + b
                ]
        b2c_ref[...] = jnp.broadcast_to(b2_ref[k : k + 1, :], (8, CH)).T


def prep(mix_factors, in_kernel, out_kernel, in_bias, out_bias):
    flows = mix_factors.shape[0]
    outs = call(
        prep_kernel,
        [
            sds((CH, 6 * CH), BF),
            sds((CH, 6 * CH), BF),
            sds((HID, IN_ROWS), BF),
            sds((HID, 9 * CH), BF),
            sds((3 * CH, 3 * HID), BF),
            sds((3 * HALF, 3 * HID), BF),
            sds((CH, 8), F32),
        ]
        * flows,
        [mix_factors, in_kernel, out_kernel, in_bias, out_bias],
        scratch=[pltpu.VMEM((IN_ROWS, HID), F32), pltpu.VMEM((9 * CH, HID), F32)],
        name="prep",
        limit=56,
    )
    return [outs[i::7] for i in range(7)]


def turn_kernel(recv_ref, above_ref, mid_ref, below_ref, ya_ref, ga_ref, stage):
    width = 2 * CH
    row = lax.broadcasted_iota(jnp.int32, (width, width), 0)
    col = lax.broadcasted_iota(jnp.int32, (width, width), 1)
    pick = (col == 4 * (row % HALF) + row // HALF).astype(BF)
    none = jnp.zeros((width, width), BF)
    first = jnp.concatenate([pick, none], axis=1)
    second = jnp.concatenate([none, pick], axis=1)
    both = jnp.concatenate([pick, pick], axis=1)
    sources, count = recv_ref.shape[0], recv_ref.shape[1]
    for s in range(sources):
        stage[s * count : (s + 1) * count, :] = recv_ref[s].astype(F32)
    pair = stage[:, : 2 * width].astype(BF)
    kept = mm_nt(both, pair)
    mid_ref[...] = mm_nt(first, pair).astype(BF)
    pair = stage[:, 2 * width : 4 * width].astype(BF)
    above_ref[...] = mm_nt(first, pair).astype(BF)
    below_ref[...] = mm_nt(second, pair).astype(BF)
    grad = mm_nt(pick, stage[:, 4 * width :].astype(BF))
    for k in range(4):
        ya_ref[:, k * COLS : (k + 1) * COLS] = kept[k * HALF : (k + 1) * HALF]
        ga_ref[:, k * COLS : (k + 1) * COLS] = grad[k * HALF : (k + 1) * HALF]


def turn(recv):
    return call(
        turn_kernel,
        [sds((2 * CH, COLS), BF)] * 3 + [sds((HALF, CELLS), F32)] * 2,
        [recv],
        scratch=[pltpu.VMEM((COLS, recv.shape[2]), F32)],
        flops=4 * 10**9,
        name="turn",
    )


def stack_planes(even, odd, factor=None):
    if factor is not None:
        even = (even.astype(F32) * factor).astype(BF)
        odd = (odd.astype(F32) * factor).astype(BF)
    left = from_left(odd.astype(F32)).astype(BF)
    right = from_right(even.astype(F32)).astype(BF)
    return jnp.concatenate([left, even, odd, right], axis=0)


def fill_input_columns(flags_ref, above_ref, mid_ref, below_ref, columns, first, count):
    refs = {-2: (above_ref, 0), -1: (above_ref, CH), 0: (mid_ref, 0)}
    refs.update({1: (mid_ref, CH), 2: (below_ref, 0), 3: (below_ref, CH)})
    for source in range(first - 1, first + count + 1):
        ref, at = refs[source]
        factor = flags_ref[0] if source < 0 else flags_ref[1] if source > 1 else None
        stacked = stack_planes(ref[at : at + HALF], ref[at + HALF : at + CH], factor)
        for a in range(3):
            target = source - a + 1 - first
            if 0 <= target < count:
                for p in range(2):
                    lane = (2 * target + p) * COLS
                    columns[a * 144 : (a + 1) * 144, lane : lane + COLS] = stacked[
                        p * HALF : p * HALF + 144
                    ]
    extra = IN_ROWS - 9 * HALF
    row = lax.broadcasted_iota(jnp.int32, (extra, count * ROW), 0)
    columns[9 * HALF :, :] = jnp.where(row < 3, 1.0, 0.0).astype(BF)


def fill_grad_columns(flags_ref, above_ref, mid_ref, below_ref, columns):
    for source in range(-2, 4):
        ref = above_ref if source < 0 else below_ref if source > 1 else mid_ref
        factor = flags_ref[0] if source < 0 else flags_ref[1] if source > 1 else None
        at = (source % 2) * 2 * CH
        stacked = stack_planes(ref[at : at + CH], ref[at + CH : at + 2 * CH], factor)
        for a in range(3):
            target = source - a + 2
            if 0 <= target < 4:
                for p in range(2):
                    lane = (2 * target + p) * COLS
                    columns[a * 288 : (a + 1) * 288, lane : lane + COLS] = stacked[
                        p * CH : p * CH + 288
                    ]


def put_out_grad(raw, moved, out_ref):
    for r in range(2):
        for p in range(2):
            lane = (2 * r + p) * COLS
            at = (2 * r + p) * CH
            out_ref[at : at + HALF] = raw[:, lane : lane + COLS].astype(BF)
            out_ref[at + HALF : at + CH] = moved[:, lane : lane + COLS].astype(BF)


def forward_kernel(with_grad, flags_ref, *refs):
    above_ref, mid_ref, below_ref, w1t_ref, w2k_ref, b2_ref, inv_ref, ya_ref, yb_ref = refs[:9]
    columns, pre, outs = refs[-3:]
    if with_grad:
        x_ref, rows, slope_ref, next_ref, grad_ref, moved_ref = refs[9:-3]
    else:
        x_ref, rows, slope_ref, scale_ref = refs[9:-3]
    fill_input_columns(flags_ref, above_ref, mid_ref, below_ref, columns, -1, 4)
    for h in range(4):
        pre[h % 2] = mm(w1t_ref[...], columns[:, h * ROW : (h + 1) * ROW])
        inside = flags_ref[0] if h == 0 else flags_ref[1] if h == 3 else None

        def activate(step, carry):
            at = pl.multiple_of(step * 16, 16)
            half = pre[h % 2, pl.ds(at, 16), :]
            bent = jnp.tanh(half)
            more = 1.0 + bent
            hidden = half * more
            slope = more * (1.0 + half * (1.0 - bent))
            if inside is not None:
                hidden = hidden * inside
                slope = slope * inside
            rows[pl.ds(h * HID + at, 16), :] = hidden.astype(BF)
            slope_ref[pl.ds(h * HID + at, 16), :] = slope
            return carry

        lax.fori_loop(0, HID // 16, activate, 0, unroll=True)
    for r in range(2):
        taps = mm(w2k_ref[...], rows[r * HID : (r + 3) * HID, :])
        even, odd = taps[:, :COLS], taps[:, COLS:]
        lane = 2 * r * COLS
        outs[:, lane : lane + COLS] = from_left(odd[:CH]) + even[CH : 2 * CH] + odd[2 * CH :]
        outs[:, lane + COLS : lane + ROW] = even[:CH] + odd[CH : 2 * CH] + from_right(even[2 * CH :])
    raw = outs[:HALF] + b2_ref[:HALF, :1]
    shift = outs[HALF:] + b2_ref[HALF:, :1]
    inverse = 1.0 + jnp.exp(-(raw + 2.0))
    scale = 1.0 / inverse
    moved_in = yb_ref[...] * inverse - shift
    x = mm_six(inv_ref[...], jnp.concatenate([ya_ref[...], moved_in], axis=0))
    x_ref[...] = x
    if with_grad:
        moved_grad = yb_ref[...]
        moved = moved_grad * scale
        moved_ref[...] = moved
        put_out_grad((moved_grad * yb_ref[...] - 1.0) * (1.0 - scale), moved, grad_ref)
        for k in range(4):
            next_ref[k * HALF : (k + 1) * HALF] = x[:HALF, k * COLS : (k + 1) * COLS].astype(BF)
    else:
        scale_ref[...] = scale


def forward(flags, above, mid, below, w1t, w2k, b2c, inv, ya, yb, with_grad):
    outs = [sds((CH, CELLS), F32), sds((4 * HID, ROW), BF), sds((4 * HID, ROW), F32)]
    if with_grad:
        outs += [
            sds((2 * CH, COLS), BF),
            sds((4 * CH, COLS), BF),
            sds((HALF, CELLS), F32),
        ]
    else:
        outs += [sds((HALF, CELLS), F32)]
    return call(
        functools.partial(forward_kernel, with_grad),
        outs,
        [flags, above, mid, below, w1t, w2k, b2c, inv, ya, yb],
        scratch=[
            pltpu.VMEM((IN_ROWS, 4 * ROW), BF),
            pltpu.VMEM((2, HID, ROW), F32),
            pltpu.VMEM((CH, CELLS), F32),
        ],
        smem=(0,),
        limit=24,
        flops=4 * 10**9,
        name="forward",
    )


def backward_kernel(
    flags_ref, above_ref, mid_ref, below_ref, w2t_ref, slope_ref, w1k_ref, gpre_ref, in_ref,
    columns, hid_grad,
):
    fill_grad_columns(flags_ref, above_ref, mid_ref, below_ref, columns)
    for h in range(4):
        hid_grad[h % 2] = mm(w2t_ref[...], columns[:, h * ROW : (h + 1) * ROW])

        def slope(step, carry):
            at = pl.multiple_of(step * 16, 16)
            gpre_ref[pl.ds(h * HID + at, 16), :] = (
                hid_grad[h % 2, pl.ds(at, 16), :] * slope_ref[pl.ds(h * HID + at, 16), :]
            ).astype(BF)
            return carry

        lax.fori_loop(0, HID // 16, slope, 0, unroll=True)
    b0, b1, b2 = slice(0, HALF), slice(HALF, CH), slice(CH, 3 * HALF)
    for r in range(2):
        taps = mm(w1k_ref[...], gpre_ref[r * HID : (r + 3) * HID, :])
        even, odd = taps[:, :COLS], taps[:, COLS:]
        in_ref[r * CH : r * CH + HALF] = odd[b0] + even[b1] + from_left(odd[b2])
        in_ref[r * CH + HALF : (r + 1) * CH] = from_right(even[b0]) + odd[b1] + even[b2]


def backward(flags, above, mid, below, w2t, slope, w1k):
    return call(
        backward_kernel,
        [sds((4 * HID, ROW), BF), sds((2 * CH, COLS), F32)],
        [flags, above, mid, below, w2t, slope, w1k],
        scratch=[pltpu.VMEM((9 * CH, 4 * ROW), BF), pltpu.VMEM((2, HID, ROW), F32)],
        smem=(0,),
        flops=6 * 10**9,
        limit=20,
        name="backward",
    )


def out_weight_kernel(core_ref, grad_ref, rows_ref, keep_ref, give_ref, bias_ref, left, right, whole):
    for r in range(2):
        at = 2 * r * CH
        stacked = stack_planes(grad_ref[at : at + CH], grad_ref[at + CH : at + 2 * CH])
        left[r] = stacked[: 3 * CH]
        right[r] = stacked[CH:]
    part = [jnp.concatenate([left[r], right[r]], axis=1) for r in range(2)]
    for a in range(3):
        whole[...] = mm_nt(part[0], rows_ref[a * HID : (a + 1) * HID]) + mm_nt(
            part[1], rows_ref[(a + 1) * HID : (a + 2) * HID]
        )
        for ref, core in ((keep_ref, core_ref[0]), (give_ref, 1 - core_ref[0])):
            ref[a] = whole[pl.ds(pl.multiple_of(core * TAP_HALF, 8), TAP_HALF), :]
    ones = jnp.ones((8, COLS), BF)
    total = mm_nt(ones, grad_ref[:CH]) + mm_nt(ones, grad_ref[CH : 2 * CH])
    bias_ref[...] = total + (
        mm_nt(ones, grad_ref[2 * CH : 3 * CH]) + mm_nt(ones, grad_ref[3 * CH :])
    )


def out_weight(core, grad, rows):
    return call(
        out_weight_kernel,
        [sds((3, TAP_HALF, HID), F32), sds((3, TAP_HALF, HID), F32), sds((8, CH), F32)],
        [core, grad, rows],
        scratch=[
            pltpu.VMEM((2, 3 * CH, COLS), BF),
            pltpu.VMEM((2, 3 * CH, COLS), BF),
            pltpu.VMEM((3 * CH, HID), F32),
        ],
        smem=(0,),
        flops=2 * 10**9,
        name="out_weight",
    )


def in_weight_kernel(
    core_ref, flags_ref, above_ref, mid_ref, below_ref, gpre_ref, keep_ref, give_ref, columns,
    whole,
):
    fill_input_columns(flags_ref, above_ref, mid_ref, below_ref, columns, 0, 2)
    whole[...] = mm_nt(columns[:, :ROW], gpre_ref[HID : 2 * HID]) + mm_nt(
        columns[:, ROW:], gpre_ref[2 * HID : 3 * HID]
    )
    for ref, core in ((keep_ref, core_ref[0]), (give_ref, 1 - core_ref[0])):
        ref[...] = whole[pl.ds(pl.multiple_of(core * IN_HALF, 8), IN_HALF), :]


def in_weight(core, flags, above, mid, below, gpre):
    return call(
        in_weight_kernel,
        [sds((IN_HALF, HID), F32), sds((IN_HALF, HID), F32)],
        [core, flags, above, mid, below, gpre],
        scratch=[pltpu.VMEM((IN_ROWS, CELLS), BF), pltpu.VMEM((IN_ROWS, HID), F32)],
        smem=(0, 1),
        flops=10**9,
        name="in_weight",
    )


def close_kernel(next_step, flow, *refs):
    in_ref, ga_ref, moved_ref, lut_ref, x_ref, mix_ref, bias_ref = refs[:7]
    whole = refs[-1]
    if next_step:
        scale_ref, gx_ref, small, grad_ref, nmoved_ref = refs[7:-1]
    else:
        gx_ref, small = refs[7:-1]
    for k in range(4):
        lane = k * COLS
        whole[:HALF, lane : lane + COLS] = (
            ga_ref[:HALF, lane : lane + COLS] + in_ref[k * HALF : (k + 1) * HALF]
        )
    whole[HALF:] = moved_ref[...]
    gx = mm_six(lut_ref[...], whole[...])
    gx_ref[...] = gx
    if next_step:
        scale = scale_ref[...]
        moved_grad = gx[HALF:]
        moved = moved_grad * scale
        nmoved_ref[...] = moved
        put_out_grad((moved_grad * x_ref[HALF:] - 1.0) * (1.0 - scale), moved, grad_ref)
    ghi, gmid, _ = split3(whole[...])
    xhi, xmid, _ = split3(x_ref[...])
    four = mm_nt(
        jnp.concatenate([ghi, gmid], axis=0), jnp.concatenate([xhi, xmid], axis=0)
    )
    outer = four[:CH, :CH] + (four[:CH, CH:] + four[CH:, :CH])
    row = lax.broadcasted_iota(jnp.int32, (CH, CH), 0)
    col = lax.broadcasted_iota(jnp.int32, (CH, CH), 1)
    eye = (row == col).astype(F32)
    mix = mix_ref[flow]
    lower = jnp.where(row > col, mix, 0.0) + eye
    upper = jnp.where(row < col, mix, 0.0) + eye
    by_upper = mm_high(outer, upper.T)
    by_lower = mm_high(lower.T, outer)
    small[:, :CH] = jnp.where(row > col, by_upper, jnp.where(row < col, by_lower, 0.0))
    small[:, CH:] = jnp.zeros((CH, 2 * 128 - CH), F32)
    small[:8, 128 : 128 + CH] = bias_ref[...]


def close(gin, ga, moved, lut, x, mix, flow, bias, scale=None):
    outs = [sds((CH, CELLS), F32), sds((CH, 256), F32)]
    ins = [gin, ga, moved, lut, x, mix, bias]
    if scale is not None:
        outs += [sds((4 * CH, COLS), BF), sds((HALF, CELLS), F32)]
        ins += [scale]
    return call(
        functools.partial(close_kernel, scale is not None, flow),
        outs,
        ins,
        scratch=[pltpu.VMEM((CH, CELLS), F32)],
        flops=10**9,
        name="close",
    )


def weave_kernel(x_ref, out_ref):
    size = 256
    row = lax.broadcasted_iota(jnp.int32, (size, size), 0)
    col = lax.broadcasted_iota(jnp.int32, (size, size), 1)
    place = (col == 2 * (row % 128) + row // 128).astype(BF)
    for r in range(2):
        for t in range(3):
            lane = r * ROW + t * 128
            pair = jnp.concatenate(
                [x_ref[:, lane : lane + 128], x_ref[:, lane + COLS : lane + COLS + 128]], axis=1
            )
            hi, mid, low = split3(pair)
            woven = mm(hi, place) + (mm(mid, place) + mm(low, place))
            out_ref[0, :, r, t * size : (t + 1) * size] = woven


def weave(x):
    return call(weave_kernel, [sds((1, CH, 2, ROW), F32)], [x], name="weave")[0]


FLOW_ROWS = 704
GROUP = 88


def merge_kernel(*refs):
    out_ref, total = refs[-2:]
    for k in range(2):
        own_in, own_out, got_in, got_out, small = refs[5 * k : 5 * k + 5]
        at = k * FLOW_ROWS
        total[at : at + IN_HALF] = own_in[...] + got_in[...]
        for a in range(3):
            start = at + IN_HALF + a * TAP_HALF
            total[start : start + TAP_HALF] = own_out[a] + got_out[a]
        start = at + FLOW_ROWS - HALF
        total[start : start + HALF, :256] = small[:HALF]
        total[start : start + HALF, 256:] = small[HALF:]
    for g in range(2 * FLOW_ROWS // GROUP):
        for lane in range(4):
            out_ref[4 * g + lane] = total[
                g * GROUP : (g + 1) * GROUP, lane * 128 : (lane + 1) * 128
            ].astype(BF)


def merge(first, second):
    shares = 2 * FLOW_ROWS // GROUP * 4
    return call(
        merge_kernel,
        [sds((shares, GROUP, 128), BF)],
        [*first, *second],
        scratch=[pltpu.VMEM((2 * FLOW_ROWS, HID), F32)],
        name="merge",
    )[0]


def total_kernel(cells, shares_ref, out_ref):
    total = shares_ref[0].astype(F32)
    for s in range(1, shares_ref.shape[0]):
        total += shares_ref[s].astype(F32)
    mean = (total * (1.0 / cells)).astype(BF)
    for s in range(shares_ref.shape[0]):
        out_ref[s] = mean


def totals(shares, cells):
    return call(
        functools.partial(total_kernel, cells), [sds(shares.shape, BF)], [shares], name="totals"
    )[0]


def half_copies(half, k, rows, win_ref, wout_ref, sems):
    at = k * FLOW_ROWS
    count = IN_HALF if half == 0 else 9 * HALF - IN_HALF
    pairs = [(at, count, win_ref.at[k, pl.ds(half * IN_HALF, count), :])]
    for a in range(3):
        start = at + IN_HALF + a * TAP_HALF
        if half == 0:
            pairs.append((start, CH, wout_ref.at[k, 3 * a + 2]))
            pairs.append((start + CH, HALF, wout_ref.at[k, 3 * a + 1, pl.ds(0, HALF), :]))
        else:
            pairs.append((start, HALF, wout_ref.at[k, 3 * a + 1, pl.ds(HALF, HALF), :]))
            pairs.append((start + HALF, CH, wout_ref.at[k, 3 * a]))
    return [
        pltpu.make_async_copy(rows.at[pl.ds(first, size), :], target, sems.at[7 * k + i])
        for i, (first, size, target) in enumerate(pairs)
    ]


def put_half(half_now, shares_ref, rows, win_ref, wout_ref, sems):
    groups = FLOW_ROWS // GROUP
    for k in range(2):
        for g in range(k * groups, (k + 1) * groups):
            for lane in range(4):
                rows[g * GROUP : (g + 1) * GROUP, lane * 128 : (lane + 1) * 128] = shares_ref[
                    4 * g + lane
                ].astype(F32)
        for half in range(2):

            @pl.when(half_now == half)
            def _():
                for copy in half_copies(half, k, rows, win_ref, wout_ref, sems):
                    copy.start()


def wait_half(half_now, rows, win_ref, wout_ref, sems):
    for half in range(2):

        @pl.when(half_now == half)
        def _():
            for k in range(2):
                for copy in half_copies(half, k, rows, win_ref, wout_ref, sems):
                    copy.wait()


def unpack_own_kernel(core_ref, mine_ref, win_ref, wout_ref, rows, sems):
    put_half(core_ref[0], mine_ref, rows, win_ref, wout_ref, sems)
    wait_half(core_ref[0], rows, win_ref, wout_ref, sems)


def unpack_other_kernel(
    core_ref, mine_ref, other_ref, _win, _wout, win_ref, wout_ref, mix_ref, bin_ref, bout_ref,
    rows, sems,
):
    put_half(1 - core_ref[0], other_ref, rows, win_ref, wout_ref, sems)
    groups = FLOW_ROWS // GROUP
    for k in range(2):
        last = 4 * ((k + 1) * groups - 1)
        parts = [
            mine_ref[last + lane].astype(F32)[GROUP - HALF :]
            + other_ref[last + lane].astype(F32)[GROUP - HALF :]
            for lane in range(4)
        ]
        mix_ref[k, :HALF] = parts[0][:, :CH]
        mix_ref[k, HALF:] = parts[2][:, :CH]
        bout_ref[k : k + 1, :] = parts[1][:1, :CH]
        row = 9 * HALF - IN_HALF
        share, row = 4 * (k * groups + row // GROUP), row % GROUP
        for lane in range(4):
            mine = mine_ref[share + lane].astype(F32)[row : row + 1]
            other = other_ref[share + lane].astype(F32)[row : row + 1]
            bin_ref[k : k + 1, lane * 128 : (lane + 1) * 128] = jnp.where(
                core_ref[0] == 1, mine, other
            )
    wait_half(1 - core_ref[0], rows, win_ref, wout_ref, sems)


KERNEL_GRADS = [((2, 9 * HALF, HID), F32), ((2, 9, CH, HID), F32)]


def unpack_own(core, mine):
    return call(
        unpack_own_kernel,
        [sds(*x) for x in KERNEL_GRADS],
        [core, mine],
        scratch=[pltpu.VMEM((2 * FLOW_ROWS, HID), F32), pltpu.SemaphoreType.DMA((14,))],
        smem=(0,),
        hbm_outs=(0, 1),
        name="unpack_own",
    )


def unpack_other(core, mine, other, win, wout):
    return call(
        unpack_other_kernel,
        [sds(*x) for x in KERNEL_GRADS]
        + [sds((2, CH, CH), F32), sds((2, HID), F32), sds((2, CH), F32)],
        [core, mine, other, win, wout],
        scratch=[pltpu.VMEM((2 * FLOW_ROWS, HID), F32), pltpu.SemaphoreType.DMA((14,))],
        smem=(0,),
        hbm=(3, 4),
        hbm_outs=(0, 1),
        alias={3: 0, 4: 1},
        name="unpack_other",
    )


def after(x, *others):
    return lax.optimization_barrier((x, *others))[0]


def local(passed_on, passed_grad, latent, mix_factors, in_kernel, in_bias, out_kernel, out_bias):
    lat_index = lax.axis_index(LAT)
    lat_count = lax.axis_size(LAT)
    forth = [(i, (i + 1) % lat_count) for i in range(lat_count)]
    back = [(t, s) for s, t in forth]
    swap = [(0, 1), (1, 0)]
    flags = jnp.stack([lat_index > 0, lat_index < lat_count - 1]).astype(F32)
    core = lax.axis_index("c").astype(jnp.int32).reshape(1)

    block = payload(
        jnp.transpose(passed_on[0], (1, 2, 0)), jnp.transpose(passed_grad[0], (1, 2, 0))
    )
    recv = lax.all_to_all(block, LAT, 0, 0, tiled=True)
    inv, lut, w1t, w2t, w2k, w1k, b2c = prep(mix_factors, in_kernel, out_kernel, in_bias, out_bias)
    w1 = in_kernel.reshape(2, 9 * HALF, HID)
    yb = latent.reshape(HALF, CELLS)

    above, mid, below, ya, ga = turn(recv)
    x1, rows1, slope1, next_mid, grad1, moved1 = forward(
        flags, above, mid, below, w1t[1], w2k[1], b2c[1], inv[1], ya, yb, True
    )
    above0 = lax.ppermute(next_mid, LAT, forth)
    below0 = lax.ppermute(next_mid, LAT, back)
    top1 = lax.ppermute(grad1, LAT, forth)
    bottom1 = lax.ppermute(grad1, LAT, back)
    keep_out1, give_out1, bias1 = out_weight(core, grad1, rows1)
    x0, rows0, slope0, scale0 = forward(
        after(flags, keep_out1), above0, next_mid, below0, w1t[0], w2k[0], b2c[0], inv[0],
        x1[:HALF], x1[HALF:], False,
    )
    got_out1 = lax.ppermute(give_out1, "c", swap)
    gpre1, in1 = backward(after(flags, x0), top1, grad1, bottom1, w2t[1], slope1, w1k[1])
    gx1, small1, grad0, moved0 = close(
        in1, ga, moved1, lut[1], x1, mix_factors, 1, bias1, scale0
    )
    top0 = lax.ppermute(grad0, LAT, forth)
    bottom0 = lax.ppermute(grad0, LAT, back)
    keep_in1, give_in1 = in_weight(after(core, grad0), flags, above, mid, below, gpre1)
    got_in1 = lax.ppermute(give_in1, "c", swap)
    keep_out0, give_out0, bias0 = out_weight(after(core, keep_in1), grad0, rows0)
    rebuilt = weave(after(x0, keep_out0))
    gpre0, in0 = backward(after(flags, rebuilt), top0, grad0, bottom0, w2t[0], slope0, w1k[0])
    got_out0 = lax.ppermute(give_out0, "c", swap)
    keep_in0, give_in0 = in_weight(after(core, in0), flags, above0, next_mid, below0, gpre0)
    got_in0 = lax.ppermute(give_in0, "c", swap)
    gx0, small0 = close(
        after(in0, keep_in0), gx1, moved0, lut[0], x0, mix_factors, 0, bias0
    )

    packed = merge(
        (keep_in0, keep_out0, got_in0, got_out0, small0),
        (keep_in1, keep_out1, got_in1, got_out1, small1),
    )
    shares = lax.all_to_all(packed, CHIPS, 0, 0, tiled=True)
    cells = float(CELLS * lat_count * lax.axis_size(ENS))
    spread = totals(shares, cells)
    mine = lax.all_to_all(spread, CHIPS, 0, 0, tiled=True)
    other = lax.ppermute(mine, "c", swap)
    win, wout = unpack_own(core, mine)
    input_grad = weave(after(gx0, mine))
    in_grad, out_grad, mix_grad, in_bias_grad, out_bias_grad = unpack_other(
        core, mine, other, win, wout
    )
    return (
        rebuilt,
        input_grad,
        mix_grad,
        in_grad.reshape(2, 9, HALF, HID),
        in_bias_grad,
        out_grad,
        out_bias_grad,
    )


def solution(mesh):
    split = Mesh(mesh.devices.reshape(4, 2, 2, 4, 2), ("y", "xl", "c", "z", "xh"))
    return jax.shard_map(
        local,
        mesh=split,
        in_specs=(
            P(ENS, None, None, LAT),
            P(ENS, None, None, LAT),
            P(ENS, None, LAT, None),
            P(),
            P(),
            P(),
            P(),
            P(),
        ),
        out_specs=(P(ENS, None, LAT, None), P(ENS, None, LAT, None), P(), P(), P(), P(), P()),
        check_vma=False,
    )
```

```python
import functools

import jax
import jax.numpy as jnp
from jax import lax
from jax.experimental import pallas as pl
from jax.experimental.pallas import tpu as pltpu
from jax.sharding import Mesh, PartitionSpec as P

BF = jnp.bfloat16
F32 = jnp.float32
HIGH = lax.Precision.HIGHEST
LAT = ("y", "xl", "c")
ENS = ("z", "xh")
CHIPS = ("y", "xl", "z", "xh")
HALF = 48
CH = 96
HID = 512
COLS = 384
ROW = 768
CELLS = 1536
IN_ROWS = 448
IN_HALF = 224
TAP_HALF = 144
MIB = 1024 * 1024


def mm(a, b):
    return lax.dot_general(a, b, (((1,), (0,)), ((), ())), preferred_element_type=F32)


def mm_nt(a, b):
    return lax.dot_general(a, b, (((1,), (1,)), ((), ())), preferred_element_type=F32)


def mm_high(a, b):
    return lax.dot_general(
        a, b, (((1,), (0,)), ((), ())), preferred_element_type=F32, precision=HIGH
    )


def split3(x):
    hi = x.astype(BF)
    rest = x - hi.astype(F32)
    mid = rest.astype(BF)
    low = (rest - mid.astype(F32)).astype(BF)
    return hi, mid, low


def from_left(x):
    lane = lax.broadcasted_iota(jnp.int32, x.shape, 1)
    return jnp.where(lane == 0, 0.0, pltpu.roll(x, 1, 1))


def from_right(x):
    width = x.shape[1]
    lane = lax.broadcasted_iota(jnp.int32, x.shape, 1)
    return jnp.where(lane == width - 1, 0.0, pltpu.roll(x, width - 1, 1))


def sds(shape, dtype):
    return jax.ShapeDtypeStruct(shape, dtype)


def call(
    body, outs, ins, scratch=(), smem=(), hbm=(), hbm_outs=(), alias=None, flops=0, name=None, limit=16
):
    moved = sum(x.size * x.dtype.itemsize for x in list(ins) + list(outs))
    return pl.pallas_call(
        body,
        out_shape=outs,
        in_specs=[
            pl.BlockSpec(
                memory_space=pltpu.SMEM if i in smem else pltpu.HBM if i in hbm else pltpu.VMEM
            )
            for i in range(len(ins))
        ],
        out_specs=[
            pl.BlockSpec(memory_space=pltpu.HBM if i in hbm_outs else pltpu.VMEM)
            for i in range(len(outs))
        ],
        scratch_shapes=list(scratch),
        input_output_aliases=alias or {},
        compiler_params=pltpu.CompilerParams(vmem_limit_bytes=limit * MIB),
        cost_estimate=pl.CostEstimate(flops=flops, bytes_accessed=moved, transcendentals=0),
        name=name,
    )(*ins)


def payload_kernel(on_ref, grad_ref, out_ref):
    width = on_ref.shape[2]
    blank = jnp.zeros(on_ref.shape[1:], BF)
    for s in range(on_ref.shape[0]):
        on = on_ref[s]
        hi = on.astype(BF)
        grad = grad_ref[s]
        out_ref[s, :, :width] = hi
        out_ref[s, :, width : 2 * width] = (on - hi.astype(F32)).astype(BF)
        if s + 1 < on_ref.shape[0]:
            out_ref[s + 1, :, 2 * width : 3 * width] = hi
        if s > 0:
            out_ref[s - 1, :, 3 * width : 4 * width] = hi
        out_ref[s, :, 4 * width :] = grad.astype(BF)
    out_ref[0, :, 2 * width : 3 * width] = blank
    out_ref[on_ref.shape[0] - 1, :, 3 * width : 4 * width] = blank


def payload(on, grad):
    bands, width, channels = on.shape
    return call(
        payload_kernel, [sds((bands, width, 5 * channels), BF)], [on, grad], name="payload", limit=56
    )[0]


def prep_kernel(
    mix_ref, w1_ref, w2_ref, b1_ref, b2_ref, *refs
):
    stage1, stage2 = refs[-2:]
    flows = mix_ref.shape[0]
    row = lax.broadcasted_iota(jnp.int32, (CH, CH), 0)
    col = lax.broadcasted_iota(jnp.int32, (CH, CH), 1)
    eye = (row == col).astype(F32)
    near = (row // 16) == (col // 16)
    units = []
    for k in range(flows):
        mix = mix_ref[k]
        units.append(jnp.where(row > col, mix, 0.0))
        units.append(jnp.where(row < col, mix, 0.0))
    inner = [jnp.where(near, u, 0.0) for u in units]
    outer = [u - i for u, i in zip(units, inner)]
    power = inner
    blocks = [eye - n for n in inner]
    for _ in range(3):
        power = [mm_high(p, p) for p in power]
        blocks = [mm_high(b, eye + p) for b, p in zip(blocks, power)]
    power = [mm_high(b, o) for b, o in zip(blocks, outer)]
    whole = [eye - p for p in power]
    for _ in range(2):
        power = [mm_high(p, p) for p in power]
        whole = [mm_high(w, eye + p) for w, p in zip(whole, power)]
    inverses = [mm_high(w, b) for w, b in zip(whole, blocks)]
    for k in range(flows):
        inv_ref, lut_ref, w1t_ref, w2t_ref, w2k_ref, w1k_ref, b2c_ref = refs[7 * k : 7 * k + 7]
        inv_ref[...] = mm_high(inverses[2 * k + 1], inverses[2 * k])
        lut_ref[...] = mm_high(units[2 * k] + eye, units[2 * k + 1] + eye).T
        for tap in range(9):
            stage1[tap * HALF : (tap + 1) * HALF, :] = 0.5 * w1_ref[k, tap].astype(F32)
            stage2[tap * CH : (tap + 1) * CH, :] = 0.5 * w2_ref[k, 8 - tap].astype(F32)
        hi, mid, low = split3(0.5 * b1_ref[k : k + 1, :])
        stage1[9 * HALF :, :] = jnp.zeros((IN_ROWS - 9 * HALF, HID), F32)
        for i, part in enumerate((hi, mid, low)):
            stage1[9 * HALF + i : 9 * HALF + i + 1, :] = part.astype(F32)
        w1t_ref[...] = stage1[...].T.astype(BF)
        w2t_ref[...] = stage2[...].T.astype(BF)
        for a in range(3):
            for b in range(3):
                w2k_ref[b * CH : (b + 1) * CH, a * HID : (a + 1) * HID] = w2_ref[k, 3 * a + b]
                w1k_ref[b * HALF : (b + 1) * HALF, a * HID : (a + 1) * HID] = w1_ref[
                    k, 3 * (2 - a) + b
                ]
        b2c_ref[...] = jnp.broadcast_to(b2_ref[k : k + 1, :], (8, CH)).T


def prep(mix_factors, in_kernel, out_kernel, in_bias, out_bias):
    flows = mix_factors.shape[0]
    outs = call(
        prep_kernel,
        [
            sds((CH, CH), F32),
            sds((CH, CH), F32),
            sds((HID, IN_ROWS), BF),
            sds((HID, 9 * CH), BF),
            sds((3 * CH, 3 * HID), BF),
            sds((3 * HALF, 3 * HID), BF),
            sds((CH, 8), F32),
        ]
        * flows,
        [mix_factors, in_kernel, out_kernel, in_bias, out_bias],
        scratch=[pltpu.VMEM((IN_ROWS, HID), F32), pltpu.VMEM((9 * CH, HID), F32)],
        name="prep",
        limit=56,
    )
    return [outs[i::7] for i in range(7)]


def turn_kernel(recv_ref, above_ref, mid_ref, below_ref, ya_ref, ga_ref, stage):
    width = 2 * CH
    row = lax.broadcasted_iota(jnp.int32, (width, width), 0)
    col = lax.broadcasted_iota(jnp.int32, (width, width), 1)
    pick = (col == 4 * (row % HALF) + row // HALF).astype(BF)
    none = jnp.zeros((width, width), BF)
    first = jnp.concatenate([pick, none], axis=1)
    second = jnp.concatenate([none, pick], axis=1)
    both = jnp.concatenate([pick, pick], axis=1)
    sources, count = recv_ref.shape[0], recv_ref.shape[1]
    for s in range(sources):
        stage[s * count : (s + 1) * count, :] = recv_ref[s].astype(F32)
    pair = stage[:, : 2 * width].astype(BF)
    kept = mm_nt(both, pair)
    mid_ref[...] = mm_nt(first, pair).astype(BF)
    pair = stage[:, 2 * width : 4 * width].astype(BF)
    above_ref[...] = mm_nt(first, pair).astype(BF)
    below_ref[...] = mm_nt(second, pair).astype(BF)
    grad = mm_nt(pick, stage[:, 4 * width :].astype(BF))
    for k in range(4):
        ya_ref[:, k * COLS : (k + 1) * COLS] = kept[k * HALF : (k + 1) * HALF]
        ga_ref[:, k * COLS : (k + 1) * COLS] = grad[k * HALF : (k + 1) * HALF]


def turn(recv):
    return call(
        turn_kernel,
        [sds((2 * CH, COLS), BF)] * 3 + [sds((HALF, CELLS), F32)] * 2,
        [recv],
        scratch=[pltpu.VMEM((COLS, recv.shape[2]), F32)],
        flops=4 * 10**9,
        name="turn",
    )


def stack_planes(even, odd, factor=None):
    if factor is not None:
        even = (even.astype(F32) * factor).astype(BF)
        odd = (odd.astype(F32) * factor).astype(BF)
    left = from_left(odd.astype(F32)).astype(BF)
    right = from_right(even.astype(F32)).astype(BF)
    return jnp.concatenate([left, even, odd, right], axis=0)


def fill_input_columns(flags_ref, above_ref, mid_ref, below_ref, columns, first, count):
    refs = {-2: (above_ref, 0), -1: (above_ref, CH), 0: (mid_ref, 0)}
    refs.update({1: (mid_ref, CH), 2: (below_ref, 0), 3: (below_ref, CH)})
    for source in range(first - 1, first + count + 1):
        ref, at = refs[source]
        factor = flags_ref[0] if source < 0 else flags_ref[1] if source > 1 else None
        stacked = stack_planes(ref[at : at + HALF], ref[at + HALF : at + CH], factor)
        for a in range(3):
            target = source - a + 1 - first
            if 0 <= target < count:
                for p in range(2):
                    lane = (2 * target + p) * COLS
                    columns[a * 144 : (a + 1) * 144, lane : lane + COLS] = stacked[
                        p * HALF : p * HALF + 144
                    ]
    extra = IN_ROWS - 9 * HALF
    row = lax.broadcasted_iota(jnp.int32, (extra, count * ROW), 0)
    columns[9 * HALF :, :] = jnp.where(row < 3, 1.0, 0.0).astype(BF)


def fill_grad_columns(flags_ref, above_ref, mid_ref, below_ref, columns):
    for source in range(-2, 4):
        ref = above_ref if source < 0 else below_ref if source > 1 else mid_ref
        factor = flags_ref[0] if source < 0 else flags_ref[1] if source > 1 else None
        at = (source % 2) * 2 * CH
        stacked = stack_planes(ref[at : at + CH], ref[at + CH : at + 2 * CH], factor)
        for a in range(3):
            target = source - a + 2
            if 0 <= target < 4:
                for p in range(2):
                    lane = (2 * target + p) * COLS
                    columns[a * 288 : (a + 1) * 288, lane : lane + COLS] = stacked[
                        p * CH : p * CH + 288
                    ]


def put_out_grad(raw, moved, out_ref):
    for r in range(2):
        for p in range(2):
            lane = (2 * r + p) * COLS
            at = (2 * r + p) * CH
            out_ref[at : at + HALF] = raw[:, lane : lane + COLS].astype(BF)
            out_ref[at + HALF : at + CH] = moved[:, lane : lane + COLS].astype(BF)


def forward_kernel(with_grad, flags_ref, *refs):
    above_ref, mid_ref, below_ref, w1t_ref, w2k_ref, b2_ref, inv_ref, ya_ref, yb_ref = refs[:9]
    columns, pre, outs = refs[-3:]
    if with_grad:
        x_ref, rows, slope_ref, next_ref, grad_ref, moved_ref = refs[9:-3]
    else:
        x_ref, rows, slope_ref, scale_ref = refs[9:-3]
    fill_input_columns(flags_ref, above_ref, mid_ref, below_ref, columns, -1, 4)
    for h in range(4):
        pre[h % 2] = mm(w1t_ref[...], columns[:, h * ROW : (h + 1) * ROW])
        inside = flags_ref[0] if h == 0 else flags_ref[1] if h == 3 else None

        def activate(step, carry):
            at = pl.multiple_of(step * 16, 16)
            half = pre[h % 2, pl.ds(at, 16), :]
            bent = jnp.tanh(half)
            more = 1.0 + bent
            hidden = half * more
            slope = more * (1.0 + half * (1.0 - bent))
            if inside is not None:
                hidden = hidden * inside
                slope = slope * inside
            rows[pl.ds(h * HID + at, 16), :] = hidden.astype(BF)
            slope_ref[pl.ds(h * HID + at, 16), :] = slope
            return carry

        lax.fori_loop(0, HID // 16, activate, 0, unroll=True)
    for r in range(2):
        taps = mm(w2k_ref[...], rows[r * HID : (r + 3) * HID, :])
        even, odd = taps[:, :COLS], taps[:, COLS:]
        lane = 2 * r * COLS
        outs[:, lane : lane + COLS] = from_left(odd[:CH]) + even[CH : 2 * CH] + odd[2 * CH :]
        outs[:, lane + COLS : lane + ROW] = even[:CH] + odd[CH : 2 * CH] + from_right(even[2 * CH :])
    raw = outs[:HALF] + b2_ref[:HALF, :1]
    shift = outs[HALF:] + b2_ref[HALF:, :1]
    inverse = 1.0 + jnp.exp(-(raw + 2.0))
    scale = 1.0 / inverse
    moved_in = yb_ref[...] * inverse - shift
    x = mm_high(inv_ref[...], jnp.concatenate([ya_ref[...], moved_in], axis=0))
    x_ref[...] = x
    if with_grad:
        moved_grad = yb_ref[...]
        moved = moved_grad * scale
        moved_ref[...] = moved
        put_out_grad((moved_grad * yb_ref[...] - 1.0) * (1.0 - scale), moved, grad_ref)
        for k in range(4):
            next_ref[k * HALF : (k + 1) * HALF] = x[:HALF, k * COLS : (k + 1) * COLS].astype(BF)
    else:
        scale_ref[...] = scale


def forward(flags, above, mid, below, w1t, w2k, b2c, inv, ya, yb, with_grad):
    outs = [sds((CH, CELLS), F32), sds((4 * HID, ROW), BF), sds((4 * HID, ROW), F32)]
    if with_grad:
        outs += [
            sds((2 * CH, COLS), BF),
            sds((4 * CH, COLS), BF),
            sds((HALF, CELLS), F32),
        ]
    else:
        outs += [sds((HALF, CELLS), F32)]
    return call(
        functools.partial(forward_kernel, with_grad),
        outs,
        [flags, above, mid, below, w1t, w2k, b2c, inv, ya, yb],
        scratch=[
            pltpu.VMEM((IN_ROWS, 4 * ROW), BF),
            pltpu.VMEM((2, HID, ROW), F32),
            pltpu.VMEM((CH, CELLS), F32),
        ],
        smem=(0,),
        limit=24,
        flops=4 * 10**9,
        name="forward",
    )


def backward_kernel(
    flags_ref, above_ref, mid_ref, below_ref, w2t_ref, slope_ref, w1k_ref, gpre_ref, in_ref,
    columns, hid_grad,
):
    fill_grad_columns(flags_ref, above_ref, mid_ref, below_ref, columns)
    for h in range(4):
        hid_grad[h % 2] = mm(w2t_ref[...], columns[:, h * ROW : (h + 1) * ROW])

        def slope(step, carry):
            at = pl.multiple_of(step * 16, 16)
            gpre_ref[pl.ds(h * HID + at, 16), :] = (
                hid_grad[h % 2, pl.ds(at, 16), :] * slope_ref[pl.ds(h * HID + at, 16), :]
            ).astype(BF)
            return carry

        lax.fori_loop(0, HID // 16, slope, 0, unroll=True)
    b0, b1, b2 = slice(0, HALF), slice(HALF, CH), slice(CH, 3 * HALF)
    for r in range(2):
        taps = mm(w1k_ref[...], gpre_ref[r * HID : (r + 3) * HID, :])
        even, odd = taps[:, :COLS], taps[:, COLS:]
        in_ref[r * CH : r * CH + HALF] = odd[b0] + even[b1] + from_left(odd[b2])
        in_ref[r * CH + HALF : (r + 1) * CH] = from_right(even[b0]) + odd[b1] + even[b2]


def backward(flags, above, mid, below, w2t, slope, w1k):
    return call(
        backward_kernel,
        [sds((4 * HID, ROW), BF), sds((2 * CH, COLS), F32)],
        [flags, above, mid, below, w2t, slope, w1k],
        scratch=[pltpu.VMEM((9 * CH, 4 * ROW), BF), pltpu.VMEM((2, HID, ROW), F32)],
        smem=(0,),
        flops=6 * 10**9,
        limit=20,
        name="backward",
    )


def out_weight_kernel(core_ref, grad_ref, rows_ref, keep_ref, give_ref, bias_ref, left, right, whole):
    for r in range(2):
        at = 2 * r * CH
        stacked = stack_planes(grad_ref[at : at + CH], grad_ref[at + CH : at + 2 * CH])
        left[r] = stacked[: 3 * CH]
        right[r] = stacked[CH:]
    part = [jnp.concatenate([left[r], right[r]], axis=1) for r in range(2)]
    for a in range(3):
        whole[...] = mm_nt(part[0], rows_ref[a * HID : (a + 1) * HID]) + mm_nt(
            part[1], rows_ref[(a + 1) * HID : (a + 2) * HID]
        )
        for ref, core in ((keep_ref, core_ref[0]), (give_ref, 1 - core_ref[0])):
            ref[a] = whole[pl.ds(pl.multiple_of(core * TAP_HALF, 8), TAP_HALF), :]
    ones = jnp.ones((8, COLS), BF)
    total = mm_nt(ones, grad_ref[:CH]) + mm_nt(ones, grad_ref[CH : 2 * CH])
    bias_ref[...] = total + (
        mm_nt(ones, grad_ref[2 * CH : 3 * CH]) + mm_nt(ones, grad_ref[3 * CH :])
    )


def out_weight(core, grad, rows):
    return call(
        out_weight_kernel,
        [sds((3, TAP_HALF, HID), F32), sds((3, TAP_HALF, HID), F32), sds((8, CH), F32)],
        [core, grad, rows],
        scratch=[
            pltpu.VMEM((2, 3 * CH, COLS), BF),
            pltpu.VMEM((2, 3 * CH, COLS), BF),
            pltpu.VMEM((3 * CH, HID), F32),
        ],
        smem=(0,),
        flops=2 * 10**9,
        name="out_weight",
    )


def in_weight_kernel(
    core_ref, flags_ref, above_ref, mid_ref, below_ref, gpre_ref, keep_ref, give_ref, columns,
    whole,
):
    fill_input_columns(flags_ref, above_ref, mid_ref, below_ref, columns, 0, 2)
    whole[...] = mm_nt(columns[:, :ROW], gpre_ref[HID : 2 * HID]) + mm_nt(
        columns[:, ROW:], gpre_ref[2 * HID : 3 * HID]
    )
    for ref, core in ((keep_ref, core_ref[0]), (give_ref, 1 - core_ref[0])):
        ref[...] = whole[pl.ds(pl.multiple_of(core * IN_HALF, 8), IN_HALF), :]


def in_weight(core, flags, above, mid, below, gpre):
    return call(
        in_weight_kernel,
        [sds((IN_HALF, HID), F32), sds((IN_HALF, HID), F32)],
        [core, flags, above, mid, below, gpre],
        scratch=[pltpu.VMEM((IN_ROWS, CELLS), BF), pltpu.VMEM((IN_ROWS, HID), F32)],
        smem=(0, 1),
        flops=10**9,
        name="in_weight",
    )


def close_kernel(next_step, flow, *refs):
    in_ref, ga_ref, moved_ref, lut_ref, x_ref, mix_ref, bias_ref = refs[:7]
    whole = refs[-1]
    if next_step:
        scale_ref, gx_ref, small, grad_ref, nmoved_ref = refs[7:-1]
    else:
        gx_ref, small = refs[7:-1]
    for k in range(4):
        lane = k * COLS
        whole[:HALF, lane : lane + COLS] = (
            ga_ref[:HALF, lane : lane + COLS] + in_ref[k * HALF : (k + 1) * HALF]
        )
    whole[HALF:] = moved_ref[...]
    gx = mm_high(lut_ref[...], whole[...])
    gx_ref[...] = gx
    if next_step:
        scale = scale_ref[...]
        moved_grad = gx[HALF:]
        moved = moved_grad * scale
        nmoved_ref[...] = moved
        put_out_grad((moved_grad * x_ref[HALF:] - 1.0) * (1.0 - scale), moved, grad_ref)
    ghi, gmid, _ = split3(whole[...])
    xhi, xmid, _ = split3(x_ref[...])
    outer = mm_nt(ghi, xhi) + (mm_nt(ghi, xmid) + mm_nt(gmid, xhi))
    row = lax.broadcasted_iota(jnp.int32, (CH, CH), 0)
    col = lax.broadcasted_iota(jnp.int32, (CH, CH), 1)
    eye = (row == col).astype(F32)
    mix = mix_ref[flow]
    lower = jnp.where(row > col, mix, 0.0) + eye
    upper = jnp.where(row < col, mix, 0.0) + eye
    by_upper = mm_high(outer, upper.T)
    by_lower = mm_high(lower.T, outer)
    small[:, :CH] = jnp.where(row > col, by_upper, jnp.where(row < col, by_lower, 0.0))
    small[:, CH:] = jnp.zeros((CH, 2 * 128 - CH), F32)
    small[:8, 128 : 128 + CH] = bias_ref[...]


def close(gin, ga, moved, lut, x, mix, flow, bias, scale=None):
    outs = [sds((CH, CELLS), F32), sds((CH, 256), F32)]
    ins = [gin, ga, moved, lut, x, mix, bias]
    if scale is not None:
        outs += [sds((4 * CH, COLS), BF), sds((HALF, CELLS), F32)]
        ins += [scale]
    return call(
        functools.partial(close_kernel, scale is not None, flow),
        outs,
        ins,
        scratch=[pltpu.VMEM((CH, CELLS), F32)],
        flops=10**9,
        name="close",
    )


def weave_kernel(x_ref, out_ref):
    size = 256
    row = lax.broadcasted_iota(jnp.int32, (size, size), 0)
    col = lax.broadcasted_iota(jnp.int32, (size, size), 1)
    place = (col == 2 * (row % 128) + row // 128).astype(BF)
    for r in range(2):
        for t in range(3):
            lane = r * ROW + t * 128
            pair = jnp.concatenate(
                [x_ref[:, lane : lane + 128], x_ref[:, lane + COLS : lane + COLS + 128]], axis=1
            )
            hi, mid, low = split3(pair)
            woven = mm(hi, place) + (mm(mid, place) + mm(low, place))
            out_ref[0, :, r, t * size : (t + 1) * size] = woven


def weave(x):
    return call(weave_kernel, [sds((1, CH, 2, ROW), F32)], [x], name="weave")[0]


FLOW_ROWS = 704
GROUP = 88


def merge_kernel(*refs):
    out_ref, total = refs[-2:]
    for k in range(2):
        own_in, own_out, got_in, got_out, small = refs[5 * k : 5 * k + 5]
        at = k * FLOW_ROWS
        total[at : at + IN_HALF] = own_in[...] + got_in[...]
        for a in range(3):
            start = at + IN_HALF + a * TAP_HALF
            total[start : start + TAP_HALF] = own_out[a] + got_out[a]
        start = at + FLOW_ROWS - HALF
        total[start : start + HALF, :256] = small[:HALF]
        total[start : start + HALF, 256:] = small[HALF:]
    for g in range(2 * FLOW_ROWS // GROUP):
        for lane in range(4):
            out_ref[4 * g + lane] = total[
                g * GROUP : (g + 1) * GROUP, lane * 128 : (lane + 1) * 128
            ].astype(BF)


def merge(first, second):
    shares = 2 * FLOW_ROWS // GROUP * 4
    return call(
        merge_kernel,
        [sds((shares, GROUP, 128), BF)],
        [*first, *second],
        scratch=[pltpu.VMEM((2 * FLOW_ROWS, HID), F32)],
        name="merge",
    )[0]


def total_kernel(cells, shares_ref, out_ref):
    total = shares_ref[0].astype(F32)
    for s in range(1, shares_ref.shape[0]):
        total += shares_ref[s].astype(F32)
    mean = (total * (1.0 / cells)).astype(BF)
    for s in range(shares_ref.shape[0]):
        out_ref[s] = mean


def totals(shares, cells):
    return call(
        functools.partial(total_kernel, cells), [sds(shares.shape, BF)], [shares], name="totals"
    )[0]


def half_copies(half, k, rows, win_ref, wout_ref, sems):
    at = k * FLOW_ROWS
    count = IN_HALF if half == 0 else 9 * HALF - IN_HALF
    pairs = [(at, count, win_ref.at[k, pl.ds(half * IN_HALF, count), :])]
    for a in range(3):
        start = at + IN_HALF + a * TAP_HALF
        if half == 0:
            pairs.append((start, CH, wout_ref.at[k, 3 * a + 2]))
            pairs.append((start + CH, HALF, wout_ref.at[k, 3 * a + 1, pl.ds(0, HALF), :]))
        else:
            pairs.append((start, HALF, wout_ref.at[k, 3 * a + 1, pl.ds(HALF, HALF), :]))
            pairs.append((start + HALF, CH, wout_ref.at[k, 3 * a]))
    return [
        pltpu.make_async_copy(rows.at[pl.ds(first, size), :], target, sems.at[7 * k + i])
        for i, (first, size, target) in enumerate(pairs)
    ]


def put_half(half_now, shares_ref, rows, win_ref, wout_ref, sems):
    groups = FLOW_ROWS // GROUP
    for k in range(2):
        for g in range(k * groups, (k + 1) * groups):
            for lane in range(4):
                rows[g * GROUP : (g + 1) * GROUP, lane * 128 : (lane + 1) * 128] = shares_ref[
                    4 * g + lane
                ].astype(F32)
        for half in range(2):

            @pl.when(half_now == half)
            def _():
                for copy in half_copies(half, k, rows, win_ref, wout_ref, sems):
                    copy.start()


def wait_half(half_now, rows, win_ref, wout_ref, sems):
    for half in range(2):

        @pl.when(half_now == half)
        def _():
            for k in range(2):
                for copy in half_copies(half, k, rows, win_ref, wout_ref, sems):
                    copy.wait()


def unpack_own_kernel(core_ref, mine_ref, x_ref, win_ref, wout_ref, woven_ref, rows, sems):
    put_half(core_ref[0], mine_ref, rows, win_ref, wout_ref, sems)
    weave_kernel(x_ref, woven_ref)
    wait_half(core_ref[0], rows, win_ref, wout_ref, sems)


def unpack_other_kernel(
    core_ref, mine_ref, other_ref, _win, _wout, win_ref, wout_ref, mix_ref, bin_ref, bout_ref,
    rows, sems,
):
    put_half(1 - core_ref[0], other_ref, rows, win_ref, wout_ref, sems)
    groups = FLOW_ROWS // GROUP
    for k in range(2):
        last = 4 * ((k + 1) * groups - 1)
        parts = [
            mine_ref[last + lane].astype(F32)[GROUP - HALF :]
            + other_ref[last + lane].astype(F32)[GROUP - HALF :]
            for lane in range(4)
        ]
        mix_ref[k, :HALF] = parts[0][:, :CH]
        mix_ref[k, HALF:] = parts[2][:, :CH]
        bout_ref[k : k + 1, :] = parts[1][:1, :CH]
        row = 9 * HALF - IN_HALF
        share, row = 4 * (k * groups + row // GROUP), row % GROUP
        for lane in range(4):
            mine = mine_ref[share + lane].astype(F32)[row : row + 1]
            other = other_ref[share + lane].astype(F32)[row : row + 1]
            bin_ref[k : k + 1, lane * 128 : (lane + 1) * 128] = jnp.where(
                core_ref[0] == 1, mine, other
            )
    wait_half(1 - core_ref[0], rows, win_ref, wout_ref, sems)


KERNEL_GRADS = [((2, 9 * HALF, HID), F32), ((2, 9, CH, HID), F32)]


def unpack_own(core, mine, x):
    return call(
        unpack_own_kernel,
        [sds(*x) for x in KERNEL_GRADS] + [sds((1, CH, 2, ROW), F32)],
        [core, mine, x],
        scratch=[pltpu.VMEM((2 * FLOW_ROWS, HID), F32), pltpu.SemaphoreType.DMA((14,))],
        smem=(0,),
        hbm_outs=(0, 1),
        name="unpack_own",
    )


def unpack_other(core, mine, other, win, wout):
    return call(
        unpack_other_kernel,
        [sds(*x) for x in KERNEL_GRADS]
        + [sds((2, CH, CH), F32), sds((2, HID), F32), sds((2, CH), F32)],
        [core, mine, other, win, wout],
        scratch=[pltpu.VMEM((2 * FLOW_ROWS, HID), F32), pltpu.SemaphoreType.DMA((14,))],
        smem=(0,),
        hbm=(3, 4),
        hbm_outs=(0, 1),
        alias={3: 0, 4: 1},
        name="unpack_other",
    )


def after(x, *others):
    return lax.optimization_barrier((x, *others))[0]


def local(passed_on, passed_grad, latent, mix_factors, in_kernel, in_bias, out_kernel, out_bias):
    lat_index = lax.axis_index(LAT)
    lat_count = lax.axis_size(LAT)
    forth = [(i, (i + 1) % lat_count) for i in range(lat_count)]
    back = [(t, s) for s, t in forth]
    swap = [(0, 1), (1, 0)]
    flags = jnp.stack([lat_index > 0, lat_index < lat_count - 1]).astype(F32)
    core = lax.axis_index("c").astype(jnp.int32).reshape(1)

    block = payload(
        jnp.transpose(passed_on[0], (1, 2, 0)), jnp.transpose(passed_grad[0], (1, 2, 0))
    )
    recv = lax.all_to_all(block, LAT, 0, 0, tiled=True)
    inv, lut, w1t, w2t, w2k, w1k, b2c = prep(mix_factors, in_kernel, out_kernel, in_bias, out_bias)
    w1 = in_kernel.reshape(2, 9 * HALF, HID)
    yb = latent.reshape(HALF, CELLS)

    above, mid, below, ya, ga = turn(recv)
    x1, rows1, slope1, next_mid, grad1, moved1 = forward(
        flags, above, mid, below, w1t[1], w2k[1], b2c[1], inv[1], ya, yb, True
    )
    above0 = lax.ppermute(next_mid, LAT, forth)
    below0 = lax.ppermute(next_mid, LAT, back)
    top1 = lax.ppermute(grad1, LAT, forth)
    bottom1 = lax.ppermute(grad1, LAT, back)
    keep_out1, give_out1, bias1 = out_weight(core, grad1, rows1)
    x0, rows0, slope0, scale0 = forward(
        after(flags, keep_out1), above0, next_mid, below0, w1t[0], w2k[0], b2c[0], inv[0],
        x1[:HALF], x1[HALF:], False,
    )
    got_out1 = lax.ppermute(give_out1, "c", swap)
    gpre1, in1 = backward(after(flags, x0), top1, grad1, bottom1, w2t[1], slope1, w1k[1])
    gx1, small1, grad0, moved0 = close(
        in1, ga, moved1, lut[1], x1, mix_factors, 1, bias1, scale0
    )
    top0 = lax.ppermute(grad0, LAT, forth)
    bottom0 = lax.ppermute(grad0, LAT, back)
    keep_in1, give_in1 = in_weight(after(core, grad0), flags, above, mid, below, gpre1)
    got_in1 = lax.ppermute(give_in1, "c", swap)
    keep_out0, give_out0, bias0 = out_weight(after(core, keep_in1), grad0, rows0)
    rebuilt = weave(after(x0, keep_out0))
    gpre0, in0 = backward(after(flags, rebuilt), top0, grad0, bottom0, w2t[0], slope0, w1k[0])
    got_out0 = lax.ppermute(give_out0, "c", swap)
    keep_in0, give_in0 = in_weight(after(core, in0), flags, above0, next_mid, below0, gpre0)
    got_in0 = lax.ppermute(give_in0, "c", swap)
    gx0, small0 = close(
        after(in0, keep_in0), gx1, moved0, lut[0], x0, mix_factors, 0, bias0
    )

    packed = merge(
        (keep_in0, keep_out0, got_in0, got_out0, small0),
        (keep_in1, keep_out1, got_in1, got_out1, small1),
    )
    shares = lax.all_to_all(packed, CHIPS, 0, 0, tiled=True)
    cells = float(CELLS * lat_count * lax.axis_size(ENS))
    spread = totals(shares, cells)
    mine = lax.all_to_all(spread, CHIPS, 0, 0, tiled=True)
    other = lax.ppermute(mine, "c", swap)
    win, wout, input_grad = unpack_own(core, mine, gx0)
    in_grad, out_grad, mix_grad, in_bias_grad, out_bias_grad = unpack_other(
        core, mine, other, win, wout
    )
    return (
        rebuilt,
        input_grad,
        mix_grad,
        in_grad.reshape(2, 9, HALF, HID),
        in_bias_grad,
        out_grad,
        out_bias_grad,
    )


def solution(mesh):
    split = Mesh(mesh.devices.reshape(4, 2, 2, 4, 2), ("y", "xl", "c", "z", "xh"))
    return jax.shard_map(
        local,
        mesh=split,
        in_specs=(
            P(ENS, None, None, LAT),
            P(ENS, None, None, LAT),
            P(ENS, None, LAT, None),
            P(),
            P(),
            P(),
            P(),
            P(),
        ),
        out_specs=(P(ENS, None, LAT, None), P(ENS, None, LAT, None), P(), P(), P(), P(), P()),
        check_vma=False,
    )
```
